128 devices in a mesh: lat: 32 (over x, z_lo, y), lon: 4 (over z_hi, core).
Axes of the slice: x: 4, y: 4, z: 4 (z_hi: 2, z_lo: 2; z = z_hi * 2 + z_lo), core: 2. Of those that a mesh axis runs over, the one named last changes fastest.
Arguments:
- ocean_state: bfloat16 [76, 256, 4096], P(None, 'lat', 'lon'), may hold values from -6 to 6
- sea_mask: int32 [256, 4096], P('lat', 'lon'), may hold values 0 or 1
- ocean_w1: bfloat16 [64, 76, 3, 3], replicated, may hold values from -0.21875 to 0.21875
- ocean_b1: float32 [64], replicated, may hold values from -3 to 3
- ocean_w2: bfloat16 [64, 64, 3, 3], replicated, may hold values from -0.25 to 0.25
- ocean_b2: float32 [64], replicated, may hold values from -3 to 3
- regrid_weight: bfloat16 [8192, 2, 128, 128], P(('lat', 'lon')), may hold values from -0.5 to 0.5
- route_dev: int32 [8192, 2], P(('lat', 'lon')), may hold values from 0 to 127, as said below
- route_row: int32 [8192, 2], P(('lat', 'lon')), may hold values from 0 to 63
- atmos_state: bfloat16 [64, 2048, 512], P(None, 'lat', 'lon'), may hold values from -6 to 6
- atmos_w1: bfloat16 [64, 64, 3, 3], replicated, may hold values from -0.25 to 0.25
- atmos_b1: float32 [64], replicated, may hold values from -3 to 3
- atmos_w2: bfloat16 [64, 64, 3, 3], replicated, may hold values from -0.25 to 0.25
- atmos_b2: float32 [64], replicated, may hold values from -3 to 3
Outputs:
- ocean_next: bfloat16 [64, 256, 4096], P(None, 'lat', 'lon')
- atmos_next: bfloat16 [64, 2048, 512], P(None, 'lat', 'lon')
The draws below stay inside these ranges and needn't reach their ends.
Inputs may be any that keep to these rules, and one draw needn't show every extreme that they name: `route_dev`: every intersection of a block of device d = a * 4 + e names a device whose latitude index (device // 4) is a - 1, a or a + 1. In the rows of one device (aligned blocks of 64 rows) no device number appears more than 32 times, and some number appears exactly 32 times; the 2 intersections of one block name different devices.
All inputs are finite; a program needn't handle non-finite values. No bound on the sum of `sea_mask` on one device may be relied on, other than what follows from the above.
Results may differ from the reference program's by a relative error of at most 0.01.
Values may be sent and summed in bfloat16 or wider, within the bound.
A program may use at most 192 MiB of HBM per device.

```python
import jax
import jax.numpy as jnp
import numpy as np
from jax import lax

CIN = 76
CH = 64
OCN_ROWS = 8
OCN_COLS = 1024
BLK = 128
INTERSECTIONS = 2
ATM_ROWS = 64
NLAT = 256
NLON = 4096
OBLK = 64
BLOCKS_ALL = 8192
AROWS = 2048
ACOLS = 512
N_LAT = 32
N_LON = 4
DEVICES = 128


def draw_route_dev(key, part):
    key = jax.random.fold_in(key, 11)
    unit = OBLK * INTERSECTIONS // 128
    counts = np.array([32, 24, 16, 8, 8, 6, 4, 6, 6, 8, 6, 4]) * unit
    bucket = np.repeat(np.arange(12), counts)
    group = jnp.asarray(bucket // 4, dtype=jnp.int32)
    column = jnp.asarray(bucket % 4, dtype=jnp.int32)
    offsets = jnp.asarray(np.array([0, -1, 1])[bucket // 4], dtype=jnp.int32)
    lat_count = DEVICES // N_LON

    def one_device(device):
        device_key = jax.random.fold_in(key, device)
        lon_orders = jnp.stack([jax.random.permutation(jax.random.fold_in(device_key, g), N_LON) for g in range(3)]).astype(jnp.int32)
        dest_lon = lon_orders[group, column]
        lat_here = device // N_LON
        moved = jnp.where((lat_here == 0) & (offsets < 0), 1, jnp.where((lat_here == lat_count - 1) & (offsets > 0), -1, offsets))
        dest = (lat_here + moved) * N_LON + dest_lon
        paired = jnp.stack([dest[:OBLK], dest[OBLK:]], axis=1)
        block_order = jax.random.permutation(jax.random.fold_in(device_key, 7), OBLK)
        return paired[block_order]
    routes = jax.vmap(one_device)(jnp.arange(DEVICES, dtype=jnp.int32))
    return routes.reshape(DEVICES * OBLK, INTERSECTIONS).astype(jnp.int32)


def place_ends(values, rng, least, top_value):
    shape = values.shape
    place = [jax.random.randint(jax.random.fold_in(rng, axis), (), 0, shape[axis]) for axis in range(len(shape))]
    values = values.at[tuple(place)].set(least)
    longest = shape.index(max(shape))
    place[longest] = (place[longest] + 1) % shape[longest]
    return values.at[tuple(place)].set(top_value)


def level_of(own_key, dims, shards, smallest, largest):
    loudness, own = 1.0, jax.random.fold_in(own_key, 6)
    for axis_at, blocks in shards:
        steps = jnp.exp(jax.random.uniform(jax.random.fold_in(own, axis_at), (blocks,), jnp.float32, smallest / len(shards), largest / len(shards)))
        loudness = loudness * jnp.repeat(steps, dims[axis_at] // blocks).reshape([-1 if axis == axis_at else 1 for axis in range(len(dims))])
    return loudness


def scatter_about(key, dims, width, limit, cuts=(), kind=jnp.bfloat16):
    loudness = level_of(key, dims, cuts, -0.22, 0.18) if cuts else 1.0
    entries = jax.random.normal(key, dims, jnp.float32) * width * loudness
    return jnp.minimum(jnp.maximum(entries, -limit), limit).astype(kind)


def setup_inputs(seed: int = 0) -> dict:
    key_list = jax.random.split(jax.random.key(seed), 15)
    return {
        "ocean_state": scatter_about(key_list[0], (CIN, NLAT, NLON), 1.0, 6.0, ((1, 32), (2, 4))),
        "sea_mask": place_ends((jax.random.randint(key_list[1], (NLAT, NLON), 0, 4) < 3).astype(jnp.int32), jax.random.fold_in(key_list[1], 1), 0, 1),
        "ocean_w1": scatter_about(key_list[2], (CH, CIN, 3, 3), (CIN * 9) ** -0.5, 0.21875),
        "ocean_b1": scatter_about(key_list[3], (CH,), 0.5, 3.0, (), jnp.float32),
        "ocean_w2": scatter_about(key_list[4], (CH, CH, 3, 3), (CH * 9) ** -0.5, 0.25),
        "ocean_b2": scatter_about(key_list[5], (CH,), 0.5, 3.0, (), jnp.float32),
        "regrid_weight": scatter_about(key_list[6], (BLOCKS_ALL, INTERSECTIONS, BLK, BLK), BLK ** -0.5, 0.5, ((0, 128),)),
        "route_dev": draw_route_dev(jax.random.fold_in(key_list[14], 71), 0),
        "route_row": place_ends(jax.random.randint(key_list[8], (BLOCKS_ALL, INTERSECTIONS), 0, ATM_ROWS), jax.random.fold_in(key_list[8], 1), 0, ATM_ROWS - 1).astype(jnp.int32),
        "atmos_state": scatter_about(key_list[9], (CH, AROWS, ACOLS), 1.0, 6.0, ((1, 32), (2, 4))),
        "atmos_w1": scatter_about(key_list[10], (CH, CH, 3, 3), (CH * 9) ** -0.5, 0.25),
        "atmos_b1": scatter_about(key_list[11], (CH,), 0.5, 3.0, (), jnp.float32),
        "atmos_w2": scatter_about(key_list[12], (CH, CH, 3, 3), (CH * 9) ** -0.5, 0.25),
        "atmos_b2": scatter_about(key_list[13], (CH,), 0.5, 3.0, (), jnp.float32),
    }


def conv_field(field, weight, bias):
    wide = jnp.concatenate([field[:, :, -1:], field, field[:, :, :1]], axis=2)
    tall = jnp.pad(wide, ((0, 0), (1, 1), (0, 0)))
    out = lax.conv_general_dilated(tall[None].astype(jnp.float32), weight.astype(jnp.float32), (1, 1), "VALID", dimension_numbers=("NCHW", "OIHW", "NCHW"), precision=lax.Precision.HIGHEST)[0]
    return out + bias[:, None, None]


def reference(ocean_state, sea_mask, ocean_w1, ocean_b1, ocean_w2, ocean_b2, regrid_weight, route_dev, route_row, atmos_state, atmos_w1, atmos_b1, atmos_w2, atmos_b2):
    mask = sea_mask.astype(jnp.float32)
    hidden = (jax.nn.silu(conv_field(ocean_state, ocean_w1, ocean_b1)) * mask).astype(jnp.bfloat16)
    ocean_next = (conv_field(hidden, ocean_w2, ocean_b2) * mask).astype(jnp.bfloat16)
    devices = N_LAT * N_LON
    across = OCN_COLS // BLK
    blocks = ocean_next.reshape(CH, N_LAT, OCN_ROWS, N_LON, across, BLK).transpose(1, 3, 0, 2, 4, 5).reshape(devices, CH, OBLK, BLK)
    weights = regrid_weight.reshape(devices, OBLK, INTERSECTIONS, BLK, BLK)
    target = (route_dev * ATM_ROWS + route_row).astype(jnp.int32).reshape(devices, OBLK * INTERSECTIONS)

    def add_device(total, items):
        block_data, weight_data, where = items
        contrib = jnp.einsum("mkao,cmo->mkca", weight_data.astype(jnp.float32), block_data.astype(jnp.float32)).astype(jnp.bfloat16)
        total = total.at[where].add(contrib.reshape(OBLK * INTERSECTIONS, CH, BLK).astype(jnp.float32))
        return total, None

    start = jnp.zeros((devices * ATM_ROWS, CH, BLK), jnp.float32)
    total, unused = lax.scan(add_device, start, (blocks, weights, target))
    flux = total.reshape(N_LAT, N_LON, ATM_ROWS, CH, BLK).transpose(3, 0, 2, 1, 4).reshape(CH, N_LAT * ATM_ROWS, N_LON * BLK)
    first = (atmos_state.astype(jnp.float32) + flux).astype(jnp.bfloat16)
    second = jax.nn.silu(conv_field(first, atmos_w1, atmos_b1)).astype(jnp.bfloat16)
    atmos_next = (first.astype(jnp.float32) + conv_field(second, atmos_w2, atmos_b2)).astype(jnp.bfloat16)
    return ocean_next, atmos_next
```

```python
import functools

import jax
import jax.numpy as jnp
from jax import lax
from jax.experimental import pallas as pl
from jax.experimental.pallas import tpu as pltpu
from jax.sharding import PartitionSpec as P

MESH = pl.DeviceIdType.MESH
F32 = jnp.float32
BF16 = jnp.bfloat16
CAP = 32
VMEM_LIMIT = 56 * 1024 * 1024


def silu(v):
    return 0.5 * v * (1.0 + jnp.tanh(0.5 * v))


def shifted_sum(taps):
    out = taps.shape[0] // 3
    columns = taps.shape[1]
    return (
        pltpu.roll(taps[0:out], 1, 1)
        + taps[out : 2 * out]
        + pltpu.roll(taps[2 * out :], columns - 1, 1)
    )


def stacked_weight(weight, padded_in):
    out, inn = weight.shape[:2]
    weight = jnp.pad(weight, ((0, 0), (0, padded_in - inn), (0, 0), (0, 0)))
    return weight.transpose(3, 0, 2, 1).reshape(3 * out, 3 * padded_in)


def ocean_kernel(
    place,
    x_ref,
    side_ref,
    top_ref,
    bottom_ref,
    w1_ref,
    b1_ref,
    w2_ref,
    b2_ref,
    regrid_ref,
    next_ref,
    slots_ref,
    tall,
    hidden,
):
    row = lax.rem(pl.program_id(0), 16)
    rows, channels, cols = x_ref.shape
    mask_at = 76

    def first_conv(j):
        field = jnp.concatenate([tall[j], tall[j + 1], tall[j + 2]], axis=0)
        taps = jnp.dot(w1_ref[...], field, preferred_element_type=F32)
        mask = tall[j + 1, mask_at : mask_at + 1, :].astype(F32)
        hidden[j] = (silu(shifted_sum(taps) + b1_ref[...]) * mask).astype(BF16)

    @pl.when(row == 0)
    def _():
        tall[0:2] = top_ref[...]
        tall[2 : 2 + rows, :, 0:cols] = x_ref[...]
        tall[2 : 2 + rows, :, cols:] = side_ref[...]
        tall[2 + rows :] = bottom_ref[...]
        first_conv(0)
        first_conv(1)

    first_conv(lax.rem(row + 2, 16))
    field = jnp.concatenate([hidden[row], hidden[row + 1], hidden[row + 2]], axis=0)
    taps = jnp.dot(w2_ref[...], field, preferred_element_type=F32)
    mask = tall[row + 2, mask_at : mask_at + 1, :].astype(F32)
    result = ((shifted_sum(taps) + b2_ref[...]) * mask).astype(BF16)[:, :cols]
    next_ref[0] = result
    blocks = regrid_ref.shape[0]
    for q in range(blocks):
        field = result[:, q * 128 : (q + 1) * 128]
        both = lax.dot_general(
            field, regrid_ref[q], (((1,), (1,)), ((), ())), preferred_element_type=F32
        ).astype(BF16)
        for k in range(2):
            slots_ref[place[(row * blocks + q) * 2 + k]] = both[:, k * 128 : (k + 1) * 128]


def ocean_step(place, x, side, top, bottom, w1, b1, w2, b2, regrid, slots):
    rows, channels, cols = x.shape
    wide = cols + 128
    out = w2.shape[0] // 3

    def whole(array):
        zeros = (0,) * array.ndim
        return pl.BlockSpec(array.shape, lambda r, place: zeros)

    blocks = regrid.shape[0] // rows
    return pl.pallas_call(
        ocean_kernel,
        out_shape=(
            jax.ShapeDtypeStruct((rows, out, cols), BF16),
            jax.ShapeDtypeStruct((slots, out, 128), BF16),
        ),
        grid_spec=pltpu.PrefetchScalarGridSpec(
            num_scalar_prefetch=1,
            grid=(rows,),
            in_specs=[whole(a) for a in (x, side, top, bottom, w1, b1, w2, b2)]
            + [pl.BlockSpec((blocks, 256, 128), lambda r, place: (r, 0, 0))],
            out_specs=[
                pl.BlockSpec((1, out, cols), lambda r, place: (r, 0, 0)),
                pl.BlockSpec((slots, out, 128), lambda r, place: (0, 0, 0)),
            ],
            scratch_shapes=[
                pltpu.VMEM((rows + 4, channels, wide), BF16),
                pltpu.VMEM((rows + 2, out, wide), BF16),
            ],
        ),
        compiler_params=pltpu.CompilerParams(vmem_limit_bytes=VMEM_LIMIT),
        name="ocean",
    )(place, x, side, top, bottom, w1, b1, w2, b2, regrid)


def exchange_kernel(
    lat_count, lon_count, data, rows, data_in, rows_in, send_sem, recv_sem, row_send, row_recv
):
    lat, lon = lax.axis_index("lat"), lax.axis_index("lon")
    barrier = pltpu.get_barrier_semaphore()

    def partners():
        for offset in (0, -1, 1):
            for step in range(lon_count):
                if offset == 0 and step == 0:
                    continue
                there = lax.rem(lon + step, lon_count)
                ok = jnp.logical_and(lat + offset >= 0, lat + offset < lat_count)
                yield offset, step, there, ok

    def copies(offset, there):
        target = {"lat": lat + offset, "lon": there}
        source = (offset + 1) * lon_count + there
        slot = (1 - offset) * lon_count + lon
        return (
            pltpu.make_async_remote_copy(
                src_ref=data.at[source],
                dst_ref=data_in.at[slot],
                send_sem=send_sem.at[source],
                recv_sem=recv_sem.at[slot],
                device_id=target,
                device_id_type=MESH,
            ),
            pltpu.make_async_remote_copy(
                src_ref=rows.at[source],
                dst_ref=rows_in.at[slot],
                send_sem=row_send.at[source],
                recv_sem=row_recv.at[slot],
                device_id=target,
                device_id_type=MESH,
            ),
        )

    def arrivals(offset, there):
        slot = (offset + 1) * lon_count + there
        return (
            pltpu.make_async_copy(data_in.at[slot], data_in.at[slot], recv_sem.at[slot]),
            pltpu.make_async_copy(rows_in.at[slot], rows_in.at[slot], row_recv.at[slot]),
        )

    for offset, step, there, ok in partners():

        @pl.when(ok)
        def _():
            pl.semaphore_signal(
                barrier, inc=1, device_id={"lat": lat + offset, "lon": there}, device_id_type=MESH
            )

    edge = jnp.logical_or(lat == 0, lat == lat_count - 1)
    pl.semaphore_wait(barrier, jnp.where(edge, 2 * lon_count - 1, 3 * lon_count - 1))

    for offset, step, there, ok in partners():

        @pl.when(ok)
        def _():
            for copy in copies(offset, there):
                copy.start()

    own = lon_count + lon
    local = (
        pltpu.make_async_copy(data.at[own], data_in.at[own], recv_sem.at[own]),
        pltpu.make_async_copy(rows.at[own], rows_in.at[own], row_recv.at[own]),
    )
    for copy in local:
        copy.start()
    for copy in local:
        copy.wait()

    for offset, step, there, ok in partners():

        @pl.when(ok)
        def _():
            for copy in copies(offset, there):
                copy.wait_send()
            for copy in arrivals(offset, there):
                copy.wait()


def exchange(data, rows, lat_count, lon_count):
    count = 3 * lon_count
    return pl.pallas_call(
        functools.partial(exchange_kernel, lat_count, lon_count),
        out_shape=(
            jax.ShapeDtypeStruct(data.shape, data.dtype),
            jax.ShapeDtypeStruct(rows.shape, rows.dtype),
        ),
        in_specs=[pl.BlockSpec(memory_space=pl.ANY)] * 2,
        out_specs=[pl.BlockSpec(memory_space=pl.ANY)] * 2,
        scratch_shapes=[pltpu.SemaphoreType.DMA((count,))] * 4,
        compiler_params=pltpu.CompilerParams(collective_id=0, has_side_effects=True),
        name="exchange",
    )(data, rows)


def merge_kernel(rows, counts, data_ref, atmos_ref, first_ref, edge_ref, total):
    step = pl.program_id(0)

    @pl.when(step == 0)
    def _():
        total[...] = atmos_ref[...].astype(F32)

    def add(s, carry):
        r = rows[step * CAP + s]
        total[r] = total[r] + data_ref[0, s].astype(F32)
        return carry

    lax.fori_loop(0, counts[step], add, 0)

    @pl.when(step == pl.num_programs(0) - 1)
    def _():
        count, channels, cols = first_ref.shape
        lane = lax.broadcasted_iota(jnp.int32, (channels, cols), 1)
        for tile in range(count // 32):
            edge = jnp.zeros((channels, cols), F32)
            for k in range(32):
                v = total[tile * 32 + k]
                first_ref[tile * 32 + k] = v.astype(BF16)
                edge = jnp.where(lane // 4 == k, pltpu.roll(v, (4 * k + 2) % cols, 1), edge)
            edge_ref[tile] = edge.astype(BF16)


def merge(rows, counts, data, atmos):
    steps = data.shape[0]
    count, channels, cols = atmos.shape
    return pl.pallas_call(
        merge_kernel,
        out_shape=(
            jax.ShapeDtypeStruct(atmos.shape, BF16),
            jax.ShapeDtypeStruct((count // 32, channels, cols), BF16),
        ),
        grid_spec=pltpu.PrefetchScalarGridSpec(
            num_scalar_prefetch=2,
            grid=(steps,),
            in_specs=[
                pl.BlockSpec((1,) + data.shape[1:], lambda s, a, b: (s, 0, 0, 0)),
                pl.BlockSpec(atmos.shape, lambda s, a, b: (0, 0, 0)),
            ],
            out_specs=[
                pl.BlockSpec(atmos.shape, lambda s, a, b: (0, 0, 0)),
                pl.BlockSpec((count // 32, channels, cols), lambda s, a, b: (0, 0, 0)),
            ],
            scratch_shapes=[pltpu.VMEM(atmos.shape, F32)],
        ),
        compiler_params=pltpu.CompilerParams(vmem_limit_bytes=VMEM_LIMIT),
        name="merge",
    )(rows, counts, data, atmos)


def atmos_kernel(
    inside, a_ref, top_ref, bottom_ref, side_ref, w1_ref, b1_ref, w2_ref, b2_ref, out_ref, tall, second
):
    count, channels, cols = a_ref.shape
    group = 2

    tall[0:2, :, 0:cols] = top_ref[...]
    tall[2 : 2 + count, :, 0:cols] = a_ref[...]
    tall[2 + count :, :, 0:cols] = bottom_ref[...]
    for j in range(count + 4):
        r = j - 2
        tile, k = (r // 32 + 1, r % 32)
        v = side_ref[tile].astype(F32)
        tall[j, :, cols:] = pltpu.roll(v, (126 - 4 * k) % cols, 1).astype(BF16)

    def conv(source, weight, start):
        fields = [
            jnp.concatenate([source[start + i + d] for d in range(3)], axis=0)
            for i in range(group)
        ]
        return jnp.dot(weight, jnp.concatenate(fields, axis=1), preferred_element_type=F32)

    def first(step, carry):
        start = step * group
        taps = conv(tall, w1_ref[...], start)
        for i in range(group):
            j = start + i
            value = silu(shifted_sum(taps[:, i * 2 * cols : (i + 1) * 2 * cols]) + b1_ref[...])
            keep = jnp.where(
                j == 0, inside[0], jnp.where(j == count + 1, inside[1], 1)
            ).astype(F32)
            second[j] = (value * keep).astype(BF16)
        return carry

    lax.fori_loop(0, (count + 2) // group, first, 0)

    def last(step, carry):
        start = step * group
        taps = conv(second, w2_ref[...], start)
        for i in range(group):
            j = start + i
            value = shifted_sum(taps[:, i * 2 * cols : (i + 1) * 2 * cols])[:, :cols]
            out_ref[j] = (a_ref[j].astype(F32) + (value + b2_ref[...])).astype(BF16)
        return carry

    lax.fori_loop(0, count // group, last, 0)


def atmos_step(inside, a, top, bottom, side, w1, b1, w2, b2):
    count, channels, cols = a.shape
    vmem = pl.BlockSpec(memory_space=pltpu.VMEM)
    return pl.pallas_call(
        atmos_kernel,
        out_shape=jax.ShapeDtypeStruct(a.shape, BF16),
        in_specs=[pl.BlockSpec(memory_space=pltpu.SMEM)] + [vmem] * 8,
        out_specs=vmem,
        scratch_shapes=[
            pltpu.VMEM((count + 4, channels, 2 * cols), BF16),
            pltpu.VMEM((count + 2, channels, 2 * cols), BF16),
        ],
        compiler_params=pltpu.CompilerParams(vmem_limit_bytes=VMEM_LIMIT),
        name="atmos",
    )(inside, a, top, bottom, side, w1, b1, w2, b2)


def from_left(value, axis, periodic):
    count = lax.axis_size(axis)
    pairs = [(i, i + 1) for i in range(count - 1)] + ([(count - 1, 0)] if periodic else [])
    return lax.ppermute(value, axis, pairs)


def from_right(value, axis, periodic):
    count = lax.axis_size(axis)
    pairs = [(i + 1, i) for i in range(count - 1)] + ([(0, count - 1)] if periodic else [])
    return lax.ppermute(value, axis, pairs)


def per_device(
    ocean_state,
    sea_mask,
    ocean_w1,
    ocean_b1,
    ocean_w2,
    ocean_b2,
    regrid_weight,
    route_dev,
    route_row,
    atmos_state,
    atmos_w1,
    atmos_b1,
    atmos_w2,
    atmos_b2,
):
    lat_count, lon_count = lax.axis_size("lat"), lax.axis_size("lon")
    lat, lon = lax.axis_index("lat"), lax.axis_index("lon")
    buckets = 3 * lon_count

    field = jnp.concatenate(
        [
            ocean_state,
            sea_mask.astype(BF16)[None],
            jnp.zeros((3,) + sea_mask.shape, BF16),
        ],
        axis=0,
    ).transpose(1, 0, 2)
    left = from_left(field[:, :, -128:], "lon", True)
    right = from_right(field[:, :, :128], "lon", True)
    lane = jnp.arange(128, dtype=jnp.int32)
    side = jnp.where(lane[None, None, :] < 64, right, left)
    top = from_left(jnp.concatenate([field[-2:], side[-2:]], axis=2), "lat", False)
    bottom = from_right(jnp.concatenate([field[:2], side[:2]], axis=2), "lat", False)

    target = route_dev.reshape(-1)
    slots = target.shape[0]
    bucket = (target // lon_count - lat + 1) * lon_count + target % lon_count
    order = jnp.arange(slots, dtype=jnp.int32)
    earlier = (bucket[:, None] == bucket[None, :]) & (order[None, :] < order[:, None])
    place = bucket * CAP + jnp.sum(earlier.astype(jnp.int32), axis=1)
    hit = jnp.arange(buckets * CAP, dtype=jnp.int32)[:, None] == place[None, :]
    rows_out = jnp.max(jnp.where(hit, route_row.reshape(-1)[None, :], -1), axis=1)
    rows_out = jnp.pad(
        rows_out.reshape(buckets, 1, CAP), ((0, 0), (0, 7), (0, 128 - CAP)), constant_values=-1
    )

    ocean_next, outgoing = ocean_step(
        place,
        field,
        side,
        top,
        bottom,
        stacked_weight(ocean_w1, 80),
        ocean_b1[:, None],
        stacked_weight(ocean_w2, 64),
        ocean_b2[:, None],
        regrid_weight.reshape(-1, 256, 128),
        buckets * CAP,
    )
    incoming, rows_in = exchange(
        outgoing.reshape((buckets, CAP) + outgoing.shape[1:]), rows_out, lat_count, lon_count
    )
    source_lat = lat + jnp.arange(buckets, dtype=jnp.int32) // lon_count - 1
    there = (source_lat >= 0) & (source_lat < lat_count)
    rows_in = rows_in[:, 0, :CAP]
    counts = jnp.where(there, jnp.sum((rows_in >= 0).astype(jnp.int32), axis=1), 0)

    first, edge = merge(rows_in.reshape(-1), counts, incoming, atmos_state.transpose(1, 0, 2))
    left = from_left(edge, "lon", True)
    right = from_right(edge, "lon", True)
    side = jnp.where(lane[None, None, :] % 4 < 2, left, right)
    top = from_left(jnp.concatenate([first[-2:], side[1:]], axis=0), "lat", False)
    bottom = from_right(jnp.concatenate([first[:2], side[:1]], axis=0), "lat", False)
    side = jnp.concatenate([top[2:], side, bottom[2:]], axis=0)
    inside = jnp.stack([lat > 0, lat < lat_count - 1]).astype(jnp.int32)
    atmos_next = atmos_step(
        inside,
        first,
        top[:2],
        bottom[:2],
        side,
        stacked_weight(atmos_w1, 64),
        atmos_b1[:, None],
        stacked_weight(atmos_w2, 64),
        atmos_b2[:, None],
    )
    return ocean_next.transpose(1, 0, 2), atmos_next.transpose(1, 0, 2)


def solution(mesh):
    in_specs = (
        P(None, "lat", "lon"),
        P("lat", "lon"),
        P(),
        P(),
        P(),
        P(),
        P(("lat", "lon"), None, None, None),
        P(("lat", "lon"), None),
        P(("lat", "lon"), None),
        P(None, "lat", "lon"),
        P(),
        P(),
        P(),
        P(),
    )
    out_specs = (P(None, "lat", "lon"), P(None, "lat", "lon"))
    return jax.shard_map(
        per_device, mesh=mesh, in_specs=in_specs, out_specs=out_specs, check_vma=False
    )
```

```python
import functools

import jax
import jax.numpy as jnp
from jax import lax
from jax.experimental import pallas as pl
from jax.experimental.pallas import tpu as pltpu
from jax.sharding import PartitionSpec as P

MESH = pl.DeviceIdType.MESH
F32 = jnp.float32
BF16 = jnp.bfloat16
VMEM_LIMIT = 56 * 1024 * 1024


def silu(v):
    return 0.5 * v * (1.0 + jnp.tanh(0.5 * v))


def shifted_sum(taps):
    out = taps.shape[0] // 3
    columns = taps.shape[1]
    return (
        pltpu.roll(taps[0:out], 1, 1)
        + taps[out : 2 * out]
        + pltpu.roll(taps[2 * out :], columns - 1, 1)
    )


def stacked_weight(weight, padded_in):
    out, inn = weight.shape[:2]
    weight = jnp.pad(weight, ((0, 0), (0, padded_in - inn), (0, 0), (0, 0)))
    return weight.transpose(3, 0, 2, 1).reshape(3 * out, 3 * padded_in)


def column(bias):
    n = bias.shape[1]
    at = lax.broadcasted_iota(jnp.int32, (n, n), 0) == lax.broadcasted_iota(jnp.int32, (n, n), 1)
    return jnp.sum(jnp.where(at, bias, 0.0), axis=1, keepdims=True)


def remote(src, dst, send_sem, recv_sem, lat, lon):
    return pltpu.make_async_remote_copy(
        src_ref=src,
        dst_ref=dst,
        send_sem=send_sem,
        recv_sem=recv_sem,
        device_id={"lat": lat, "lon": lon},
        device_id_type=MESH,
    )


def landed(ref, sem):
    return pltpu.make_async_copy(ref, ref, sem)


def greet(partners, waits):
    barrier = pltpu.get_barrier_semaphore()
    for lat, lon, ok in partners:

        @pl.when(ok)
        def _():
            pl.semaphore_signal(
                barrier, inc=1, device_id={"lat": lat, "lon": lon}, device_id_type=MESH
            )

    pl.semaphore_wait(barrier, waits)


def whole_any(count):
    return [pl.BlockSpec(memory_space=pl.ANY)] * count


def ocean_halo_kernel(
    lat_count, lon_count, field, top, bottom, left, right, send_sem, recv_sem
):
    lat, lon = lax.axis_index("lat"), lax.axis_index("lon")
    rows, _, cols = field.shape
    west = lax.rem(lon + lon_count - 1, lon_count)
    east = lax.rem(lon + 1, lon_count)
    up, down, always = lat > 0, lat < lat_count - 1, lat >= 0
    edge = jnp.logical_or(lat == 0, lat == lat_count - 1)
    partners = [(lat, west, always), (lat, east, always)]
    for there, ok in ((lat - 1, up), (lat + 1, down)):
        partners += [(there, side, ok) for side in (west, lon, east)]
    greet(partners, jnp.where(edge, 5, 8))

    lo, hi = pl.ds(0, 128), pl.ds(cols - 128, 128)
    first, last = pl.ds(0, 2), pl.ds(rows - 2, 2)
    own, above, below = pl.ds(2, rows), pl.ds(0, 2), pl.ds(rows + 2, 2)
    moves = [
        (field.at[:, :, lo], right.at[own], lat, west, always),
        (field.at[:, :, hi], left.at[own], lat, east, always),
        (field.at[first], bottom, lat - 1, lon, up),
        (field.at[last], top, lat + 1, lon, down),
        (field.at[first, :, lo], right.at[below], lat - 1, west, up),
        (field.at[first, :, hi], left.at[below], lat - 1, east, up),
        (field.at[last, :, lo], right.at[above], lat + 1, west, down),
        (field.at[last, :, hi], left.at[above], lat + 1, east, down),
    ]
    arrives = [always, always, down, up, down, down, up, up]
    copies = [
        (remote(src, dst, send_sem.at[i], recv_sem.at[i], a, b), ok)
        for i, (src, dst, a, b, ok) in enumerate(moves)
    ]
    for copy, ok in copies:
        pl.when(ok)(copy.start)
    for i, (copy, ok) in enumerate(copies):
        pl.when(ok)(copy.wait_send)
        pl.when(arrives[i])(landed(moves[i][1], recv_sem.at[i]).wait)


def ocean_halo(field, lat_count, lon_count):
    rows, channels, cols = field.shape
    shapes = [(2, channels, cols)] * 2 + [(rows + 4, channels, 128)] * 2
    return pl.pallas_call(
        functools.partial(ocean_halo_kernel, lat_count, lon_count),
        out_shape=[jax.ShapeDtypeStruct(s, BF16) for s in shapes],
        in_specs=whole_any(1),
        out_specs=whole_any(4),
        scratch_shapes=[pltpu.SemaphoreType.DMA((8,))] * 2,
        compiler_params=pltpu.CompilerParams(collective_id=0, has_side_effects=True),
        name="ocean_halo",
    )(field)


def ocean_kernel(
    lat_count,
    meta,
    x_ref,
    top_ref,
    bottom_ref,
    left_ref,
    right_ref,
    w1_ref,
    b1_ref,
    w2_ref,
    b2_ref,
    regrid_ref,
    next_ref,
    lists,
    codes,
    tall,
    hidden,
    contrib,
    filled,
    sem,
):
    row = lax.rem(pl.program_id(0), 16)
    rows, channels, cols = x_ref.shape
    mask_at = 76
    b1, b2 = column(b1_ref[...]), column(b2_ref[...])

    def first_conv(j):
        field = jnp.concatenate([tall[j], tall[j + 1], tall[j + 2]], axis=0)
        taps = jnp.dot(w1_ref[...], field, preferred_element_type=F32)
        mask = tall[j + 1, mask_at : mask_at + 1, :].astype(F32)
        hidden[j] = (silu(shifted_sum(taps) + b1) * mask).astype(BF16)

    @pl.when(row == 0)
    def _():
        lat = lax.axis_index("lat")
        lane = lax.broadcasted_iota(jnp.int32, (channels, 128), 1)
        tall[2 : 2 + rows, :, 0:cols] = x_ref[...]
        for j in range(rows + 4):
            side = jnp.where(lane < 64, right_ref[j], left_ref[j])
            if j < 2 or j >= rows + 2:
                inside = lat > 0 if j < 2 else lat < lat_count - 1
                main = top_ref[j] if j < 2 else bottom_ref[j - rows - 2]
                tall[j, :, 0:cols] = jnp.where(inside, main, jnp.zeros_like(main))
                side = jnp.where(inside, side, jnp.zeros_like(side))
            tall[j, :, cols:] = side
        for i in range(3):
            filled[i] = 0
        first_conv(0)
        first_conv(1)

    first_conv(lax.rem(row + 2, 16))
    field = jnp.concatenate([hidden[row], hidden[row + 1], hidden[row + 2]], axis=0)
    taps = jnp.dot(w2_ref[...], field, preferred_element_type=F32)
    mask = tall[row + 2, mask_at : mask_at + 1, :].astype(F32)
    result = ((shifted_sum(taps) + b2) * mask).astype(BF16)[:, :cols]
    next_ref[0] = result
    blocks = regrid_ref.shape[0]
    capacity = lists.shape[1]
    for q in range(blocks):
        field = result[:, q * 128 : (q + 1) * 128]
        both = lax.dot_general(
            field, regrid_ref[q], (((1,), (1,)), ((), ())), preferred_element_type=F32
        ).astype(BF16)
        for k in range(2):
            i = (row * blocks + q) * 2 + k
            contrib[i] = both[:, k * 128 : (k + 1) * 128]
            which = meta[i] // 256
            at = filled[which]
            filled[which] = at + 1
            codes[which, 0, at] = lax.rem(meta[i], 256)
            pltpu.make_async_copy(contrib.at[i], lists.at[which, at], sem).start()

    @pl.when(row == rows - 1)
    def _():
        for i in range(3):
            codes[i, 1, 0] = filled[i]
        pltpu.make_async_copy(contrib, contrib, sem).wait()


def ocean_step(meta, x, top, bottom, left, right, w1, b1, w2, b2, regrid, lat_count):
    rows, channels, cols = x.shape
    wide = cols + 128
    out = w2.shape[0] // 3
    slots = meta.shape[0]

    def whole(array):
        zeros = (0,) * array.ndim
        return pl.BlockSpec(array.shape, lambda r, meta: zeros)

    blocks = regrid.shape[0] // rows
    return pl.pallas_call(
        functools.partial(ocean_kernel, lat_count),
        out_shape=(
            jax.ShapeDtypeStruct((rows, out, cols), BF16),
            jax.ShapeDtypeStruct((3, slots, out, 128), BF16),
            jax.ShapeDtypeStruct((3, 8, 128), jnp.int32),
        ),
        grid_spec=pltpu.PrefetchScalarGridSpec(
            num_scalar_prefetch=1,
            grid=(rows,),
            in_specs=[whole(a) for a in (x, top, bottom, left, right, w1, b1, w2, b2)]
            + [pl.BlockSpec((blocks, 256, 128), lambda r, meta: (r, 0, 0))],
            out_specs=[
                pl.BlockSpec((1, out, cols), lambda r, meta: (r, 0, 0)),
                pl.BlockSpec(memory_space=pl.ANY),
                pl.BlockSpec(memory_space=pltpu.SMEM),
            ],
            scratch_shapes=[
                pltpu.VMEM((rows + 4, channels, wide), BF16),
                pltpu.VMEM((rows + 2, out, wide), BF16),
                pltpu.VMEM((slots, out, 128), BF16),
                pltpu.SMEM((3,), jnp.int32),
                pltpu.SemaphoreType.DMA,
            ],
        ),
        compiler_params=pltpu.CompilerParams(vmem_limit_bytes=VMEM_LIMIT),
        name="ocean",
    )(meta, x, top, bottom, left, right, w1, b1, w2, b2, regrid)


def lists_kernel(lat_count, count, lists, codes, north, north_codes, south, south_codes, send, recv):
    lat, lon = lax.axis_index("lat"), lax.axis_index("lon")
    up, down = lat > 0, lat < lat_count - 1
    greet([(lat - 1, lon, up), (lat + 1, lon, down)], jnp.where(jnp.logical_and(up, down), 2, 1))
    some = pl.ds(0, count)
    moves = [
        (lists.at[0, some], south.at[some], lat - 1, up, down),
        (codes.at[0], south_codes, lat - 1, up, down),
        (lists.at[2, some], north.at[some], lat + 1, down, up),
        (codes.at[2], north_codes, lat + 1, down, up),
    ]
    copies = [
        remote(src, dst, send.at[i], recv.at[i], there, lon)
        for i, (src, dst, there, _, _) in enumerate(moves)
    ]
    for copy, move in zip(copies, moves):
        pl.when(move[3])(copy.start)
    for i, (copy, move) in enumerate(zip(copies, moves)):
        pl.when(move[3])(copy.wait_send)
        pl.when(move[4])(landed(move[1], recv.at[i]).wait)


def send_lists(lists, codes, count, collective_id, lat_count):
    one = jax.ShapeDtypeStruct(lists.shape[1:], BF16)
    code = jax.ShapeDtypeStruct(codes.shape[1:], jnp.int32)
    return pl.pallas_call(
        functools.partial(lists_kernel, lat_count, count),
        out_shape=[one, code, one, code],
        in_specs=whole_any(2),
        out_specs=whole_any(4),
        scratch_shapes=[pltpu.SemaphoreType.DMA((4,))] * 2,
        compiler_params=pltpu.CompilerParams(collective_id=collective_id, has_side_effects=True),
        name="send_lists",
    )(lists, codes)


PIECE = 16


def merge_kernel(
    lat_count, own_codes, north_codes, south_codes, lists, north, south, out, slots, total, packed, sem, out_sem
):
    lat = lax.axis_index("lat")
    own_count = own_codes[1, 1, 0]
    north_count = jnp.where(lat > 0, north_codes[1, 0], 0)
    south_count = jnp.where(lat < lat_count - 1, south_codes[1, 0], 0)
    capacity = slots.shape[1]
    sources = (
        (lists.at[1], lambda s: own_codes[1, 0, s], own_count),
        (north, lambda s: north_codes[0, s], north_count),
        (south, lambda s: south_codes[0, s], south_count),
    )

    def pieces(i, action):
        for p in range(capacity // PIECE):
            some = pl.ds(p * PIECE, PIECE)
            copy = pltpu.make_async_copy(sources[i][0].at[some], slots.at[i, some], sem.at[i, p])
            pl.when(sources[i][2] > p * PIECE)(getattr(copy, action))

    for i in range(3):
        pieces(i, "start")
    total[...] = jnp.zeros_like(total)
    for i in range(3):
        pieces(i, "wait")
        _, code, count = sources[i]

        def add(s, carry):
            r = code(s)
            total[r] = total[r] + slots[i, s].astype(F32)
            return carry

        lax.fori_loop(0, count, add, 0)
    parts, rows = out.shape[:2]
    copies = []
    for e in range(parts):
        packed[e] = total[e * rows : (e + 1) * rows].astype(BF16)
        copies.append(pltpu.make_async_copy(packed.at[e], out.at[e], out_sem.at[e]))
        copies[-1].start()
    for copy in copies:
        copy.wait()


def merge(codes, lists, north, north_codes, south, south_codes, lat_count, lon_count, rows):
    slots, channels, cols = lists.shape[1:]
    smem = pl.BlockSpec(memory_space=pltpu.SMEM)
    shape = (lon_count, rows, channels, cols)
    return pl.pallas_call(
        functools.partial(merge_kernel, lat_count),
        out_shape=jax.ShapeDtypeStruct(shape, BF16),
        in_specs=[smem] * 3 + whole_any(3),
        out_specs=pl.BlockSpec(memory_space=pl.ANY),
        scratch_shapes=[
            pltpu.VMEM((3, slots, channels, cols), BF16),
            pltpu.VMEM((lon_count * rows, channels, cols), F32),
            pltpu.VMEM(shape, BF16),
            pltpu.SemaphoreType.DMA((3, slots // PIECE)),
            pltpu.SemaphoreType.DMA((lon_count,)),
        ],
        compiler_params=pltpu.CompilerParams(vmem_limit_bytes=VMEM_LIMIT),
        name="merge",
    )(codes, north_codes, south_codes, lists, north, south)


def gather_kernel(
    lat_count,
    lon_count,
    dense,
    atmos,
    first,
    top,
    bottom,
    left,
    right,
    mine,
    from_core,
    to_z,
    from_z,
    edges,
    load_sem,
    core_send,
    core_recv,
    z_send,
    z_recv,
    halo_send,
    halo_recv,
):
    lat, lon = lax.axis_index("lat"), lax.axis_index("lon")
    west = lax.rem(lon + lon_count - 1, lon_count)
    east = lax.rem(lon + 1, lon_count)
    across = lax.rem(lon + 2, lon_count)
    core = lax.rem(lon, 2)
    beside = lon + 1 - 2 * core
    beside_across = lax.rem(beside + 2, lon_count)
    up, down, always = lat > 0, lat < lat_count - 1, lat >= 0
    edge = jnp.logical_or(lat == 0, lat == lat_count - 1)
    partners = [(lat, there, always) for there in (west, east, across)]
    for there, ok in ((lat - 1, up), (lat + 1, down)):
        partners += [(there, side, ok) for side in (west, lon, east)]
    greet(partners, jnp.where(edge, 6, 9))

    rows, channels, cols = first.shape
    chunks = to_z.shape[0] // 16
    some = [pl.ds(c * 16, 16) for c in range(chunks)]
    core_copies, loads = [], []
    for part, (theirs, ours) in enumerate(((beside_across, across), (beside, lon))):
        for c in range(chunks):
            core_copies.append(
                remote(
                    dense.at[theirs, some[c]],
                    from_core.at[part, some[c]],
                    core_send.at[part, c],
                    core_recv.at[part, c],
                    lat,
                    beside,
                )
            )
            loads.append(
                pltpu.make_async_copy(
                    dense.at[ours, some[c]], mine.at[part, some[c]], load_sem.at[part, c]
                )
            )
    for a, b in zip(core_copies, loads):
        a.start()
        b.start()
    z_copies = []
    for c in range(chunks):
        loads[c].wait()
        landed(from_core.at[0, some[c]], core_recv.at[0, c]).wait()
        to_z[some[c]] = (
            mine[0, some[c]].astype(F32) + from_core[0, some[c]].astype(F32)
        ).astype(BF16)
        z_copies.append(
            remote(to_z.at[some[c]], from_z.at[some[c]], z_send.at[c], z_recv.at[c], lat, across)
        )
        z_copies[c].start()
    for c in range(chunks):
        loads[chunks + c].wait()
        landed(from_core.at[1, some[c]], core_recv.at[1, c]).wait()
    lane = lax.broadcasted_iota(jnp.int32, (channels, cols), 1)
    for c in range(chunks):
        landed(from_z.at[some[c]], z_recv.at[c]).wait()
        tile = c * 16 // 32
        part = jnp.zeros((channels, cols), F32) if c % 2 == 0 else part
        for k in range(16):
            r = c * 16 + k
            flux = mine[1, r].astype(F32) + from_core[1, r].astype(F32) + from_z[r].astype(F32)
            v = (atmos[r].astype(F32) + flux).astype(BF16)
            first[r] = v
            at = r % 32
            part = jnp.where(
                lane // 4 == at, pltpu.roll(v.astype(F32), (4 * at + 2) % cols, 1), part
            )
        if c % 2 == 1:
            edges[tile] = part.astype(BF16)
    tiles = edges.shape[0]
    lo, hi = edges.at[0], edges.at[tiles - 1]
    moves = [
        (edges, right.at[pl.ds(1, tiles)], lat, west, always, always),
        (edges, left.at[pl.ds(1, tiles)], lat, east, always, always),
        (first.at[pl.ds(0, 2)], bottom, lat - 1, lon, up, down),
        (first.at[pl.ds(rows - 2, 2)], top, lat + 1, lon, down, up),
        (lo, right.at[tiles + 1], lat - 1, west, up, down),
        (lo, left.at[tiles + 1], lat - 1, east, up, down),
        (hi, right.at[0], lat + 1, west, down, up),
        (hi, left.at[0], lat + 1, east, down, up),
    ]
    copies = [
        remote(src, dst, halo_send.at[i], halo_recv.at[i], a, b)
        for i, (src, dst, a, b, _, _) in enumerate(moves)
    ]
    for copy, move in zip(copies, moves):
        pl.when(move[4])(copy.start)
    for copy in core_copies + z_copies:
        copy.wait_send()
    for i, (copy, move) in enumerate(zip(copies, moves)):
        pl.when(move[4])(copy.wait_send)
        pl.when(move[5])(landed(move[1], halo_recv.at[i]).wait)


def gather(dense, atmos, lat_count, lon_count):
    rows, channels, cols = atmos.shape
    tiles = rows // 32
    vmem = pl.BlockSpec(memory_space=pltpu.VMEM)
    dma = pltpu.SemaphoreType.DMA
    shapes = [(rows, channels, cols)] + [(2, channels, cols)] * 2 + [(tiles + 2, channels, cols)] * 2
    return pl.pallas_call(
        functools.partial(gather_kernel, lat_count, lon_count),
        out_shape=[jax.ShapeDtypeStruct(s, BF16) for s in shapes],
        in_specs=whole_any(1) + [vmem],
        out_specs=[vmem] + whole_any(4),
        scratch_shapes=[
            pltpu.VMEM((2, rows, channels, cols), BF16),
            pltpu.VMEM((2, rows, channels, cols), BF16),
            pltpu.VMEM((rows, channels, cols), BF16),
            pltpu.VMEM((rows, channels, cols), BF16),
            pltpu.VMEM((tiles, channels, cols), BF16),
            dma((2, rows // 16)),
            dma((2, rows // 16)),
            dma((2, rows // 16)),
            dma((rows // 16,)),
            dma((rows // 16,)),
            dma((8,)),
            dma((8,)),
        ],
        compiler_params=pltpu.CompilerParams(
            collective_id=1, has_side_effects=True, vmem_limit_bytes=VMEM_LIMIT
        ),
        name="gather",
    )(dense, atmos)


def atmos_kernel(
    lat_count, a_ref, top_ref, bottom_ref, left_ref, right_ref, w1_ref, b1_ref, w2_ref, b2_ref, out_ref, tall, second
):
    count, channels, cols = a_ref.shape
    group = 2
    lat = lax.axis_index("lat")
    b1, b2 = column(b1_ref[...]), column(b2_ref[...])

    tall[2 : 2 + count, :, 0:cols] = a_ref[...]
    lane = lax.broadcasted_iota(jnp.int32, (channels, cols), 1)
    for tile in range(count // 32 + 2):
        side = jnp.where(lane % 4 < 2, left_ref[tile], right_ref[tile]).astype(F32)
        for k in range(32):
            r = tile * 32 - 32 + k
            if r < -2 or r >= count + 2:
                continue
            v = pltpu.roll(side, (126 - 4 * k) % cols, 1).astype(BF16)
            if r < 0 or r >= count:
                inside = lat > 0 if r < 0 else lat < lat_count - 1
                main = top_ref[r + 2] if r < 0 else bottom_ref[r - count]
                tall[r + 2, :, 0:cols] = jnp.where(inside, main, jnp.zeros_like(main))
                v = jnp.where(inside, v, jnp.zeros_like(v))
            tall[r + 2, :, cols:] = v

    def conv(source, weight, start):
        fields = [
            jnp.concatenate([source[start + i + d] for d in range(3)], axis=0)
            for i in range(group)
        ]
        return jnp.dot(weight, jnp.concatenate(fields, axis=1), preferred_element_type=F32)

    def first(step, carry):
        start = step * group
        taps = conv(tall, w1_ref[...], start)
        for i in range(group):
            j = start + i
            value = silu(shifted_sum(taps[:, i * 2 * cols : (i + 1) * 2 * cols]) + b1)
            outside = jnp.logical_or(
                jnp.logical_and(j == 0, lat == 0),
                jnp.logical_and(j == count + 1, lat == lat_count - 1),
            )
            second[j] = jnp.where(outside, 0.0, value).astype(BF16)
        return carry

    lax.fori_loop(0, (count + 2) // group, first, 0)

    def last(step, carry):
        start = step * group
        taps = conv(second, w2_ref[...], start)
        for i in range(group):
            j = start + i
            value = shifted_sum(taps[:, i * 2 * cols : (i + 1) * 2 * cols])[:, :cols]
            out_ref[j] = (a_ref[j].astype(F32) + (value + b2)).astype(BF16)
        return carry

    lax.fori_loop(0, count // group, last, 0)


def atmos_step(a, top, bottom, left, right, w1, b1, w2, b2, lat_count):
    count, channels, cols = a.shape
    vmem = pl.BlockSpec(memory_space=pltpu.VMEM)
    return pl.pallas_call(
        functools.partial(atmos_kernel, lat_count),
        out_shape=jax.ShapeDtypeStruct(a.shape, BF16),
        in_specs=[vmem] * 9,
        out_specs=vmem,
        scratch_shapes=[
            pltpu.VMEM((count + 4, channels, 2 * cols), BF16),
            pltpu.VMEM((count + 2, channels, 2 * cols), BF16),
        ],
        compiler_params=pltpu.CompilerParams(vmem_limit_bytes=VMEM_LIMIT),
        name="atmos",
    )(a, top, bottom, left, right, w1, b1, w2, b2)


def per_device(
    ocean_state,
    sea_mask,
    ocean_w1,
    ocean_b1,
    ocean_w2,
    ocean_b2,
    regrid_weight,
    route_dev,
    route_row,
    atmos_state,
    atmos_w1,
    atmos_b1,
    atmos_w2,
    atmos_b2,
):
    lat_count, lon_count = lax.axis_size("lat"), lax.axis_size("lon")
    lat = lax.axis_index("lat")
    atmos_rows = atmos_state.shape[1]

    field = jnp.concatenate(
        [
            ocean_state,
            sea_mask.astype(BF16)[None],
            jnp.zeros((3,) + sea_mask.shape, BF16),
        ],
        axis=0,
    ).transpose(1, 0, 2)
    top, bottom, left, right = ocean_halo(field, lat_count, lon_count)

    meta = (route_dev - (lat - 1) * lon_count) * atmos_rows + route_row

    ocean_next, lists, codes = ocean_step(
        meta.reshape(-1),
        field,
        top,
        bottom,
        left,
        right,
        stacked_weight(ocean_w1, 80),
        ocean_b1[None, :],
        stacked_weight(ocean_w2, 64),
        ocean_b2[None, :],
        regrid_weight.reshape(-1, 256, 128),
        lat_count,
    )
    north, north_codes, south, south_codes = send_lists(
        lists, codes, lists.shape[1], 2, lat_count
    )
    dense = merge(
        codes, lists, north, north_codes, south, south_codes, lat_count, lon_count, atmos_rows
    )
    first, top, bottom, left, right = gather(
        dense, atmos_state.transpose(1, 0, 2), lat_count, lon_count
    )
    atmos_next = atmos_step(
        first,
        top,
        bottom,
        left,
        right,
        stacked_weight(atmos_w1, 64),
        atmos_b1[None, :],
        stacked_weight(atmos_w2, 64),
        atmos_b2[None, :],
        lat_count,
    )
    return ocean_next.transpose(1, 0, 2), atmos_next.transpose(1, 0, 2)


def solution(mesh):
    in_specs = (
        P(None, "lat", "lon"),
        P("lat", "lon"),
        P(),
        P(),
        P(),
        P(),
        P(("lat", "lon"), None, None, None),
        P(("lat", "lon"), None),
        P(("lat", "lon"), None),
        P(None, "lat", "lon"),
        P(),
        P(),
        P(),
        P(),
    )
    out_specs = (P(None, "lat", "lon"), P(None, "lat", "lon"))
    return jax.shard_map(
        per_device, mesh=mesh, in_specs=in_specs, out_specs=out_specs, check_vma=False
    )
```

```python
import functools

import jax
import jax.numpy as jnp
from jax import lax
from jax.experimental import pallas as pl
from jax.experimental.pallas import tpu as pltpu
from jax.sharding import PartitionSpec as P

MESH = pl.DeviceIdType.MESH
F32 = jnp.float32
BF16 = jnp.bfloat16
VMEM_LIMIT = 56 * 1024 * 1024
GROUPS = 4


def silu(v):
    return 0.5 * v * (1.0 + jnp.tanh(0.5 * v))


def shifted_sum(taps):
    out = taps.shape[0] // 3
    columns = taps.shape[1]
    return (
        pltpu.roll(taps[0:out], 1, 1)
        + taps[out : 2 * out]
        + pltpu.roll(taps[2 * out :], columns - 1, 1)
    )


def stacked_weight(weight, padded_in):
    out, inn = weight.shape[:2]
    weight = jnp.pad(weight, ((0, 0), (0, padded_in - inn), (0, 0), (0, 0)))
    return weight.transpose(3, 0, 2, 1).reshape(3 * out, 3 * padded_in)


def column(bias):
    n = bias.shape[1]
    at = lax.broadcasted_iota(jnp.int32, (n, n), 0) == lax.broadcasted_iota(jnp.int32, (n, n), 1)
    return jnp.sum(jnp.where(at, bias, 0.0), axis=1, keepdims=True)


def remote(src, dst, send_sem, recv_sem, lat, lon):
    return pltpu.make_async_remote_copy(
        src_ref=src,
        dst_ref=dst,
        send_sem=send_sem,
        recv_sem=recv_sem,
        device_id={"lat": lat, "lon": lon},
        device_id_type=MESH,
    )


def landed(ref, sem):
    return pltpu.make_async_copy(ref, ref, sem)


def greet(partners, waits):
    barrier = pltpu.get_barrier_semaphore()
    for lat, lon, ok in partners:

        @pl.when(ok)
        def _():
            pl.semaphore_signal(
                barrier, inc=1, device_id={"lat": lat, "lon": lon}, device_id_type=MESH
            )

    pl.semaphore_wait(barrier, waits)


def whole_any(count):
    return [pl.BlockSpec(memory_space=pl.ANY)] * count


def ocean_halo_kernel(
    lat_count,
    lon_count,
    field,
    index,
    top,
    bottom,
    left,
    right,
    north_index,
    south_index,
    send_sem,
    recv_sem,
):
    lat, lon = lax.axis_index("lat"), lax.axis_index("lon")
    rows, _, cols = field.shape
    west = lax.rem(lon + lon_count - 1, lon_count)
    east = lax.rem(lon + 1, lon_count)
    up, down, always = lat > 0, lat < lat_count - 1, lat >= 0
    edge = jnp.logical_or(lat == 0, lat == lat_count - 1)
    partners = [(lat, west, always), (lat, east, always)]
    for there, ok in ((lat - 1, up), (lat + 1, down)):
        partners += [(there, side, ok) for side in (west, lon, east)]
    greet(partners, jnp.where(edge, 5, 8))

    lo, hi = pl.ds(0, 128), pl.ds(cols - 128, 128)
    first, last = pl.ds(0, 2), pl.ds(rows - 2, 2)
    own, above, below = pl.ds(2, rows), pl.ds(0, 2), pl.ds(rows + 2, 2)
    moves = [
        (field.at[:, :, lo], right.at[own], lat, west, always),
        (field.at[:, :, hi], left.at[own], lat, east, always),
        (field.at[first], bottom, lat - 1, lon, up),
        (field.at[last], top, lat + 1, lon, down),
        (field.at[first, :, lo], right.at[below], lat - 1, west, up),
        (field.at[first, :, hi], left.at[below], lat - 1, east, up),
        (field.at[last, :, lo], right.at[above], lat + 1, west, down),
        (field.at[last, :, hi], left.at[above], lat + 1, east, down),
        (index.at[0], south_index, lat - 1, lon, up),
        (index.at[2], north_index, lat + 1, lon, down),
    ]
    arrives = [always, always, down, up, down, down, up, up, down, up]
    copies = [
        (remote(src, dst, send_sem.at[i], recv_sem.at[i], a, b), ok)
        for i, (src, dst, a, b, ok) in enumerate(moves)
    ]
    for copy, ok in copies:
        pl.when(ok)(copy.start)
    for i, (copy, ok) in enumerate(copies):
        pl.when(ok)(copy.wait_send)
        pl.when(arrives[i])(landed(moves[i][1], recv_sem.at[i]).wait)


def ocean_halo(field, index, lat_count, lon_count):
    rows, channels, cols = field.shape
    shapes = [(2, channels, cols)] * 2 + [(rows + 4, channels, 128)] * 2
    table = jax.ShapeDtypeStruct(index.shape[1:], jnp.int32)
    return pl.pallas_call(
        functools.partial(ocean_halo_kernel, lat_count, lon_count),
        out_shape=[jax.ShapeDtypeStruct(s, BF16) for s in shapes] + [table] * 2,
        in_specs=whole_any(2),
        out_specs=whole_any(6),
        scratch_shapes=[pltpu.SemaphoreType.DMA((10,))] * 2,
        compiler_params=pltpu.CompilerParams(collective_id=0, has_side_effects=True),
        name="ocean_halo",
    )(field, index)


def ocean_kernel(
    lat_count,
    meta,
    x_ref,
    top_ref,
    bottom_ref,
    left_ref,
    right_ref,
    w1_ref,
    b1_ref,
    w2_ref,
    b2_ref,
    regrid_ref,
    next_ref,
    slots_ref,
    tall,
    hidden,
    sums,
):
    row = lax.rem(pl.program_id(0), 16)
    rows, channels, cols = x_ref.shape
    mask_at = 76
    b1, b2 = column(b1_ref[...]), column(b2_ref[...])

    def first_conv(j):
        field = jnp.concatenate([tall[j], tall[j + 1], tall[j + 2]], axis=0)
        taps = jnp.dot(w1_ref[...], field, preferred_element_type=F32)
        mask = tall[j + 1, mask_at : mask_at + 1, :].astype(F32)
        hidden[j] = (silu(shifted_sum(taps) + b1) * mask).astype(BF16)

    @pl.when(row == 0)
    def _():
        lat = lax.axis_index("lat")
        lane = lax.broadcasted_iota(jnp.int32, (channels, 128), 1)
        tall[2 : 2 + rows, :, 0:cols] = x_ref[...]
        for j in range(rows + 4):
            side = jnp.where(lane < 64, right_ref[j], left_ref[j])
            if j < 2 or j >= rows + 2:
                inside = lat > 0 if j < 2 else lat < lat_count - 1
                main = top_ref[j] if j < 2 else bottom_ref[j - rows - 2]
                tall[j, :, 0:cols] = jnp.where(inside, main, jnp.zeros_like(main))
                side = jnp.where(inside, side, jnp.zeros_like(side))
            tall[j, :, cols:] = side
        first_conv(0)
        first_conv(1)

    first_conv(lax.rem(row + 2, 16))
    field = jnp.concatenate([hidden[row], hidden[row + 1], hidden[row + 2]], axis=0)
    taps = jnp.dot(w2_ref[...], field, preferred_element_type=F32)
    mask = tall[row + 2, mask_at : mask_at + 1, :].astype(F32)
    result = ((shifted_sum(taps) + b2) * mask).astype(BF16)[:, :cols]
    next_ref[0] = result
    blocks = regrid_ref.shape[0]
    for q in range(blocks):
        field = result[:, q * 128 : (q + 1) * 128]
        both = lax.dot_general(
            field, regrid_ref[q], (((1,), (1,)), ((), ())), preferred_element_type=F32
        ).astype(BF16)
        for k in range(2):
            what = meta[(row * blocks + q) * 2 + k]
            at = what // 2
            value = both[:, k * 128 : (k + 1) * 128].astype(F32)
            sums[at] = jnp.where(lax.rem(what, 2) == 1, value, sums[at] + value)

    @pl.when(row == rows - 1)
    def _():
        groups, slots, size = slots_ref.shape[:3]

        def rounded(i, carry):
            for g in range(groups):
                slots_ref[g, i] = sums[i, g * size : (g + 1) * size].astype(BF16)
            return carry

        lax.fori_loop(0, slots, rounded, 0)


def ocean_step(meta, x, top, bottom, left, right, w1, b1, w2, b2, regrid, lat_count):
    rows, channels, cols = x.shape
    wide = cols + 128
    out = w2.shape[0] // 3
    slots = meta.shape[0]

    def whole(array):
        zeros = (0,) * array.ndim
        return pl.BlockSpec(array.shape, lambda r, meta: zeros)

    blocks = regrid.shape[0] // rows
    return pl.pallas_call(
        functools.partial(ocean_kernel, lat_count),
        out_shape=(
            jax.ShapeDtypeStruct((rows, out, cols), BF16),
            jax.ShapeDtypeStruct((GROUPS, slots, out // GROUPS, 128), BF16),
        ),
        grid_spec=pltpu.PrefetchScalarGridSpec(
            num_scalar_prefetch=1,
            grid=(rows,),
            in_specs=[whole(a) for a in (x, top, bottom, left, right, w1, b1, w2, b2)]
            + [pl.BlockSpec((blocks, 256, 128), lambda r, meta: (r, 0, 0))],
            out_specs=[
                pl.BlockSpec((1, out, cols), lambda r, meta: (r, 0, 0)),
                pl.BlockSpec((GROUPS, slots, out // GROUPS, 128), lambda r, meta: (0, 0, 0, 0)),
            ],
            scratch_shapes=[
                pltpu.VMEM((rows + 4, channels, wide), BF16),
                pltpu.VMEM((rows + 2, out, wide), BF16),
                pltpu.VMEM((slots, out, 128), F32),
            ],
        ),
        compiler_params=pltpu.CompilerParams(vmem_limit_bytes=VMEM_LIMIT),
        name="ocean",
    )(meta, x, top, bottom, left, right, w1, b1, w2, b2, regrid)


def couple_kernel(
    lat_count,
    lon_count,
    count,
    own_index,
    north_index,
    south_index,
    slots,
    atmos,
    first,
    top,
    bottom,
    left,
    right,
    *scratch,
):
    lat, lon = lax.axis_index("lat"), lax.axis_index("lon")
    west = lax.rem(lon + lon_count - 1, lon_count)
    east = lax.rem(lon + 1, lon_count)
    across = lax.rem(lon + 2, lon_count)
    beside = lon + 1 - 2 * lax.rem(lon, 2)
    beside_across = lax.rem(beside + 2, lon_count)
    up, down, always = lat > 0, lat < lat_count - 1, lat >= 0
    edge = jnp.logical_or(lat == 0, lat == lat_count - 1)
    partners = [(lat, there, always) for there in (west, east, across)]
    for there, ok in ((lat - 1, up), (lat + 1, down)):
        partners += [(there, side, ok) for side in (west, lon, east)]
    greet(partners, jnp.where(edge, 6, 9))

    groups, total, size, cols = slots.shape
    rows, channels = first.shape[:2]
    own, north, south = (scratch[i * groups : (i + 1) * groups] for i in range(3))
    away, mine, from_core, to_z, from_z, edges = scratch[3 * groups : 3 * groups + 6]
    load_sem, y_send, y_recv, core_send, core_recv, z_send, z_recv, halo_send, halo_recv = scratch[
        3 * groups + 6 :
    ]
    low, high = pl.ds(0, count), pl.ds(total - count, count)
    everything = pl.ds(0, total)
    to_south, to_north, loads = [], [], []
    for g in range(groups):
        to_south.append(
            remote(
                slots.at[g, high], north[g].at[high], y_send.at[0, g], y_recv.at[0, g], lat + 1, lon
            )
        )
        to_north.append(
            remote(
                slots.at[g, low], south[g].at[low], y_send.at[1, g], y_recv.at[1, g], lat - 1, lon
            )
        )
        loads.append(
            pltpu.make_async_copy(slots.at[g], own[g].at[everything], load_sem.at[g])
        )
        pl.when(down)(to_south[g].start)
        pl.when(up)(to_north[g].start)
        loads[g].start()
    for buffer in (own, north, south):
        for g in range(groups):
            buffer[g][total] = jnp.zeros((size, cols), BF16)

    def dense(g, lon_there, store):
        def row(t, carry):
            at = lon_there * rows + t
            i, j = at // 128, lax.rem(at, 128)
            a = own_index[1, i, j]
            b = jnp.where(up, north_index[i, j], total)
            c = jnp.where(down, south_index[i, j], total)
            value = own[g][a].astype(F32) + north[g][b].astype(F32) + south[g][c].astype(F32)
            store(t, value.astype(BF16))
            return carry

        lax.fori_loop(0, rows, row, 0, unroll=8)

    core_copies, z_copies = [], []
    for g in range(groups):
        loads[g].wait()
        pl.when(up)(landed(north[g].at[high], y_recv.at[0, g]).wait)
        pl.when(down)(landed(south[g].at[low], y_recv.at[1, g]).wait)
        for part, (theirs, ours) in enumerate(((beside_across, across), (beside, lon))):

            def put_away(t, value):
                away[part, g, t] = value

            def put_mine(t, value):
                mine[part, g, t] = value

            dense(g, theirs, put_away)
            copy = remote(
                away.at[part, g],
                from_core.at[part, g],
                core_send.at[part, g],
                core_recv.at[part, g],
                lat,
                beside,
            )
            copy.start()
            core_copies.append(copy)
            dense(g, ours, put_mine)
            if part == 0:
                landed(from_core.at[0, g], core_recv.at[0, g]).wait()
                to_z[g] = (mine[0, g].astype(F32) + from_core[0, g].astype(F32)).astype(BF16)
                copy = remote(
                    to_z.at[g], from_z.at[g], z_send.at[g], z_recv.at[g], lat, across
                )
                copy.start()
                z_copies.append(copy)

    lane = lax.broadcasted_iota(jnp.int32, (size, cols), 1)
    tiles = edges.shape[0]
    for g in range(groups):
        landed(from_core.at[1, g], core_recv.at[1, g]).wait()
        landed(from_z.at[g], z_recv.at[g]).wait()
        part = pl.ds(g * size, size)
        for tile in range(tiles):
            edge = jnp.zeros((size, cols), F32)
            for k in range(32):
                r = tile * 32 + k
                flux = (
                    mine[1, g, r].astype(F32)
                    + from_core[1, g, r].astype(F32)
                    + from_z[g, r].astype(F32)
                )
                v = (atmos[r, part].astype(F32) + flux).astype(BF16)
                first[r, part] = v
                rolled = pltpu.roll(v.astype(F32), (4 * k + 2) % cols, 1)
                edge = jnp.where(lane // 4 == k, rolled, edge)
            edges[tile, part] = edge.astype(BF16)
    lo, hi = edges.at[0], edges.at[tiles - 1]
    moves = [
        (edges, right.at[pl.ds(1, tiles)], lat, west, always, always),
        (edges, left.at[pl.ds(1, tiles)], lat, east, always, always),
        (first.at[pl.ds(0, 2)], bottom, lat - 1, lon, up, down),
        (first.at[pl.ds(rows - 2, 2)], top, lat + 1, lon, down, up),
        (lo, right.at[tiles + 1], lat - 1, west, up, down),
        (lo, left.at[tiles + 1], lat - 1, east, up, down),
        (hi, right.at[0], lat + 1, west, down, up),
        (hi, left.at[0], lat + 1, east, down, up),
    ]
    copies = [
        remote(src, dst, halo_send.at[i], halo_recv.at[i], a, b)
        for i, (src, dst, a, b, _, _) in enumerate(moves)
    ]
    for copy, move in zip(copies, moves):
        pl.when(move[4])(copy.start)
    for copy in core_copies + z_copies:
        copy.wait_send()
    for g in range(groups):
        pl.when(down)(to_south[g].wait_send)
        pl.when(up)(to_north[g].wait_send)
    for i, (copy, move) in enumerate(zip(copies, moves)):
        pl.when(move[4])(copy.wait_send)
        pl.when(move[5])(landed(move[1], halo_recv.at[i]).wait)


def couple(index, north_index, south_index, slots, atmos, count, collective_id, lat_count, lon_count):
    groups, total, size, cols = slots.shape
    rows, channels, cols = atmos.shape
    tiles = rows // 32
    vmem = pl.BlockSpec(memory_space=pltpu.VMEM)
    smem = pl.BlockSpec(memory_space=pltpu.SMEM)
    dma = pltpu.SemaphoreType.DMA
    shapes = [(rows, channels, cols)] + [(2, channels, cols)] * 2 + [(tiles + 2, channels, cols)] * 2
    received = pltpu.VMEM((total + 1, size, cols), BF16)
    one = pltpu.VMEM((groups, rows, size, cols), BF16)
    two = pltpu.VMEM((2, groups, rows, size, cols), BF16)
    return pl.pallas_call(
        functools.partial(couple_kernel, lat_count, lon_count, count),
        out_shape=[jax.ShapeDtypeStruct(s, BF16) for s in shapes],
        in_specs=[smem] * 3 + whole_any(1) + [vmem],
        out_specs=[vmem] + whole_any(4),
        scratch_shapes=[received] * (3 * groups)
        + [two] * 3
        + [one] * 2
        + [pltpu.VMEM((tiles, channels, cols), BF16)]
        + [dma((groups,))]
        + [dma((2, groups))] * 4
        + [dma((groups,))] * 2
        + [dma((8,))] * 2,
        compiler_params=pltpu.CompilerParams(
            collective_id=collective_id, has_side_effects=True, vmem_limit_bytes=VMEM_LIMIT
        ),
        name="couple",
    )(index, north_index, south_index, slots, atmos)


def atmos_kernel(
    lat_count, a_ref, top_ref, bottom_ref, left_ref, right_ref, w1_ref, b1_ref, w2_ref, b2_ref, out_ref, tall, second
):
    count, channels, cols = a_ref.shape
    group = 2
    lat = lax.axis_index("lat")
    b1, b2 = column(b1_ref[...]), column(b2_ref[...])

    tall[2 : 2 + count, :, 0:cols] = a_ref[...]
    lane = lax.broadcasted_iota(jnp.int32, (channels, cols), 1)
    for tile in range(count // 32 + 2):
        side = jnp.where(lane % 4 < 2, left_ref[tile], right_ref[tile]).astype(F32)
        for k in range(32):
            r = tile * 32 - 32 + k
            if r < -2 or r >= count + 2:
                continue
            v = pltpu.roll(side, (126 - 4 * k) % cols, 1).astype(BF16)
            if r < 0 or r >= count:
                inside = lat > 0 if r < 0 else lat < lat_count - 1
                main = top_ref[r + 2] if r < 0 else bottom_ref[r - count]
                tall[r + 2, :, 0:cols] = jnp.where(inside, main, jnp.zeros_like(main))
                v = jnp.where(inside, v, jnp.zeros_like(v))
            tall[r + 2, :, cols:] = v

    def conv(source, weight, start):
        fields = [
            jnp.concatenate([source[start + i + d] for d in range(3)], axis=0)
            for i in range(group)
        ]
        return jnp.dot(weight, jnp.concatenate(fields, axis=1), preferred_element_type=F32)

    def first(step, carry):
        start = step * group
        taps = conv(tall, w1_ref[...], start)
        for i in range(group):
            j = start + i
            value = silu(shifted_sum(taps[:, i * 2 * cols : (i + 1) * 2 * cols]) + b1)
            outside = jnp.logical_or(
                jnp.logical_and(j == 0, lat == 0),
                jnp.logical_and(j == count + 1, lat == lat_count - 1),
            )
            second[j] = jnp.where(outside, 0.0, value).astype(BF16)
        return carry

    lax.fori_loop(0, (count + 2) // group, first, 0)

    def last(step, carry):
        start = step * group
        taps = conv(second, w2_ref[...], start)
        for i in range(group):
            j = start + i
            value = shifted_sum(taps[:, i * 2 * cols : (i + 1) * 2 * cols])[:, :cols]
            out_ref[j] = (a_ref[j].astype(F32) + (value + b2)).astype(BF16)
        return carry

    lax.fori_loop(0, count // group, last, 0)


def atmos_step(a, top, bottom, left, right, w1, b1, w2, b2, lat_count):
    count, channels, cols = a.shape
    vmem = pl.BlockSpec(memory_space=pltpu.VMEM)
    return pl.pallas_call(
        functools.partial(atmos_kernel, lat_count),
        out_shape=jax.ShapeDtypeStruct(a.shape, BF16),
        in_specs=[vmem] * 9,
        out_specs=vmem,
        scratch_shapes=[
            pltpu.VMEM((count + 4, channels, 2 * cols), BF16),
            pltpu.VMEM((count + 2, channels, 2 * cols), BF16),
        ],
        compiler_params=pltpu.CompilerParams(vmem_limit_bytes=VMEM_LIMIT),
        name="atmos",
    )(a, top, bottom, left, right, w1, b1, w2, b2)


def per_device(
    ocean_state,
    sea_mask,
    ocean_w1,
    ocean_b1,
    ocean_w2,
    ocean_b2,
    regrid_weight,
    route_dev,
    route_row,
    atmos_state,
    atmos_w1,
    atmos_b1,
    atmos_w2,
    atmos_b2,
):
    lat_count, lon_count = lax.axis_size("lat"), lax.axis_size("lon")
    lat = lax.axis_index("lat")
    atmos_rows = atmos_state.shape[1]

    field = jnp.concatenate(
        [
            ocean_state,
            sea_mask.astype(BF16)[None],
            jnp.zeros((3,) + sea_mask.shape, BF16),
        ],
        axis=0,
    ).transpose(1, 0, 2)
    key = ((route_dev - (lat - 1) * lon_count) * atmos_rows + route_row).reshape(-1)
    count = key.shape[0]
    order = jnp.arange(count, dtype=jnp.int32)
    place = jnp.sum((key[None, :] < key[:, None]).astype(jnp.int32), axis=1)
    again = (key[None, :] == key[:, None]) & (order[None, :] < order[:, None])
    meta = place * 2 + 1 - jnp.max(again.astype(jnp.int32), axis=1)
    per_step = lon_count * atmos_rows
    lanes = jnp.arange(8 * 128, dtype=jnp.int32)
    number = jnp.where(lanes < per_step, lanes, -4 * per_step).reshape(1, 8, 128)
    number = number + jnp.arange(3, dtype=jnp.int32)[:, None, None] * per_step
    index = jnp.min(
        jnp.where(number[..., None] == key[None, None, None, :], place[None, None, None, :], count),
        axis=3,
    )
    top, bottom, left, right, north_index, south_index = ocean_halo(
        field, index, lat_count, lon_count
    )
    ocean_next, slots = ocean_step(
        meta,
        field,
        top,
        bottom,
        left,
        right,
        stacked_weight(ocean_w1, 80),
        ocean_b1[None, :],
        stacked_weight(ocean_w2, 64),
        ocean_b2[None, :],
        regrid_weight.reshape(-1, 256, 128),
        lat_count,
    )
    first, top, bottom, left, right = couple(
        index,
        north_index,
        south_index,
        slots,
        atmos_state.transpose(1, 0, 2),
        count,
        1,
        lat_count,
        lon_count,
    )
    atmos_next = atmos_step(
        first,
        top,
        bottom,
        left,
        right,
        stacked_weight(atmos_w1, 64),
        atmos_b1[None, :],
        stacked_weight(atmos_w2, 64),
        atmos_b2[None, :],
        lat_count,
    )
    return ocean_next.transpose(1, 0, 2), atmos_next.transpose(1, 0, 2)


def solution(mesh):
    in_specs = (
        P(None, "lat", "lon"),
        P("lat", "lon"),
        P(),
        P(),
        P(),
        P(),
        P(("lat", "lon"), None, None, None),
        P(("lat", "lon"), None),
        P(("lat", "lon"), None),
        P(None, "lat", "lon"),
        P(),
        P(),
        P(),
        P(),
    )
    out_specs = (P(None, "lat", "lon"), P(None, "lat", "lon"))
    return jax.shard_map(
        per_device, mesh=mesh, in_specs=in_specs, out_specs=out_specs, check_vma=False
    )
```

```python
import functools

import jax
import jax.numpy as jnp
from jax import lax
from jax.experimental import pallas as pl
from jax.experimental.pallas import tpu as pltpu
from jax.sharding import PartitionSpec as P

MESH = pl.DeviceIdType.MESH
F32 = jnp.float32
BF16 = jnp.bfloat16
VMEM_LIMIT = 56 * 1024 * 1024
GROUPS = 4
FIRST_ROWS = 11
LAST_ROWS = 16
LENGTHS = (32, 48, 64)


def silu(v):
    return 0.5 * v * (1.0 + jnp.tanh(0.5 * v))


def shifted_sum(taps):
    out = taps.shape[0] // 3
    columns = taps.shape[1]
    return (
        pltpu.roll(taps[0:out], 1, 1)
        + taps[out : 2 * out]
        + pltpu.roll(taps[2 * out :], columns - 1, 1)
    )


def stacked_weight(weight, padded_in):
    out, inn = weight.shape[:2]
    weight = jnp.pad(weight, ((0, 0), (0, padded_in - inn), (0, 0), (0, 0)))
    return weight.transpose(3, 0, 2, 1).reshape(3 * out, 3 * padded_in)


def column(bias):
    n = bias.shape[1]
    at = lax.broadcasted_iota(jnp.int32, (n, n), 0) == lax.broadcasted_iota(jnp.int32, (n, n), 1)
    return jnp.sum(jnp.where(at, bias, 0.0), axis=1, keepdims=True)


def remote(src, dst, send_sem, recv_sem, lat, lon):
    return pltpu.make_async_remote_copy(
        src_ref=src,
        dst_ref=dst,
        send_sem=send_sem,
        recv_sem=recv_sem,
        device_id={"lat": lat, "lon": lon},
        device_id_type=MESH,
    )


def landed(ref, sem):
    return pltpu.make_async_copy(ref, ref, sem)


def greet(partners, waits):
    barrier = pltpu.get_barrier_semaphore()
    for lat, lon, ok in partners:

        @pl.when(ok)
        def _():
            pl.semaphore_signal(
                barrier, inc=1, device_id={"lat": lat, "lon": lon}, device_id_type=MESH
            )

    pl.semaphore_wait(barrier, waits)


def whole_any(count):
    return [pl.BlockSpec(memory_space=pl.ANY)] * count


def ocean_halo_kernel(
    lat_count,
    lon_count,
    field,
    index,
    top,
    bottom,
    left,
    right,
    north_index,
    south_index,
    send_sem,
    recv_sem,
):
    lat, lon = lax.axis_index("lat"), lax.axis_index("lon")
    rows, _, cols = field.shape
    west = lax.rem(lon + lon_count - 1, lon_count)
    east = lax.rem(lon + 1, lon_count)
    up, down, always = lat > 0, lat < lat_count - 1, lat >= 0
    edge = jnp.logical_or(lat == 0, lat == lat_count - 1)
    partners = [(lat, west, always), (lat, east, always)]
    for there, ok in ((lat - 1, up), (lat + 1, down)):
        partners += [(there, side, ok) for side in (west, lon, east)]
    greet(partners, jnp.where(edge, 5, 8))

    lo, hi = pl.ds(0, 128), pl.ds(cols - 128, 128)
    first, last = pl.ds(0, 2), pl.ds(rows - 2, 2)
    own, above, below = pl.ds(2, rows), pl.ds(0, 2), pl.ds(rows + 2, 2)
    moves = [
        (field.at[:, :, lo], right.at[own], lat, west, always),
        (field.at[:, :, hi], left.at[own], lat, east, always),
        (field.at[first], bottom, lat - 1, lon, up),
        (field.at[last], top, lat + 1, lon, down),
        (field.at[first, :, lo], right.at[below], lat - 1, west, up),
        (field.at[first, :, hi], left.at[below], lat - 1, east, up),
        (field.at[last, :, lo], right.at[above], lat + 1, west, down),
        (field.at[last, :, hi], left.at[above], lat + 1, east, down),
        (index.at[0], south_index, lat - 1, lon, up),
        (index.at[2], north_index, lat + 1, lon, down),
    ]
    arrives = [always, always, down, up, down, down, up, up, down, up]
    copies = [
        (remote(src, dst, send_sem.at[i], recv_sem.at[i], a, b), ok)
        for i, (src, dst, a, b, ok) in enumerate(moves)
    ]
    for copy, ok in copies:
        pl.when(ok)(copy.start)
    for i, (copy, ok) in enumerate(copies):
        pl.when(ok)(copy.wait_send)
        pl.when(arrives[i])(landed(moves[i][1], recv_sem.at[i]).wait)


def ocean_halo(field, index, lat_count, lon_count):
    rows, channels, cols = field.shape
    shapes = [(2, channels, cols)] * 2 + [(rows + 4, channels, 128)] * 2
    table = jax.ShapeDtypeStruct(index.shape[1:], jnp.int32)
    return pl.pallas_call(
        functools.partial(ocean_halo_kernel, lat_count, lon_count),
        out_shape=[jax.ShapeDtypeStruct(s, BF16) for s in shapes] + [table] * 2,
        in_specs=whole_any(2),
        out_specs=whole_any(6),
        scratch_shapes=[pltpu.SemaphoreType.DMA((10,))] * 2,
        compiler_params=pltpu.CompilerParams(collective_id=0, has_side_effects=True),
        name="ocean_halo",
    )(field, index)


def ocean_kernel(
    lat_count,
    meta,
    x_ref,
    top_ref,
    bottom_ref,
    left_ref,
    right_ref,
    w1_ref,
    b1_ref,
    w2_ref,
    b2_ref,
    regrid_ref,
    next_ref,
    slots_ref,
    tall,
    hidden,
    sums,
):
    row = lax.rem(pl.program_id(0), 16)
    rows, channels, cols = x_ref.shape
    mask_at = 76
    b1, b2 = column(b1_ref[...]), column(b2_ref[...])

    def first_conv(j):
        field = jnp.concatenate([tall[j], tall[j + 1], tall[j + 2]], axis=0)
        taps = jnp.dot(w1_ref[...], field, preferred_element_type=F32)
        mask = tall[j + 1, mask_at : mask_at + 1, :].astype(F32)
        hidden[j] = (silu(shifted_sum(taps) + b1) * mask).astype(BF16)

    @pl.when(row == 0)
    def _():
        lat = lax.axis_index("lat")
        lane = lax.broadcasted_iota(jnp.int32, (channels, 128), 1)
        tall[2 : 2 + rows, :, 0:cols] = x_ref[...]
        for j in range(rows + 4):
            side = jnp.where(lane < 64, right_ref[j], left_ref[j])
            if j < 2 or j >= rows + 2:
                inside = lat > 0 if j < 2 else lat < lat_count - 1
                main = top_ref[j] if j < 2 else bottom_ref[j - rows - 2]
                tall[j, :, 0:cols] = jnp.where(inside, main, jnp.zeros_like(main))
                side = jnp.where(inside, side, jnp.zeros_like(side))
            tall[j, :, cols:] = side
        first_conv(0)
        first_conv(1)

    first_conv(lax.rem(row + 2, 16))
    field = jnp.concatenate([hidden[row], hidden[row + 1], hidden[row + 2]], axis=0)
    taps = jnp.dot(w2_ref[...], field, preferred_element_type=F32)
    mask = tall[row + 2, mask_at : mask_at + 1, :].astype(F32)
    result = ((shifted_sum(taps) + b2) * mask).astype(BF16)[:, :cols]
    next_ref[0] = result
    blocks = regrid_ref.shape[0]
    for q in range(blocks):
        field = result[:, q * 128 : (q + 1) * 128]
        both = lax.dot_general(
            field, regrid_ref[q], (((1,), (1,)), ((), ())), preferred_element_type=F32
        ).astype(BF16)
        for k in range(2):
            what = meta[(row * blocks + q) * 2 + k]
            at = what // 2
            value = both[:, k * 128 : (k + 1) * 128].astype(F32)
            sums[at] = jnp.where(lax.rem(what, 2) == 1, value, sums[at] + value)

    @pl.when(row == rows - 1)
    def _():
        groups, slots, size = slots_ref.shape[:3]

        def rounded(i, carry):
            for g in range(groups):
                slots_ref[g, i] = sums[i, g * size : (g + 1) * size].astype(BF16)
            return carry

        lax.fori_loop(0, slots, rounded, 0)


def ocean_step(meta, x, top, bottom, left, right, w1, b1, w2, b2, regrid, lat_count):
    rows, channels, cols = x.shape
    wide = cols + 128
    out = w2.shape[0] // 3
    slots = meta.shape[0]

    def whole(array):
        zeros = (0,) * array.ndim
        return pl.BlockSpec(array.shape, lambda r, meta: zeros)

    blocks = regrid.shape[0] // rows
    return pl.pallas_call(
        functools.partial(ocean_kernel, lat_count),
        out_shape=(
            jax.ShapeDtypeStruct((rows, out, cols), BF16),
            jax.ShapeDtypeStruct((GROUPS, slots, out // GROUPS, 128), BF16),
        ),
        grid_spec=pltpu.PrefetchScalarGridSpec(
            num_scalar_prefetch=1,
            grid=(rows,),
            in_specs=[whole(a) for a in (x, top, bottom, left, right, w1, b1, w2, b2)]
            + [pl.BlockSpec((blocks, 256, 128), lambda r, meta: (r, 0, 0))],
            out_specs=[
                pl.BlockSpec((1, out, cols), lambda r, meta: (r, 0, 0)),
                pl.BlockSpec((GROUPS, slots, out // GROUPS, 128), lambda r, meta: (0, 0, 0, 0)),
            ],
            scratch_shapes=[
                pltpu.VMEM((rows + 4, channels, wide), BF16),
                pltpu.VMEM((rows + 2, out, wide), BF16),
                pltpu.VMEM((slots, out, 128), F32),
            ],
        ),
        compiler_params=pltpu.CompilerParams(vmem_limit_bytes=VMEM_LIMIT),
        name="ocean",
    )(meta, x, top, bottom, left, right, w1, b1, w2, b2, regrid)


def couple_kernel(
    lat_count,
    lon_count,
    count,
    own_index,
    north_index,
    south_index,
    slots,
    atmos,
    first,
    top,
    bottom,
    left,
    right,
    *scratch,
):
    lat, lon = lax.axis_index("lat"), lax.axis_index("lon")
    west = lax.rem(lon + lon_count - 1, lon_count)
    east = lax.rem(lon + 1, lon_count)
    across = lax.rem(lon + 2, lon_count)
    beside = lon + 1 - 2 * lax.rem(lon, 2)
    beside_across = lax.rem(beside + 2, lon_count)
    up, down, always = lat > 0, lat < lat_count - 1, lat >= 0
    edge = jnp.logical_or(lat == 0, lat == lat_count - 1)
    partners = [(lat, there, always) for there in (west, east, across)]
    for there, ok in ((lat - 1, up), (lat + 1, down)):
        partners += [(there, side, ok) for side in (west, lon, east)]
    greet(partners, jnp.where(edge, 6, 9))

    groups, total, size, cols = slots.shape
    rows, channels = first.shape[:2]
    own, north, south = (scratch[i * groups : (i + 1) * groups] for i in range(3))
    away, mine, from_core, to_z, from_z, edges = scratch[3 * groups : 3 * groups + 6]
    load_sem, y_send, y_recv, core_send, core_recv, z_send, z_recv, halo_send, halo_recv = scratch[
        3 * groups + 6 :
    ]
    low, high = pl.ds(0, count), pl.ds(total - count, count)
    everything = pl.ds(0, total)
    to_south, to_north, loads = [], [], []
    for g in range(groups):
        to_south.append(
            remote(
                slots.at[g, high], north[g].at[high], y_send.at[0, g], y_recv.at[0, g], lat + 1, lon
            )
        )
        to_north.append(
            remote(
                slots.at[g, low], south[g].at[low], y_send.at[1, g], y_recv.at[1, g], lat - 1, lon
            )
        )
        loads.append(
            pltpu.make_async_copy(slots.at[g], own[g].at[everything], load_sem.at[g])
        )
        pl.when(down)(to_south[g].start)
        pl.when(up)(to_north[g].start)
        loads[g].start()
    for buffer in (own, north, south):
        for g in range(groups):
            buffer[g][total] = jnp.zeros((size, cols), BF16)

    def dense(g, lon_there, store):
        def row(t, carry):
            at = lon_there * rows + t
            i, j = at // 128, lax.rem(at, 128)
            a = own_index[1, i, j]
            b = jnp.where(up, north_index[i, j], total)
            c = jnp.where(down, south_index[i, j], total)
            value = own[g][a].astype(F32) + north[g][b].astype(F32) + south[g][c].astype(F32)
            store(t, value.astype(BF16))
            return carry

        lax.fori_loop(0, rows, row, 0, unroll=8)

    core_copies, z_copies = [], []
    for g in range(groups):
        loads[g].wait()
        pl.when(up)(landed(north[g].at[high], y_recv.at[0, g]).wait)
        pl.when(down)(landed(south[g].at[low], y_recv.at[1, g]).wait)
        for part, (theirs, ours) in enumerate(((beside_across, across), (beside, lon))):

            def put_away(t, value):
                away[part, g, t] = value

            def put_mine(t, value):
                mine[part, g, t] = value

            dense(g, theirs, put_away)
            copy = remote(
                away.at[part, g],
                from_core.at[part, g],
                core_send.at[part, g],
                core_recv.at[part, g],
                lat,
                beside,
            )
            copy.start()
            core_copies.append(copy)
            dense(g, ours, put_mine)
            if part == 0:
                landed(from_core.at[0, g], core_recv.at[0, g]).wait()
                to_z[g] = (mine[0, g].astype(F32) + from_core[0, g].astype(F32)).astype(BF16)
                copy = remote(
                    to_z.at[g], from_z.at[g], z_send.at[g], z_recv.at[g], lat, across
                )
                copy.start()
                z_copies.append(copy)

    lane = lax.broadcasted_iota(jnp.int32, (size, cols), 1)
    tiles = edges.shape[0]
    for g in range(groups):
        landed(from_core.at[1, g], core_recv.at[1, g]).wait()
        landed(from_z.at[g], z_recv.at[g]).wait()
        part = pl.ds(g * size, size)
        for tile in range(tiles):
            edge = jnp.zeros((size, cols), F32)
            for k in range(32):
                r = tile * 32 + k
                flux = (
                    mine[1, g, r].astype(F32)
                    + from_core[1, g, r].astype(F32)
                    + from_z[g, r].astype(F32)
                )
                v = (atmos[r, part].astype(F32) + flux).astype(BF16)
                first[r, part] = v
                rolled = pltpu.roll(v.astype(F32), (4 * k + 2) % cols, 1)
                edge = jnp.where(lane // 4 == k, rolled, edge)
            edges[tile, part] = edge.astype(BF16)
    lo, hi = edges.at[0], edges.at[tiles - 1]
    moves = [
        (edges, right.at[pl.ds(1, tiles)], lat, west, always, always),
        (edges, left.at[pl.ds(1, tiles)], lat, east, always, always),
        (first.at[pl.ds(0, 2)], bottom, lat - 1, lon, up, down),
        (first.at[pl.ds(rows - 2, 2)], top, lat + 1, lon, down, up),
        (lo, right.at[tiles + 1], lat - 1, west, up, down),
        (lo, left.at[tiles + 1], lat - 1, east, up, down),
        (hi, right.at[0], lat + 1, west, down, up),
        (hi, left.at[0], lat + 1, east, down, up),
    ]
    copies = [
        remote(src, dst, halo_send.at[i], halo_recv.at[i], a, b)
        for i, (src, dst, a, b, _, _) in enumerate(moves)
    ]
    for copy, move in zip(copies, moves):
        pl.when(move[4])(copy.start)
    for copy in core_copies + z_copies:
        copy.wait_send()
    for g in range(groups):
        pl.when(down)(to_south[g].wait_send)
        pl.when(up)(to_north[g].wait_send)
    for i, (copy, move) in enumerate(zip(copies, moves)):
        pl.when(move[4])(copy.wait_send)
        pl.when(move[5])(landed(move[1], halo_recv.at[i]).wait)


def couple(index, north_index, south_index, slots, atmos, count, collective_id, lat_count, lon_count):
    groups, total, size, cols = slots.shape
    rows, channels, cols = atmos.shape
    tiles = rows // 32
    vmem = pl.BlockSpec(memory_space=pltpu.VMEM)
    smem = pl.BlockSpec(memory_space=pltpu.SMEM)
    dma = pltpu.SemaphoreType.DMA
    shapes = [(rows, channels, cols)] + [(2, channels, cols)] * 2 + [(tiles + 2, channels, cols)] * 2
    received = pltpu.VMEM((total + 1, size, cols), BF16)
    one = pltpu.VMEM((groups, rows, size, cols), BF16)
    two = pltpu.VMEM((2, groups, rows, size, cols), BF16)
    return pl.pallas_call(
        functools.partial(couple_kernel, lat_count, lon_count, count),
        out_shape=[jax.ShapeDtypeStruct(s, BF16) for s in shapes],
        in_specs=[smem] * 3 + whole_any(1) + [vmem],
        out_specs=[vmem] + whole_any(4),
        scratch_shapes=[received] * (3 * groups)
        + [two] * 3
        + [one] * 2
        + [pltpu.VMEM((tiles, channels, cols), BF16)]
        + [dma((groups,))]
        + [dma((2, groups))] * 4
        + [dma((groups,))] * 2
        + [dma((8,))] * 2,
        compiler_params=pltpu.CompilerParams(
            collective_id=collective_id, has_side_effects=True, vmem_limit_bytes=VMEM_LIMIT
        ),
        name="couple",
    )(index, north_index, south_index, slots, atmos)


def atmos_kernel(
    lat_count, a_ref, top_ref, bottom_ref, left_ref, right_ref, w1_ref, b1_ref, w2_ref, b2_ref, out_ref, tall, second
):
    count, channels, cols = a_ref.shape
    lat = lax.axis_index("lat")
    b1, b2 = column(b1_ref[...]), column(b2_ref[...])

    tall[2 : 2 + count, :, 0:cols] = a_ref[...]
    lane = lax.broadcasted_iota(jnp.int32, (channels, cols), 1)
    for tile in range(count // 32 + 2):
        side = jnp.where(lane % 4 < 2, left_ref[tile], right_ref[tile]).astype(F32)
        for k in range(32):
            r = tile * 32 - 32 + k
            if r < -2 or r >= count + 2:
                continue
            v = pltpu.roll(side, (126 - 4 * k) % cols, 1).astype(BF16)
            if r < 0 or r >= count:
                inside = lat > 0 if r < 0 else lat < lat_count - 1
                main = top_ref[r + 2] if r < 0 else bottom_ref[r - count]
                tall[r + 2, :, 0:cols] = jnp.where(inside, main, jnp.zeros_like(main))
                v = jnp.where(inside, v, jnp.zeros_like(v))
            tall[r + 2, :, cols:] = v

    def conv(source, weight, start, group):
        fields = [
            jnp.concatenate([source[start + i + d] for d in range(3)], axis=0)
            for i in range(group)
        ]
        return jnp.dot(weight, jnp.concatenate(fields, axis=1), preferred_element_type=F32)

    def first(step, carry):
        group = FIRST_ROWS
        start = step * group
        taps = conv(tall, w1_ref[...], start, group)
        for i in range(group):
            j = start + i
            value = silu(shifted_sum(taps[:, i * 2 * cols : (i + 1) * 2 * cols]) + b1)
            outside = jnp.logical_or(
                jnp.logical_and(j == 0, lat == 0),
                jnp.logical_and(j == count + 1, lat == lat_count - 1),
            )
            second[j] = jnp.where(outside, 0.0, value).astype(BF16)
        return carry

    lax.fori_loop(0, (count + 2) // FIRST_ROWS, first, 0)

    def last(step, carry):
        group = LAST_ROWS
        start = step * group
        taps = conv(second, w2_ref[...], start, group)
        for i in range(group):
            j = start + i
            value = shifted_sum(taps[:, i * 2 * cols : (i + 1) * 2 * cols])[:, :cols]
            out_ref[j] = (a_ref[j].astype(F32) + (value + b2)).astype(BF16)
        return carry

    lax.fori_loop(0, count // LAST_ROWS, last, 0)


def atmos_step(a, top, bottom, left, right, w1, b1, w2, b2, lat_count):
    count, channels, cols = a.shape
    vmem = pl.BlockSpec(memory_space=pltpu.VMEM)
    return pl.pallas_call(
        functools.partial(atmos_kernel, lat_count),
        out_shape=jax.ShapeDtypeStruct(a.shape, BF16),
        in_specs=[vmem] * 9,
        out_specs=vmem,
        scratch_shapes=[
            pltpu.VMEM((count + 4, channels, 2 * cols), BF16),
            pltpu.VMEM((count + 2, channels, 2 * cols), BF16),
        ],
        compiler_params=pltpu.CompilerParams(vmem_limit_bytes=VMEM_LIMIT),
        name="atmos",
    )(a, top, bottom, left, right, w1, b1, w2, b2)


def per_device(
    ocean_state,
    sea_mask,
    ocean_w1,
    ocean_b1,
    ocean_w2,
    ocean_b2,
    regrid_weight,
    route_dev,
    route_row,
    atmos_state,
    atmos_w1,
    atmos_b1,
    atmos_w2,
    atmos_b2,
):
    lat_count, lon_count = lax.axis_size("lat"), lax.axis_size("lon")
    lat = lax.axis_index("lat")
    atmos_rows = atmos_state.shape[1]

    field = jnp.concatenate(
        [
            ocean_state,
            sea_mask.astype(BF16)[None],
            jnp.zeros((3,) + sea_mask.shape, BF16),
        ],
        axis=0,
    ).transpose(1, 0, 2)
    key = ((route_dev - (lat - 1) * lon_count) * atmos_rows + route_row).reshape(-1)
    count = key.shape[0]
    order = jnp.arange(count, dtype=jnp.int32)
    place = jnp.sum((key[None, :] < key[:, None]).astype(jnp.int32), axis=1)
    again = (key[None, :] == key[:, None]) & (order[None, :] < order[:, None])
    meta = place * 2 + 1 - jnp.max(again.astype(jnp.int32), axis=1)
    per_step = lon_count * atmos_rows
    longest = jnp.maximum(
        jnp.sum((key < per_step).astype(jnp.int32)), jnp.sum((key >= 2 * per_step).astype(jnp.int32))
    )
    longest = lax.pmax(longest, ("lat", "lon"))
    which = sum((longest > n).astype(jnp.int32) for n in LENGTHS if n < count)
    lanes = jnp.arange(8 * 128, dtype=jnp.int32)
    number = jnp.where(lanes < per_step, lanes, -4 * per_step).reshape(1, 8, 128)
    number = number + jnp.arange(3, dtype=jnp.int32)[:, None, None] * per_step
    index = jnp.min(
        jnp.where(number[..., None] == key[None, None, None, :], place[None, None, None, :], count),
        axis=3,
    )
    top, bottom, left, right, north_index, south_index = ocean_halo(
        field, index, lat_count, lon_count
    )
    ocean_next, slots = ocean_step(
        meta,
        field,
        top,
        bottom,
        left,
        right,
        stacked_weight(ocean_w1, 80),
        ocean_b1[None, :],
        stacked_weight(ocean_w2, 64),
        ocean_b2[None, :],
        regrid_weight.reshape(-1, 256, 128),
        lat_count,
    )
    lengths = [n for n in LENGTHS if n < count] + [count]

    def coupled(at):
        def branch(*operands):
            return tuple(couple(*operands, lengths[at], 1 + at, lat_count, lon_count))

        return branch

    first, top, bottom, left, right = lax.switch(
        which,
        [coupled(at) for at in range(len(lengths))],
        index,
        north_index,
        south_index,
        slots,
        atmos_state.transpose(1, 0, 2),
    )
    atmos_next = atmos_step(
        first,
        top,
        bottom,
        left,
        right,
        stacked_weight(atmos_w1, 64),
        atmos_b1[None, :],
        stacked_weight(atmos_w2, 64),
        atmos_b2[None, :],
        lat_count,
    )
    return ocean_next.transpose(1, 0, 2), atmos_next.transpose(1, 0, 2)


def solution(mesh):
    in_specs = (
        P(None, "lat", "lon"),
        P("lat", "lon"),
        P(),
        P(),
        P(),
        P(),
        P(("lat", "lon"), None, None, None),
        P(("lat", "lon"), None),
        P(("lat", "lon"), None),
        P(None, "lat", "lon"),
        P(),
        P(),
        P(),
        P(),
    )
    out_specs = (P(None, "lat", "lon"), P(None, "lat", "lon"))
    return jax.shard_map(
        per_device, mesh=mesh, in_specs=in_specs, out_specs=out_specs, check_vma=False
    )
```

```python
import functools

import jax
import jax.numpy as jnp
from jax import lax
from jax.experimental import pallas as pl
from jax.experimental.pallas import tpu as pltpu
from jax.sharding import PartitionSpec as P

MESH = pl.DeviceIdType.MESH
F32 = jnp.float32
BF16 = jnp.bfloat16
VMEM_LIMIT = 56 * 1024 * 1024
GROUPS = 4
FIRST_ROWS = 11
LAST_ROWS = 16
LENGTHS = (32, 48, 64)


def silu(v):
    return 0.5 * v * (1.0 + jnp.tanh(0.5 * v))


def shifted_sum(taps):
    out = taps.shape[0] // 3
    columns = taps.shape[1]
    return (
        pltpu.roll(taps[0:out], 1, 1)
        + taps[out : 2 * out]
        + pltpu.roll(taps[2 * out :], columns - 1, 1)
    )


def stacked_weight(weight, padded_in):
    out, inn = weight.shape[:2]
    weight = jnp.pad(weight, ((0, 0), (0, padded_in - inn), (0, 0), (0, 0)))
    return weight.transpose(3, 0, 2, 1).reshape(3 * out, 3 * padded_in)


def column(bias):
    n = bias.shape[1]
    at = lax.broadcasted_iota(jnp.int32, (n, n), 0) == lax.broadcasted_iota(jnp.int32, (n, n), 1)
    return jnp.sum(jnp.where(at, bias, 0.0), axis=1, keepdims=True)


def remote(src, dst, send_sem, recv_sem, lat, lon):
    return pltpu.make_async_remote_copy(
        src_ref=src,
        dst_ref=dst,
        send_sem=send_sem,
        recv_sem=recv_sem,
        device_id={"lat": lat, "lon": lon},
        device_id_type=MESH,
    )


def landed(ref, sem):
    return pltpu.make_async_copy(ref, ref, sem)


def greet(partners, waits):
    barrier = pltpu.get_barrier_semaphore()
    for lat, lon, ok in partners:

        @pl.when(ok)
        def _():
            pl.semaphore_signal(
                barrier, inc=1, device_id={"lat": lat, "lon": lon}, device_id_type=MESH
            )

    pl.semaphore_wait(barrier, waits)


def whole_any(count):
    return [pl.BlockSpec(memory_space=pl.ANY)] * count


def ocean_halo_kernel(
    lat_count,
    lon_count,
    field,
    index,
    longest,
    top,
    bottom,
    left,
    right,
    north_index,
    south_index,
    longest_of_all,
    gathered,
    partial,
    send_sem,
    recv_sem,
    max_send,
    max_recv,
):
    lat, lon = lax.axis_index("lat"), lax.axis_index("lon")
    rows, _, cols = field.shape
    west = lax.rem(lon + lon_count - 1, lon_count)
    east = lax.rem(lon + 1, lon_count)
    up, down, always = lat > 0, lat < lat_count - 1, lat >= 0
    edge = jnp.logical_or(lat == 0, lat == lat_count - 1)
    partners = [(lat, west, always), (lat, east, always)]
    for there, ok in ((lat - 1, up), (lat + 1, down)):
        partners += [(there, side, ok) for side in (west, lon, east)]
    four, inner = lat // 4, lax.rem(lat, 4)
    fours = lat_count // 4
    rounds = [
        [(lat, lax.rem(lon + k, lon_count)) for k in range(1, lon_count)],
        [(four * 4 + lax.rem(inner + k, 4), lon) for k in range(1, 4)],
        [(lax.rem(four + k, fours) * 4 + inner, lon) for k in range(1, fours)],
    ]
    partners += [(a, b, always) for peers in rounds for a, b in peers]
    greet(partners, jnp.where(edge, 5, 8) + sum(len(peers) for peers in rounds))

    lo, hi = pl.ds(0, 128), pl.ds(cols - 128, 128)
    first, last = pl.ds(0, 2), pl.ds(rows - 2, 2)
    own, above, below = pl.ds(2, rows), pl.ds(0, 2), pl.ds(rows + 2, 2)
    moves = [
        (field.at[:, :, lo], right.at[own], lat, west, always),
        (field.at[:, :, hi], left.at[own], lat, east, always),
        (field.at[first], bottom, lat - 1, lon, up),
        (field.at[last], top, lat + 1, lon, down),
        (field.at[first, :, lo], right.at[below], lat - 1, west, up),
        (field.at[first, :, hi], left.at[below], lat - 1, east, up),
        (field.at[last, :, lo], right.at[above], lat + 1, west, down),
        (field.at[last, :, hi], left.at[above], lat + 1, east, down),
        (index.at[0], south_index, lat - 1, lon, up),
        (index.at[2], north_index, lat + 1, lon, down),
    ]
    arrives = [always, always, down, up, down, down, up, up, down, up]
    copies = [
        (remote(src, dst, send_sem.at[i], recv_sem.at[i], a, b), ok)
        for i, (src, dst, a, b, ok) in enumerate(moves)
    ]
    for copy, ok in copies:
        pl.when(ok)(copy.start)
    held, at, small = longest, 0, []
    for number, peers in enumerate(rounds):
        slots = range(at, at + len(peers))
        for i, (a, b) in zip(slots, peers):
            small.append(remote(held, gathered.at[i], max_send.at[i], max_recv.at[i], a, b))
            small[-1].start()
        value = held[...]
        for i in slots:
            landed(gathered.at[i], max_recv.at[i]).wait()
            value = jnp.maximum(value, gathered[i])
        held = longest_of_all if number == 2 else partial.at[number]
        held[...] = value
        at += len(peers)
    for copy in small:
        copy.wait_send()
    for i, (copy, ok) in enumerate(copies):
        pl.when(ok)(copy.wait_send)
        pl.when(arrives[i])(landed(moves[i][1], recv_sem.at[i]).wait)


def ocean_halo(field, index, longest, lat_count, lon_count):
    rows, channels, cols = field.shape
    shapes = [(2, channels, cols)] * 2 + [(rows + 4, channels, 128)] * 2
    table = jax.ShapeDtypeStruct(index.shape[1:], jnp.int32)
    vmem = pl.BlockSpec(memory_space=pltpu.VMEM)
    peers = lon_count - 1 + 3 + lat_count // 4 - 1
    return pl.pallas_call(
        functools.partial(ocean_halo_kernel, lat_count, lon_count),
        out_shape=[jax.ShapeDtypeStruct(s, BF16) for s in shapes] + [table] * 3,
        in_specs=whole_any(2) + [vmem],
        out_specs=whole_any(6) + [vmem],
        scratch_shapes=[
            pltpu.VMEM((peers, 8, 128), jnp.int32),
            pltpu.VMEM((2, 8, 128), jnp.int32),
            pltpu.SemaphoreType.DMA((10,)),
            pltpu.SemaphoreType.DMA((10,)),
            pltpu.SemaphoreType.DMA((peers,)),
            pltpu.SemaphoreType.DMA((peers,)),
        ],
        compiler_params=pltpu.CompilerParams(collective_id=0, has_side_effects=True),
        name="ocean_halo",
    )(field, index, longest)


def ocean_kernel(
    lat_count,
    meta,
    x_ref,
    top_ref,
    bottom_ref,
    left_ref,
    right_ref,
    w1_ref,
    b1_ref,
    w2_ref,
    b2_ref,
    regrid_ref,
    next_ref,
    slots_ref,
    tall,
    hidden,
    sums,
):
    row = lax.rem(pl.program_id(0), 16)
    rows, channels, cols = x_ref.shape
    mask_at = 76
    b1, b2 = column(b1_ref[...]), column(b2_ref[...])

    def first_conv(j):
        field = jnp.concatenate([tall[j], tall[j + 1], tall[j + 2]], axis=0)
        taps = jnp.dot(w1_ref[...], field, preferred_element_type=F32)
        mask = tall[j + 1, mask_at : mask_at + 1, :].astype(F32)
        hidden[j] = (silu(shifted_sum(taps) + b1) * mask).astype(BF16)

    @pl.when(row == 0)
    def _():
        lat = lax.axis_index("lat")
        lane = lax.broadcasted_iota(jnp.int32, (channels, 128), 1)
        tall[2 : 2 + rows, :, 0:cols] = x_ref[...]
        for j in range(rows + 4):
            side = jnp.where(lane < 64, right_ref[j], left_ref[j])
            if j < 2 or j >= rows + 2:
                inside = lat > 0 if j < 2 else lat < lat_count - 1
                main = top_ref[j] if j < 2 else bottom_ref[j - rows - 2]
                tall[j, :, 0:cols] = jnp.where(inside, main, jnp.zeros_like(main))
                side = jnp.where(inside, side, jnp.zeros_like(side))
            tall[j, :, cols:] = side
        first_conv(0)
        first_conv(1)

    first_conv(lax.rem(row + 2, 16))
    field = jnp.concatenate([hidden[row], hidden[row + 1], hidden[row + 2]], axis=0)
    taps = jnp.dot(w2_ref[...], field, preferred_element_type=F32)
    mask = tall[row + 2, mask_at : mask_at + 1, :].astype(F32)
    result = ((shifted_sum(taps) + b2) * mask).astype(BF16)[:, :cols]
    next_ref[0] = result
    blocks = regrid_ref.shape[0]
    for q in range(blocks):
        field = result[:, q * 128 : (q + 1) * 128]
        both = lax.dot_general(
            field, regrid_ref[q], (((1,), (1,)), ((), ())), preferred_element_type=F32
        ).astype(BF16)
        for k in range(2):
            what = meta[(row * blocks + q) * 2 + k]
            at = what // 2
            value = both[:, k * 128 : (k + 1) * 128].astype(F32)
            sums[at] = jnp.where(lax.rem(what, 2) == 1, value, sums[at] + value)

    @pl.when(row == rows - 1)
    def _():
        groups, slots, size = slots_ref.shape[:3]

        def rounded(i, carry):
            for g in range(groups):
                slots_ref[g, i] = sums[i, g * size : (g + 1) * size].astype(BF16)
            return carry

        lax.fori_loop(0, slots, rounded, 0)


def ocean_step(meta, x, top, bottom, left, right, w1, b1, w2, b2, regrid, lat_count):
    rows, channels, cols = x.shape
    wide = cols + 128
    out = w2.shape[0] // 3
    slots = meta.shape[0]

    def whole(array):
        zeros = (0,) * array.ndim
        return pl.BlockSpec(array.shape, lambda r, meta: zeros)

    blocks = regrid.shape[0] // rows
    return pl.pallas_call(
        functools.partial(ocean_kernel, lat_count),
        out_shape=(
            jax.ShapeDtypeStruct((rows, out, cols), BF16),
            jax.ShapeDtypeStruct((GROUPS, slots, out // GROUPS, 128), BF16),
        ),
        grid_spec=pltpu.PrefetchScalarGridSpec(
            num_scalar_prefetch=1,
            grid=(rows,),
            in_specs=[whole(a) for a in (x, top, bottom, left, right, w1, b1, w2, b2)]
            + [pl.BlockSpec((blocks, 256, 128), lambda r, meta: (r, 0, 0))],
            out_specs=[
                pl.BlockSpec((1, out, cols), lambda r, meta: (r, 0, 0)),
                pl.BlockSpec((GROUPS, slots, out // GROUPS, 128), lambda r, meta: (0, 0, 0, 0)),
            ],
            scratch_shapes=[
                pltpu.VMEM((rows + 4, channels, wide), BF16),
                pltpu.VMEM((rows + 2, out, wide), BF16),
                pltpu.VMEM((slots, out, 128), F32),
            ],
        ),
        compiler_params=pltpu.CompilerParams(vmem_limit_bytes=VMEM_LIMIT),
        name="ocean",
    )(meta, x, top, bottom, left, right, w1, b1, w2, b2, regrid)


def couple_kernel(
    lat_count,
    lon_count,
    count,
    own_index,
    north_index,
    south_index,
    slots,
    atmos,
    first,
    top,
    bottom,
    left,
    right,
    *scratch,
):
    lat, lon = lax.axis_index("lat"), lax.axis_index("lon")
    west = lax.rem(lon + lon_count - 1, lon_count)
    east = lax.rem(lon + 1, lon_count)
    across = lax.rem(lon + 2, lon_count)
    beside = lon + 1 - 2 * lax.rem(lon, 2)
    beside_across = lax.rem(beside + 2, lon_count)
    up, down, always = lat > 0, lat < lat_count - 1, lat >= 0
    edge = jnp.logical_or(lat == 0, lat == lat_count - 1)
    partners = [(lat, there, always) for there in (west, east, across)]
    for there, ok in ((lat - 1, up), (lat + 1, down)):
        partners += [(there, side, ok) for side in (west, lon, east)]
    greet(partners, jnp.where(edge, 6, 9))

    groups, total, size, cols = slots.shape
    rows, channels = first.shape[:2]
    own, north, south = (scratch[i * groups : (i + 1) * groups] for i in range(3))
    away, mine, from_core, to_z, from_z, edges = scratch[3 * groups : 3 * groups + 6]
    load_sem, y_send, y_recv, core_send, core_recv, z_send, z_recv, halo_send, halo_recv = scratch[
        3 * groups + 6 :
    ]
    low, high = pl.ds(0, count), pl.ds(total - count, count)
    everything = pl.ds(0, total)
    to_south, to_north, loads = [], [], []
    for g in range(groups):
        to_south.append(
            remote(
                slots.at[g, high], north[g].at[high], y_send.at[0, g], y_recv.at[0, g], lat + 1, lon
            )
        )
        to_north.append(
            remote(
                slots.at[g, low], south[g].at[low], y_send.at[1, g], y_recv.at[1, g], lat - 1, lon
            )
        )
        loads.append(
            pltpu.make_async_copy(slots.at[g], own[g].at[everything], load_sem.at[g])
        )
        pl.when(down)(to_south[g].start)
        pl.when(up)(to_north[g].start)
        loads[g].start()
    for buffer in (own, north, south):
        for g in range(groups):
            buffer[g][total] = jnp.zeros((size, cols), BF16)

    def dense(g, lon_there, store):
        def row(t, carry):
            at = lon_there * rows + t
            i, j = at // 128, lax.rem(at, 128)
            a = own_index[1, i, j]
            b = jnp.where(up, north_index[i, j], total)
            c = jnp.where(down, south_index[i, j], total)
            value = own[g][a].astype(F32) + north[g][b].astype(F32) + south[g][c].astype(F32)
            store(t, value.astype(BF16))
            return carry

        lax.fori_loop(0, rows, row, 0, unroll=8)

    core_copies, z_copies = [], []
    for g in range(groups):
        loads[g].wait()
        pl.when(up)(landed(north[g].at[high], y_recv.at[0, g]).wait)
        pl.when(down)(landed(south[g].at[low], y_recv.at[1, g]).wait)
        for part, (theirs, ours) in enumerate(((beside_across, across), (beside, lon))):

            def put_away(t, value):
                away[part, g, t] = value

            def put_mine(t, value):
                mine[part, g, t] = value

            dense(g, theirs, put_away)
            copy = remote(
                away.at[part, g],
                from_core.at[part, g],
                core_send.at[part, g],
                core_recv.at[part, g],
                lat,
                beside,
            )
            copy.start()
            core_copies.append(copy)
            dense(g, ours, put_mine)
            if part == 0:
                landed(from_core.at[0, g], core_recv.at[0, g]).wait()
                to_z[g] = (mine[0, g].astype(F32) + from_core[0, g].astype(F32)).astype(BF16)
                copy = remote(
                    to_z.at[g], from_z.at[g], z_send.at[g], z_recv.at[g], lat, across
                )
                copy.start()
                z_copies.append(copy)

    lane = lax.broadcasted_iota(jnp.int32, (size, cols), 1)
    tiles = edges.shape[0]
    for g in range(groups):
        landed(from_core.at[1, g], core_recv.at[1, g]).wait()
        landed(from_z.at[g], z_recv.at[g]).wait()
        part = pl.ds(g * size, size)
        for tile in range(tiles):
            edge = jnp.zeros((size, cols), F32)
            for k in range(32):
                r = tile * 32 + k
                flux = (
                    mine[1, g, r].astype(F32)
                    + from_core[1, g, r].astype(F32)
                    + from_z[g, r].astype(F32)
                )
                v = (atmos[r, part].astype(F32) + flux).astype(BF16)
                first[r, part] = v
                rolled = pltpu.roll(v.astype(F32), (4 * k + 2) % cols, 1)
                edge = jnp.where(lane // 4 == k, rolled, edge)
            edges[tile, part] = edge.astype(BF16)
    lo, hi = edges.at[0], edges.at[tiles - 1]
    moves = [
        (edges, right.at[pl.ds(1, tiles)], lat, west, always, always),
        (edges, left.at[pl.ds(1, tiles)], lat, east, always, always),
        (first.at[pl.ds(0, 2)], bottom, lat - 1, lon, up, down),
        (first.at[pl.ds(rows - 2, 2)], top, lat + 1, lon, down, up),
        (lo, right.at[tiles + 1], lat - 1, west, up, down),
        (lo, left.at[tiles + 1], lat - 1, east, up, down),
        (hi, right.at[0], lat + 1, west, down, up),
        (hi, left.at[0], lat + 1, east, down, up),
    ]
    copies = [
        remote(src, dst, halo_send.at[i], halo_recv.at[i], a, b)
        for i, (src, dst, a, b, _, _) in enumerate(moves)
    ]
    for copy, move in zip(copies, moves):
        pl.when(move[4])(copy.start)
    for copy in core_copies + z_copies:
        copy.wait_send()
    for g in range(groups):
        pl.when(down)(to_south[g].wait_send)
        pl.when(up)(to_north[g].wait_send)
    for i, (copy, move) in enumerate(zip(copies, moves)):
        pl.when(move[4])(copy.wait_send)
        pl.when(move[5])(landed(move[1], halo_recv.at[i]).wait)


def couple(index, north_index, south_index, slots, atmos, count, collective_id, lat_count, lon_count):
    groups, total, size, cols = slots.shape
    rows, channels, cols = atmos.shape
    tiles = rows // 32
    vmem = pl.BlockSpec(memory_space=pltpu.VMEM)
    smem = pl.BlockSpec(memory_space=pltpu.SMEM)
    dma = pltpu.SemaphoreType.DMA
    shapes = [(rows, channels, cols)] + [(2, channels, cols)] * 2 + [(tiles + 2, channels, cols)] * 2
    received = pltpu.VMEM((total + 1, size, cols), BF16)
    one = pltpu.VMEM((groups, rows, size, cols), BF16)
    two = pltpu.VMEM((2, groups, rows, size, cols), BF16)
    return pl.pallas_call(
        functools.partial(couple_kernel, lat_count, lon_count, count),
        out_shape=[jax.ShapeDtypeStruct(s, BF16) for s in shapes],
        in_specs=[smem] * 3 + whole_any(1) + [vmem],
        out_specs=[vmem] + whole_any(4),
        scratch_shapes=[received] * (3 * groups)
        + [two] * 3
        + [one] * 2
        + [pltpu.VMEM((tiles, channels, cols), BF16)]
        + [dma((groups,))]
        + [dma((2, groups))] * 4
        + [dma((groups,))] * 2
        + [dma((8,))] * 2,
        compiler_params=pltpu.CompilerParams(
            collective_id=collective_id, has_side_effects=True, vmem_limit_bytes=VMEM_LIMIT
        ),
        name="couple",
    )(index, north_index, south_index, slots, atmos)


def atmos_kernel(
    lat_count, a_ref, top_ref, bottom_ref, left_ref, right_ref, w1_ref, b1_ref, w2_ref, b2_ref, out_ref, tall, second
):
    count, channels, cols = a_ref.shape
    lat = lax.axis_index("lat")
    b1, b2 = column(b1_ref[...]), column(b2_ref[...])

    tall[2 : 2 + count, :, 0:cols] = a_ref[...]
    lane = lax.broadcasted_iota(jnp.int32, (channels, cols), 1)
    for tile in range(count // 32 + 2):
        side = jnp.where(lane % 4 < 2, left_ref[tile], right_ref[tile]).astype(F32)
        for k in range(32):
            r = tile * 32 - 32 + k
            if r < -2 or r >= count + 2:
                continue
            v = pltpu.roll(side, (126 - 4 * k) % cols, 1).astype(BF16)
            if r < 0 or r >= count:
                inside = lat > 0 if r < 0 else lat < lat_count - 1
                main = top_ref[r + 2] if r < 0 else bottom_ref[r - count]
                tall[r + 2, :, 0:cols] = jnp.where(inside, main, jnp.zeros_like(main))
                v = jnp.where(inside, v, jnp.zeros_like(v))
            tall[r + 2, :, cols:] = v

    def conv(source, weight, start, group):
        fields = [
            jnp.concatenate([source[start + i + d] for d in range(3)], axis=0)
            for i in range(group)
        ]
        return jnp.dot(weight, jnp.concatenate(fields, axis=1), preferred_element_type=F32)

    def first(step, carry):
        group = FIRST_ROWS
        start = step * group
        taps = conv(tall, w1_ref[...], start, group)
        for i in range(group):
            j = start + i
            value = silu(shifted_sum(taps[:, i * 2 * cols : (i + 1) * 2 * cols]) + b1)
            outside = jnp.logical_or(
                jnp.logical_and(j == 0, lat == 0),
                jnp.logical_and(j == count + 1, lat == lat_count - 1),
            )
            second[j] = jnp.where(outside, 0.0, value).astype(BF16)
        return carry

    lax.fori_loop(0, (count + 2) // FIRST_ROWS, first, 0)

    def last(step, carry):
        group = LAST_ROWS
        start = step * group
        taps = conv(second, w2_ref[...], start, group)
        for i in range(group):
            j = start + i
            value = shifted_sum(taps[:, i * 2 * cols : (i + 1) * 2 * cols])[:, :cols]
            out_ref[j] = (a_ref[j].astype(F32) + (value + b2)).astype(BF16)
        return carry

    lax.fori_loop(0, count // LAST_ROWS, last, 0)


def atmos_step(a, top, bottom, left, right, w1, b1, w2, b2, lat_count):
    count, channels, cols = a.shape
    vmem = pl.BlockSpec(memory_space=pltpu.VMEM)
    return pl.pallas_call(
        functools.partial(atmos_kernel, lat_count),
        out_shape=jax.ShapeDtypeStruct(a.shape, BF16),
        in_specs=[vmem] * 9,
        out_specs=vmem,
        scratch_shapes=[
            pltpu.VMEM((count + 4, channels, 2 * cols), BF16),
            pltpu.VMEM((count + 2, channels, 2 * cols), BF16),
        ],
        compiler_params=pltpu.CompilerParams(vmem_limit_bytes=VMEM_LIMIT),
        name="atmos",
    )(a, top, bottom, left, right, w1, b1, w2, b2)


def per_device(
    ocean_state,
    sea_mask,
    ocean_w1,
    ocean_b1,
    ocean_w2,
    ocean_b2,
    regrid_weight,
    route_dev,
    route_row,
    atmos_state,
    atmos_w1,
    atmos_b1,
    atmos_w2,
    atmos_b2,
):
    lat_count, lon_count = lax.axis_size("lat"), lax.axis_size("lon")
    lat = lax.axis_index("lat")
    atmos_rows = atmos_state.shape[1]

    field = jnp.concatenate(
        [
            ocean_state,
            sea_mask.astype(BF16)[None],
            jnp.zeros((3,) + sea_mask.shape, BF16),
        ],
        axis=0,
    ).transpose(1, 0, 2)
    key = ((route_dev - (lat - 1) * lon_count) * atmos_rows + route_row).reshape(-1)
    count = key.shape[0]
    order = jnp.arange(count, dtype=jnp.int32)
    place = jnp.sum((key[None, :] < key[:, None]).astype(jnp.int32), axis=1)
    again = (key[None, :] == key[:, None]) & (order[None, :] < order[:, None])
    meta = place * 2 + 1 - jnp.max(again.astype(jnp.int32), axis=1)
    per_step = lon_count * atmos_rows
    longest = jnp.maximum(
        jnp.sum((key < per_step).astype(jnp.int32)), jnp.sum((key >= 2 * per_step).astype(jnp.int32))
    )
    lanes = jnp.arange(8 * 128, dtype=jnp.int32)
    number = jnp.where(lanes < per_step, lanes, -4 * per_step).reshape(1, 8, 128)
    number = number + jnp.arange(3, dtype=jnp.int32)[:, None, None] * per_step
    index = jnp.min(
        jnp.where(number[..., None] == key[None, None, None, :], place[None, None, None, :], count),
        axis=3,
    )
    top, bottom, left, right, north_index, south_index, longest = ocean_halo(
        field, index, jnp.full((8, 128), longest, jnp.int32), lat_count, lon_count
    )
    which = sum((longest[0, 0] > n).astype(jnp.int32) for n in LENGTHS if n < count)
    ocean_next, slots = ocean_step(
        meta,
        field,
        top,
        bottom,
        left,
        right,
        stacked_weight(ocean_w1, 80),
        ocean_b1[None, :],
        stacked_weight(ocean_w2, 64),
        ocean_b2[None, :],
        regrid_weight.reshape(-1, 256, 128),
        lat_count,
    )
    lengths = [n for n in LENGTHS if n < count] + [count]

    def coupled(at):
        def branch(*operands):
            return tuple(couple(*operands, lengths[at], 1 + at, lat_count, lon_count))

        return branch

    first, top, bottom, left, right = lax.switch(
        which,
        [coupled(at) for at in range(len(lengths))],
        index,
        north_index,
        south_index,
        slots,
        atmos_state.transpose(1, 0, 2),
    )
    atmos_next = atmos_step(
        first,
        top,
        bottom,
        left,
        right,
        stacked_weight(atmos_w1, 64),
        atmos_b1[None, :],
        stacked_weight(atmos_w2, 64),
        atmos_b2[None, :],
        lat_count,
    )
    return ocean_next.transpose(1, 0, 2), atmos_next.transpose(1, 0, 2)


def solution(mesh):
    in_specs = (
        P(None, "lat", "lon"),
        P("lat", "lon"),
        P(),
        P(),
        P(),
        P(),
        P(("lat", "lon"), None, None, None),
        P(("lat", "lon"), None),
        P(("lat", "lon"), None),
        P(None, "lat", "lon"),
        P(),
        P(),
        P(),
        P(),
    )
    out_specs = (P(None, "lat", "lon"), P(None, "lat", "lon"))
    return jax.shard_map(
        per_device, mesh=mesh, in_specs=in_specs, out_specs=out_specs, check_vma=False
    )
```

```python
import functools

import jax
import jax.numpy as jnp
from jax import lax
from jax.experimental import pallas as pl
from jax.experimental.pallas import tpu as pltpu
from jax.sharding import PartitionSpec as P

MESH = pl.DeviceIdType.MESH
F32 = jnp.float32
BF16 = jnp.bfloat16
VMEM_LIMIT = 56 * 1024 * 1024
GROUPS = 4
FIRST_ROWS = 11
LAST_ROWS = 16
SHORT = 48


def silu(v):
    return 0.5 * v * (1.0 + jnp.tanh(0.5 * v))


def shifted_sum(taps):
    out = taps.shape[0] // 3
    columns = taps.shape[1]
    return (
        pltpu.roll(taps[0:out], 1, 1)
        + taps[out : 2 * out]
        + pltpu.roll(taps[2 * out :], columns - 1, 1)
    )


def stacked_weight(weight, padded_in):
    out, inn = weight.shape[:2]
    weight = jnp.pad(weight, ((0, 0), (0, padded_in - inn), (0, 0), (0, 0)))
    return weight.transpose(3, 0, 2, 1).reshape(3 * out, 3 * padded_in)


def column(bias):
    n = bias.shape[1]
    at = lax.broadcasted_iota(jnp.int32, (n, n), 0) == lax.broadcasted_iota(jnp.int32, (n, n), 1)
    return jnp.sum(jnp.where(at, bias, jnp.zeros_like(bias)), axis=1, keepdims=True)


def remote(src, dst, send_sem, recv_sem, lat, lon):
    return pltpu.make_async_remote_copy(
        src_ref=src,
        dst_ref=dst,
        send_sem=send_sem,
        recv_sem=recv_sem,
        device_id={"lat": lat, "lon": lon},
        device_id_type=MESH,
    )


def landed(ref, sem):
    return pltpu.make_async_copy(ref, ref, sem)


def greet(partners, waits):
    barrier = pltpu.get_barrier_semaphore()
    for lat, lon, ok in partners:

        @pl.when(ok)
        def _():
            pl.semaphore_signal(
                barrier, inc=1, device_id={"lat": lat, "lon": lon}, device_id_type=MESH
            )

    pl.semaphore_wait(barrier, waits)


def whole_any(count):
    return [pl.BlockSpec(memory_space=pl.ANY)] * count


def ocean_halo_kernel(
    lat_count,
    lon_count,
    atmos_rows,
    field,
    key_ref,
    top,
    bottom,
    left,
    right,
    index,
    north_index,
    south_index,
    meta,
    longest,
    edges,
    send_sem,
    recv_sem,
):
    lat, lon = lax.axis_index("lat"), lax.axis_index("lon")
    rows, channels, cols = field.shape
    west = lax.rem(lon + lon_count - 1, lon_count)
    east = lax.rem(lon + 1, lon_count)
    up, down, always = lat > 0, lat < lat_count - 1, lat >= 0
    edge = jnp.logical_or(lat == 0, lat == lat_count - 1)
    partners = [(lat, west, always), (lat, east, always)]
    for there, ok in ((lat - 1, up), (lat + 1, down)):
        partners += [(there, side, ok) for side in (west, lon, east)]

    key = key_ref[...]
    count = key.shape[1]
    key_down = column(key)
    across = lax.broadcasted_iota(jnp.int32, (count, count), 1)
    along = lax.broadcasted_iota(jnp.int32, (count, count), 0)
    place = jnp.sum((key_down < key).astype(jnp.int32), axis=0, keepdims=True)
    again = jnp.logical_and(key_down == key, along < across).astype(jnp.int32)
    meta[...] = place * 2 + 1 - jnp.max(again, axis=0, keepdims=True)
    place_down = column(place)
    per_step = lon_count * atmos_rows
    lane = lax.broadcasted_iota(jnp.int32, (1, count), 1)
    for step in range(3):
        for row in range(8):
            if row * count < per_step:
                number = lane + (step * per_step + row * count)
                places = jnp.min(
                    jnp.where(key_down == number, place_down, count), axis=0, keepdims=True
                )
                index[step, row : row + 1, :] = places
            else:
                index[step, row : row + 1, :] = jnp.full((1, count), count, jnp.int32)
    low = jnp.sum((key < per_step).astype(jnp.int32), axis=1, keepdims=True)
    high = jnp.sum((key >= 2 * per_step).astype(jnp.int32), axis=1, keepdims=True)
    longest[...] = jnp.broadcast_to(jnp.maximum(low, high), longest.shape)

    lane = lax.broadcasted_iota(jnp.int32, (channels, 128), 1)
    tile = jnp.zeros((channels, 128), F32)
    for k in range(rows):
        both = jnp.where(lane < 64, field[k, :, 0:128], field[k, :, cols - 128 :]).astype(F32)
        tile = jnp.where(lane // 4 == k, pltpu.roll(both, (4 * k + 2) % 128, 1), tile)
    edges[...] = tile.astype(BF16)

    greet(partners, jnp.where(edge, 5, 8))
    moves = [
        (field.at[pl.ds(0, 2)], bottom, lat - 1, lon, up, down),
        (field.at[pl.ds(rows - 2, 2)], top, lat + 1, lon, down, up),
        (edges, right.at[1], lat, west, always, always),
        (edges, left.at[1], lat, east, always, always),
        (edges, right.at[2], lat - 1, west, up, down),
        (edges, left.at[2], lat - 1, east, up, down),
        (edges, right.at[0], lat + 1, west, down, up),
        (edges, left.at[0], lat + 1, east, down, up),
        (index.at[0], south_index, lat - 1, lon, up, down),
        (index.at[2], north_index, lat + 1, lon, down, up),
    ]
    copies = [
        remote(src, dst, send_sem.at[i], recv_sem.at[i], a, b)
        for i, (src, dst, a, b, _, _) in enumerate(moves)
    ]
    for copy, move in zip(copies, moves):
        pl.when(move[4])(copy.start)
    for i, (copy, move) in enumerate(zip(copies, moves)):
        pl.when(move[4])(copy.wait_send)
        pl.when(move[5])(landed(move[1], recv_sem.at[i]).wait)


def ocean_halo(field, key, lat_count, lon_count, atmos_rows):
    rows, channels, cols = field.shape
    shapes = [(2, channels, cols)] * 2 + [(3, channels, 128)] * 2
    table = jax.ShapeDtypeStruct((8, key.shape[1]), jnp.int32)
    vmem = pl.BlockSpec(memory_space=pltpu.VMEM)
    return pl.pallas_call(
        functools.partial(ocean_halo_kernel, lat_count, lon_count, atmos_rows),
        out_shape=[jax.ShapeDtypeStruct(s, BF16) for s in shapes]
        + [jax.ShapeDtypeStruct((3,) + table.shape, jnp.int32), table, table]
        + [jax.ShapeDtypeStruct(key.shape, jnp.int32), table],
        in_specs=[vmem] * 2,
        out_specs=whole_any(4) + [vmem] + whole_any(2) + [vmem] * 2,
        scratch_shapes=[
            pltpu.VMEM((channels, 128), BF16),
            pltpu.SemaphoreType.DMA((10,)),
            pltpu.SemaphoreType.DMA((10,)),
        ],
        compiler_params=pltpu.CompilerParams(
            collective_id=0, has_side_effects=True, vmem_limit_bytes=VMEM_LIMIT
        ),
        name="ocean_halo",
    )(field, key)


def ocean_kernel(
    lat_count,
    meta,
    x_ref,
    top_ref,
    bottom_ref,
    left_ref,
    right_ref,
    w1_ref,
    b1_ref,
    w2_ref,
    b2_ref,
    regrid_ref,
    next_ref,
    slots_ref,
    tall,
    hidden,
    sums,
):
    row = lax.rem(pl.program_id(0), 16)
    rows, channels, cols = x_ref.shape
    mask_at = 76
    b1, b2 = column(b1_ref[...]), column(b2_ref[...])

    def first_conv(j):
        field = jnp.concatenate([tall[j], tall[j + 1], tall[j + 2]], axis=0)
        taps = jnp.dot(w1_ref[...], field, preferred_element_type=F32)
        mask = tall[j + 1, mask_at : mask_at + 1, :].astype(F32)
        hidden[j] = (silu(shifted_sum(taps) + b1) * mask).astype(BF16)

    @pl.when(row == 0)
    def _():
        lat = lax.axis_index("lat")
        lane = lax.broadcasted_iota(jnp.int32, (channels, 128), 1)
        tall[2 : 2 + rows, :, 0:cols] = x_ref[...]
        for tile in range(3):
            both = jnp.where(lane % 4 < 2, left_ref[tile], right_ref[tile]).astype(F32)
            for k in range(rows):
                j = (tile - 1) * rows + k + 2
                if j < 0 or j >= rows + 4:
                    continue
                side = pltpu.roll(both, (126 - 4 * k) % 128, 1).astype(BF16)
                if tile != 1:
                    inside = lat > 0 if tile == 0 else lat < lat_count - 1
                    main = top_ref[j] if tile == 0 else bottom_ref[j - rows - 2]
                    tall[j, :, 0:cols] = jnp.where(inside, main, jnp.zeros_like(main))
                    side = jnp.where(inside, side, jnp.zeros_like(side))
                tall[j, :, cols:] = side
        first_conv(0)
        first_conv(1)

    first_conv(lax.rem(row + 2, 16))
    field = jnp.concatenate([hidden[row], hidden[row + 1], hidden[row + 2]], axis=0)
    taps = jnp.dot(w2_ref[...], field, preferred_element_type=F32)
    mask = tall[row + 2, mask_at : mask_at + 1, :].astype(F32)
    result = ((shifted_sum(taps) + b2) * mask).astype(BF16)[:, :cols]
    next_ref[0] = result
    blocks = regrid_ref.shape[0]
    for q in range(blocks):
        field = result[:, q * 128 : (q + 1) * 128]
        both = lax.dot_general(
            field, regrid_ref[q], (((1,), (1,)), ((), ())), preferred_element_type=F32
        ).astype(BF16)
        for k in range(2):
            what = meta[0, (row * blocks + q) * 2 + k]
            at = what // 2
            value = both[:, k * 128 : (k + 1) * 128].astype(F32)
            sums[at] = jnp.where(lax.rem(what, 2) == 1, value, sums[at] + value)

    @pl.when(row == rows - 1)
    def _():
        groups, slots, size = slots_ref.shape[:3]

        def rounded(i, carry):
            for g in range(groups):
                slots_ref[g, i] = sums[i, g * size : (g + 1) * size].astype(BF16)
            return carry

        lax.fori_loop(0, slots, rounded, 0)


def ocean_step(meta, x, top, bottom, left, right, w1, b1, w2, b2, regrid, lat_count):
    rows, channels, cols = x.shape
    wide = cols + 128
    out = w2.shape[0] // 3
    slots = meta.shape[1]

    def whole(array):
        zeros = (0,) * array.ndim
        return pl.BlockSpec(array.shape, lambda r, meta: zeros)

    blocks = regrid.shape[0] // rows
    return pl.pallas_call(
        functools.partial(ocean_kernel, lat_count),
        out_shape=(
            jax.ShapeDtypeStruct((rows, out, cols), BF16),
            jax.ShapeDtypeStruct((GROUPS, slots, out // GROUPS, 128), BF16),
        ),
        grid_spec=pltpu.PrefetchScalarGridSpec(
            num_scalar_prefetch=1,
            grid=(rows,),
            in_specs=[whole(a) for a in (x, top, bottom, left, right, w1, b1, w2, b2)]
            + [pl.BlockSpec((blocks, 256, 128), lambda r, meta: (r, 0, 0))],
            out_specs=[
                pl.BlockSpec((1, out, cols), lambda r, meta: (r, 0, 0)),
                pl.BlockSpec((GROUPS, slots, out // GROUPS, 128), lambda r, meta: (0, 0, 0, 0)),
            ],
            scratch_shapes=[
                pltpu.VMEM((rows + 4, channels, wide), BF16),
                pltpu.VMEM((rows + 2, out, wide), BF16),
                pltpu.VMEM((slots, out, 128), F32),
            ],
        ),
        compiler_params=pltpu.CompilerParams(vmem_limit_bytes=VMEM_LIMIT),
        name="ocean",
    )(meta, x, top, bottom, left, right, w1, b1, w2, b2, regrid)


def couple_kernel(
    lat_count,
    lon_count,
    count,
    own_index,
    north_index,
    south_index,
    slots,
    atmos,
    longest,
    first,
    top,
    bottom,
    left,
    right,
    longest_of_all,
    *scratch,
):
    lat, lon = lax.axis_index("lat"), lax.axis_index("lon")
    west = lax.rem(lon + lon_count - 1, lon_count)
    east = lax.rem(lon + 1, lon_count)
    across = lax.rem(lon + 2, lon_count)
    beside = lon + 1 - 2 * lax.rem(lon, 2)
    beside_across = lax.rem(beside + 2, lon_count)
    up, down, always = lat > 0, lat < lat_count - 1, lat >= 0
    edge = jnp.logical_or(lat == 0, lat == lat_count - 1)
    partners = [(lat, there, always) for there in (west, east, across)]
    for there, ok in ((lat - 1, up), (lat + 1, down)):
        partners += [(there, side, ok) for side in (west, lon, east)]
    four, inner = lat // 4, lax.rem(lat, 4)
    fours = lat_count // 4
    rounds = [
        [(lat, lax.rem(lon + k, lon_count)) for k in range(1, lon_count)],
        [(four * 4 + lax.rem(inner + k, 4), lon) for k in range(1, 4)],
        [(lax.rem(four + k, fours) * 4 + inner, lon) for k in range(1, fours)],
    ]
    partners += [(a, b, always) for peers in rounds[1:] for a, b in peers]
    greet(partners, jnp.where(edge, 6, 9) + sum(len(peers) for peers in rounds[1:]))

    groups, total, size, cols = slots.shape
    rows, channels = first.shape[:2]
    own, north, south = (scratch[i * groups : (i + 1) * groups] for i in range(3))
    away, mine, from_core, to_z, from_z, edges = scratch[3 * groups : 3 * groups + 6]
    load_sem, y_send, y_recv, core_send, core_recv, z_send, z_recv, halo_send, halo_recv = scratch[
        3 * groups + 6 : 3 * groups + 15
    ]
    gathered, partial, max_send, max_recv = scratch[3 * groups + 15 :]
    held, waiting, small = longest, [], []

    def send_maximum(number):
        begin = sum(len(peers) for peers in rounds[:number])
        for i, (a, b) in enumerate(rounds[number], begin):
            small.append(remote(held, gathered.at[i], max_send.at[i], max_recv.at[i], a, b))
            small[-1].start()
            waiting.append(i)

    def receive_maximum(target):
        value = held[...]
        for i in waiting:
            landed(gathered.at[i], max_recv.at[i]).wait()
            value = jnp.maximum(value, gathered[i])
        waiting.clear()
        target[...] = value
        return target

    send_maximum(0)
    low, high = pl.ds(0, count), pl.ds(total - count, count)
    everything = pl.ds(0, total)
    to_south, to_north, loads = [], [], []
    for g in range(groups):
        to_south.append(
            remote(
                slots.at[g, high], north[g].at[high], y_send.at[0, g], y_recv.at[0, g], lat + 1, lon
            )
        )
        to_north.append(
            remote(
                slots.at[g, low], south[g].at[low], y_send.at[1, g], y_recv.at[1, g], lat - 1, lon
            )
        )
        loads.append(
            pltpu.make_async_copy(slots.at[g], own[g].at[everything], load_sem.at[g])
        )
        pl.when(down)(to_south[g].start)
        pl.when(up)(to_north[g].start)
        loads[g].start()
    for buffer in (own, north, south):
        for g in range(groups):
            buffer[g][total] = jnp.zeros((size, cols), BF16)

    def dense(g, lon_there, store):
        def row(t, carry):
            at = lon_there * rows + t
            i, j = at // 128, lax.rem(at, 128)
            a = own_index[1, i, j]
            b = jnp.where(up, north_index[i, j], total)
            c = jnp.where(down, south_index[i, j], total)
            value = own[g][a].astype(F32) + north[g][b].astype(F32) + south[g][c].astype(F32)
            store(t, value.astype(BF16))
            return carry

        lax.fori_loop(0, rows, row, 0, unroll=8)

    core_copies, z_copies = [], []
    for g in range(groups):
        loads[g].wait()
        pl.when(up)(landed(north[g].at[high], y_recv.at[0, g]).wait)
        pl.when(down)(landed(south[g].at[low], y_recv.at[1, g]).wait)
        for part, (theirs, ours) in enumerate(((beside_across, across), (beside, lon))):

            def put_away(t, value):
                away[part, g, t] = value

            def put_mine(t, value):
                mine[part, g, t] = value

            dense(g, theirs, put_away)
            copy = remote(
                away.at[part, g],
                from_core.at[part, g],
                core_send.at[part, g],
                core_recv.at[part, g],
                lat,
                beside,
            )
            copy.start()
            core_copies.append(copy)
            dense(g, ours, put_mine)
            if part == 0:
                landed(from_core.at[0, g], core_recv.at[0, g]).wait()
                to_z[g] = (mine[0, g].astype(F32) + from_core[0, g].astype(F32)).astype(BF16)
                copy = remote(
                    to_z.at[g], from_z.at[g], z_send.at[g], z_recv.at[g], lat, across
                )
                copy.start()
                z_copies.append(copy)
        if g < 2:
            held = receive_maximum(partial.at[g])
            send_maximum(g + 1)

    lane = lax.broadcasted_iota(jnp.int32, (size, cols), 1)
    tiles = edges.shape[0]
    for g in range(groups):
        landed(from_core.at[1, g], core_recv.at[1, g]).wait()
        landed(from_z.at[g], z_recv.at[g]).wait()
        part = pl.ds(g * size, size)
        for tile in range(tiles):
            edge = jnp.zeros((size, cols), F32)
            for k in range(32):
                r = tile * 32 + k
                flux = (
                    mine[1, g, r].astype(F32)
                    + from_core[1, g, r].astype(F32)
                    + from_z[g, r].astype(F32)
                )
                v = (atmos[r, part].astype(F32) + flux).astype(BF16)
                first[r, part] = v
                rolled = pltpu.roll(v.astype(F32), (4 * k + 2) % cols, 1)
                edge = jnp.where(lane // 4 == k, rolled, edge)
            edges[tile, part] = edge.astype(BF16)
    lo, hi = edges.at[0], edges.at[tiles - 1]
    moves = [
        (edges, right.at[pl.ds(1, tiles)], lat, west, always, always),
        (edges, left.at[pl.ds(1, tiles)], lat, east, always, always),
        (first.at[pl.ds(0, 2)], bottom, lat - 1, lon, up, down),
        (first.at[pl.ds(rows - 2, 2)], top, lat + 1, lon, down, up),
        (lo, right.at[tiles + 1], lat - 1, west, up, down),
        (lo, left.at[tiles + 1], lat - 1, east, up, down),
        (hi, right.at[0], lat + 1, west, down, up),
        (hi, left.at[0], lat + 1, east, down, up),
    ]
    copies = [
        remote(src, dst, halo_send.at[i], halo_recv.at[i], a, b)
        for i, (src, dst, a, b, _, _) in enumerate(moves)
    ]
    for copy, move in zip(copies, moves):
        pl.when(move[4])(copy.start)
    receive_maximum(longest_of_all)
    for copy in core_copies + z_copies + small:
        copy.wait_send()
    for g in range(groups):
        pl.when(down)(to_south[g].wait_send)
        pl.when(up)(to_north[g].wait_send)
    for i, (copy, move) in enumerate(zip(copies, moves)):
        pl.when(move[4])(copy.wait_send)
        pl.when(move[5])(landed(move[1], halo_recv.at[i]).wait)


def couple(
    index, north_index, south_index, slots, atmos, longest, count, collective_id, lat_count, lon_count
):
    groups, total, size, cols = slots.shape
    rows, channels, cols = atmos.shape
    tiles = rows // 32
    vmem = pl.BlockSpec(memory_space=pltpu.VMEM)
    smem = pl.BlockSpec(memory_space=pltpu.SMEM)
    dma = pltpu.SemaphoreType.DMA
    shapes = [(rows, channels, cols)] + [(2, channels, cols)] * 2 + [(tiles + 2, channels, cols)] * 2
    received = pltpu.VMEM((total + 1, size, cols), BF16)
    peers = lon_count - 1 + 3 + lat_count // 4 - 1
    one = pltpu.VMEM((groups, rows, size, cols), BF16)
    two = pltpu.VMEM((2, groups, rows, size, cols), BF16)
    return pl.pallas_call(
        functools.partial(couple_kernel, lat_count, lon_count, count),
        out_shape=[jax.ShapeDtypeStruct(s, BF16) for s in shapes]
        + [jax.ShapeDtypeStruct(longest.shape, jnp.int32)],
        in_specs=[smem] * 3 + whole_any(1) + [vmem] * 2,
        out_specs=[vmem] + whole_any(4) + [vmem],
        scratch_shapes=[received] * (3 * groups)
        + [two] * 3
        + [one] * 2
        + [pltpu.VMEM((tiles, channels, cols), BF16)]
        + [dma((groups,))]
        + [dma((2, groups))] * 4
        + [dma((groups,))] * 2
        + [dma((8,))] * 2
        + [pltpu.VMEM((peers,) + longest.shape, jnp.int32)]
        + [pltpu.VMEM((2,) + longest.shape, jnp.int32)]
        + [dma((peers,))] * 2,
        compiler_params=pltpu.CompilerParams(
            collective_id=collective_id, has_side_effects=True, vmem_limit_bytes=VMEM_LIMIT
        ),
        name="couple",
    )(index, north_index, south_index, slots, atmos, longest)


def atmos_kernel(
    lat_count, a_ref, top_ref, bottom_ref, left_ref, right_ref, w1_ref, b1_ref, w2_ref, b2_ref, out_ref, tall, second
):
    count, channels, cols = a_ref.shape
    lat = lax.axis_index("lat")
    b1, b2 = column(b1_ref[...]), column(b2_ref[...])

    tall[2 : 2 + count, :, 0:cols] = a_ref[...]
    lane = lax.broadcasted_iota(jnp.int32, (channels, cols), 1)
    for tile in range(count // 32 + 2):
        side = jnp.where(lane % 4 < 2, left_ref[tile], right_ref[tile]).astype(F32)
        for k in range(32):
            r = tile * 32 - 32 + k
            if r < -2 or r >= count + 2:
                continue
            v = pltpu.roll(side, (126 - 4 * k) % cols, 1).astype(BF16)
            if r < 0 or r >= count:
                inside = lat > 0 if r < 0 else lat < lat_count - 1
                main = top_ref[r + 2] if r < 0 else bottom_ref[r - count]
                tall[r + 2, :, 0:cols] = jnp.where(inside, main, jnp.zeros_like(main))
                v = jnp.where(inside, v, jnp.zeros_like(v))
            tall[r + 2, :, cols:] = v

    def conv(source, weight, start, group):
        fields = [
            jnp.concatenate([source[start + i + d] for d in range(3)], axis=0)
            for i in range(group)
        ]
        return jnp.dot(weight, jnp.concatenate(fields, axis=1), preferred_element_type=F32)

    def first(step, carry):
        group = FIRST_ROWS
        start = step * group
        taps = conv(tall, w1_ref[...], start, group)
        for i in range(group):
            j = start + i
            value = silu(shifted_sum(taps[:, i * 2 * cols : (i + 1) * 2 * cols]) + b1)
            outside = jnp.logical_or(
                jnp.logical_and(j == 0, lat == 0),
                jnp.logical_and(j == count + 1, lat == lat_count - 1),
            )
            second[j] = jnp.where(outside, 0.0, value).astype(BF16)
        return carry

    lax.fori_loop(0, (count + 2) // FIRST_ROWS, first, 0)

    def last(step, carry):
        group = LAST_ROWS
        start = step * group
        taps = conv(second, w2_ref[...], start, group)
        for i in range(group):
            j = start + i
            value = shifted_sum(taps[:, i * 2 * cols : (i + 1) * 2 * cols])[:, :cols]
            out_ref[j] = (a_ref[j].astype(F32) + (value + b2)).astype(BF16)
        return carry

    lax.fori_loop(0, count // LAST_ROWS, last, 0)


def atmos_step(a, top, bottom, left, right, w1, b1, w2, b2, lat_count):
    count, channels, cols = a.shape
    vmem = pl.BlockSpec(memory_space=pltpu.VMEM)
    return pl.pallas_call(
        functools.partial(atmos_kernel, lat_count),
        out_shape=jax.ShapeDtypeStruct(a.shape, BF16),
        in_specs=[vmem] * 9,
        out_specs=vmem,
        scratch_shapes=[
            pltpu.VMEM((count + 4, channels, 2 * cols), BF16),
            pltpu.VMEM((count + 2, channels, 2 * cols), BF16),
        ],
        compiler_params=pltpu.CompilerParams(vmem_limit_bytes=VMEM_LIMIT),
        name="atmos",
    )(a, top, bottom, left, right, w1, b1, w2, b2)


def per_device(
    ocean_state,
    sea_mask,
    ocean_w1,
    ocean_b1,
    ocean_w2,
    ocean_b2,
    regrid_weight,
    route_dev,
    route_row,
    atmos_state,
    atmos_w1,
    atmos_b1,
    atmos_w2,
    atmos_b2,
):
    lat_count, lon_count = lax.axis_size("lat"), lax.axis_size("lon")
    lat = lax.axis_index("lat")
    atmos_rows = atmos_state.shape[1]

    field = jnp.concatenate(
        [
            ocean_state,
            sea_mask.astype(BF16)[None],
            jnp.zeros((3,) + sea_mask.shape, BF16),
        ],
        axis=0,
    ).transpose(1, 0, 2)
    key = ((route_dev - (lat - 1) * lon_count) * atmos_rows + route_row).reshape(1, -1)
    count = key.shape[1]
    top, bottom, left, right, index, north_index, south_index, meta, longest = ocean_halo(
        field, key, lat_count, lon_count, atmos_rows
    )
    ocean_next, slots = ocean_step(
        meta,
        field,
        top,
        bottom,
        left,
        right,
        stacked_weight(ocean_w1, 80),
        ocean_b1[None, :],
        stacked_weight(ocean_w2, 64),
        ocean_b2[None, :],
        regrid_weight.reshape(-1, 256, 128),
        lat_count,
    )
    operands = (index, north_index, south_index, slots, atmos_state.transpose(1, 0, 2), longest)
    *coupled, longest = couple(*operands, SHORT, 1, lat_count, lon_count)
    first, top, bottom, left, right = lax.cond(
        longest[0, 0] > SHORT,
        lambda short, operands: tuple(couple(*operands, count, 2, lat_count, lon_count)[:5]),
        lambda short, operands: short,
        tuple(coupled),
        operands,
    )
    atmos_next = atmos_step(
        first,
        top,
        bottom,
        left,
        right,
        stacked_weight(atmos_w1, 64),
        atmos_b1[None, :],
        stacked_weight(atmos_w2, 64),
        atmos_b2[None, :],
        lat_count,
    )
    return ocean_next.transpose(1, 0, 2), atmos_next.transpose(1, 0, 2)


def solution(mesh):
    in_specs = (
        P(None, "lat", "lon"),
        P("lat", "lon"),
        P(),
        P(),
        P(),
        P(),
        P(("lat", "lon"), None, None, None),
        P(("lat", "lon"), None),
        P(("lat", "lon"), None),
        P(None, "lat", "lon"),
        P(),
        P(),
        P(),
        P(),
    )
    out_specs = (P(None, "lat", "lon"), P(None, "lat", "lon"))
    return jax.shard_map(
        per_device, mesh=mesh, in_specs=in_specs, out_specs=out_specs, check_vma=False
    )
```

```python
import functools

import jax
import jax.numpy as jnp
from jax import lax
from jax.experimental import pallas as pl
from jax.experimental.pallas import tpu as pltpu
from jax.sharding import PartitionSpec as P

MESH = pl.DeviceIdType.MESH
F32 = jnp.float32
BF16 = jnp.bfloat16
VMEM_LIMIT = 56 * 1024 * 1024
GROUPS = 4
FIRST_ROWS = 11
LAST_ROWS = 16
SHORT = 32
EDGE_SHORT = 48


def silu(v):
    return 0.5 * v * (1.0 + jnp.tanh(0.5 * v))


def shifted_sum(taps):
    out = taps.shape[0] // 3
    columns = taps.shape[1]
    return (
        pltpu.roll(taps[0:out], 1, 1)
        + taps[out : 2 * out]
        + pltpu.roll(taps[2 * out :], columns - 1, 1)
    )


def stack_weight(weight_ref, out_ref):
    out, inn = weight_ref.shape[2:]
    padded = out_ref.shape[1] // 3
    for dc in range(3):
        pieces = []
        for dr in range(3):
            pieces.append(weight_ref[dr, dc].astype(F32))
            if padded > inn:
                pieces.append(jnp.zeros((out, padded - inn), F32))
        out_ref[dc * out : (dc + 1) * out, :] = jnp.concatenate(pieces, axis=1).astype(BF16)


def column(bias):
    n = bias.shape[1]
    at = lax.broadcasted_iota(jnp.int32, (n, n), 0) == lax.broadcasted_iota(jnp.int32, (n, n), 1)
    return jnp.sum(jnp.where(at, bias, jnp.zeros_like(bias)), axis=1, keepdims=True)


def remote(src, dst, send_sem, recv_sem, lat, lon):
    return pltpu.make_async_remote_copy(
        src_ref=src,
        dst_ref=dst,
        send_sem=send_sem,
        recv_sem=recv_sem,
        device_id={"lat": lat, "lon": lon},
        device_id_type=MESH,
    )


def landed(ref, sem):
    return pltpu.make_async_copy(ref, ref, sem)


def greet(partners):
    barrier = pltpu.get_barrier_semaphore()
    for lat, lon, ok in partners:

        @pl.when(ok)
        def _():
            pl.semaphore_signal(
                barrier, inc=1, device_id={"lat": lat, "lon": lon}, device_id_type=MESH
            )


def greeted(waits):
    pl.semaphore_wait(pltpu.get_barrier_semaphore(), waits)


def whole_any(count):
    return [pl.BlockSpec(memory_space=pl.ANY)] * count


def ocean_halo_kernel(
    lat_count,
    lon_count,
    atmos_rows,
    field,
    dev_ref,
    row_ref,
    w1_ref,
    w2_ref,
    w3_ref,
    w4_ref,
    top,
    bottom,
    left,
    right,
    index,
    north_index,
    south_index,
    meta,
    overflow,
    w1_out,
    w2_out,
    w3_out,
    w4_out,
    edges,
    send_sem,
    recv_sem,
):
    lat, lon = lax.axis_index("lat"), lax.axis_index("lon")
    rows, channels, cols = field.shape
    west = lax.rem(lon + lon_count - 1, lon_count)
    east = lax.rem(lon + 1, lon_count)
    up, down, always = lat > 0, lat < lat_count - 1, lat >= 0
    edge = jnp.logical_or(lat == 0, lat == lat_count - 1)
    partners = [(lat, west, always), (lat, east, always)]
    for there, ok in ((lat - 1, up), (lat + 1, down)):
        partners += [(there, side, ok) for side in (west, lon, east)]
    greet(partners)

    keys = (dev_ref[...] - (lat - 1) * lon_count) * atmos_rows + row_ref[...]
    key = jnp.concatenate([keys[k : k + 1] for k in range(keys.shape[0])], axis=1)
    count = key.shape[1]
    key_down = column(key)
    blocks = keys.shape[1]
    across = lax.broadcasted_iota(jnp.int32, (count, count), 1)
    across = lax.rem(across, blocks) * keys.shape[0] + lax.div(across, blocks)
    along = lax.broadcasted_iota(jnp.int32, (count, count), 0)
    along = lax.rem(along, blocks) * keys.shape[0] + lax.div(along, blocks)
    place = jnp.sum((key_down < key).astype(jnp.int32), axis=0, keepdims=True)
    again = jnp.logical_and(key_down == key, along < across).astype(jnp.int32)
    meta[...] = place * 2 + 1 - jnp.max(again, axis=0, keepdims=True)
    place_down = column(place)
    per_step = lon_count * atmos_rows
    lane = lax.broadcasted_iota(jnp.int32, (1, count), 1)
    for step in range(3):
        for row in range(8):
            if row * count < per_step:
                number = lane + (step * per_step + row * count)
                places = jnp.min(
                    jnp.where(key_down == number, place_down, count), axis=0, keepdims=True
                )
                index[step, row : row + 1, :] = places
            else:
                index[step, row : row + 1, :] = jnp.full((1, count), count, jnp.int32)
    low = jnp.sum((key < per_step).astype(jnp.int32), axis=1, keepdims=True)
    high = jnp.sum((key >= 2 * per_step).astype(jnp.int32), axis=1, keepdims=True)
    most = jnp.where(edge, EDGE_SHORT, SHORT)
    long = (jnp.maximum(low, high) > most).astype(jnp.int32)
    overflow[...] = jnp.broadcast_to(long, overflow.shape)

    lane = lax.broadcasted_iota(jnp.int32, (channels, 128), 1)
    tile = jnp.zeros((channels, 128), F32)
    for k in range(rows):
        both = jnp.where(lane < 64, field[k, :, 0:128], field[k, :, cols - 128 :]).astype(F32)
        tile = jnp.where(lane // 4 == k, pltpu.roll(both, (4 * k + 2) % 128, 1), tile)
    edges[...] = tile.astype(BF16)

    greeted(jnp.where(edge, 5, 8))
    moves = [
        (field.at[pl.ds(0, 2)], bottom, lat - 1, lon, up, down),
        (field.at[pl.ds(rows - 2, 2)], top, lat + 1, lon, down, up),
        (edges, right.at[1], lat, west, always, always),
        (edges, left.at[1], lat, east, always, always),
        (edges, right.at[2], lat - 1, west, up, down),
        (edges, left.at[2], lat - 1, east, up, down),
        (edges, right.at[0], lat + 1, west, down, up),
        (edges, left.at[0], lat + 1, east, down, up),
        (index.at[0], south_index, lat - 1, lon, up, down),
        (index.at[2], north_index, lat + 1, lon, down, up),
    ]
    copies = [
        remote(src, dst, send_sem.at[i], recv_sem.at[i], a, b)
        for i, (src, dst, a, b, _, _) in enumerate(moves)
    ]
    for copy, move in zip(copies, moves):
        pl.when(move[4])(copy.start)
    for weight, out in ((w1_ref, w1_out), (w2_ref, w2_out), (w3_ref, w3_out), (w4_ref, w4_out)):
        stack_weight(weight, out)
    for i, (copy, move) in enumerate(zip(copies, moves)):
        pl.when(move[4])(copy.wait_send)
        pl.when(move[5])(landed(move[1], recv_sem.at[i]).wait)


def ocean_halo(field, route_dev, route_row, weights, lat_count, lon_count, atmos_rows):
    rows, channels, cols = field.shape
    count = route_dev.size
    weights = [w.transpose(2, 3, 0, 1) for w in weights]
    stacked = [
        jax.ShapeDtypeStruct((3 * w.shape[2], 3 * (-(-w.shape[3] // 16) * 16)), BF16) for w in weights
    ]
    shapes = [(2, channels, cols)] * 2 + [(3, channels, 128)] * 2
    table = jax.ShapeDtypeStruct((8, count), jnp.int32)
    vmem = pl.BlockSpec(memory_space=pltpu.VMEM)
    return pl.pallas_call(
        functools.partial(ocean_halo_kernel, lat_count, lon_count, atmos_rows),
        out_shape=[jax.ShapeDtypeStruct(s, BF16) for s in shapes]
        + [jax.ShapeDtypeStruct((3,) + table.shape, jnp.int32), table, table]
        + [jax.ShapeDtypeStruct((1, count), jnp.int32), table]
        + stacked,
        in_specs=[vmem] * 7,
        out_specs=whole_any(4) + [vmem] + whole_any(2) + [vmem] * 6,
        scratch_shapes=[
            pltpu.VMEM((channels, 128), BF16),
            pltpu.SemaphoreType.DMA((10,)),
            pltpu.SemaphoreType.DMA((10,)),
        ],
        compiler_params=pltpu.CompilerParams(
            collective_id=0, has_side_effects=True, vmem_limit_bytes=VMEM_LIMIT
        ),
        name="ocean_halo",
    )(field, route_dev.T, route_row.T, *weights)


def ocean_kernel(
    lat_count,
    meta,
    x_ref,
    top_ref,
    bottom_ref,
    left_ref,
    right_ref,
    w1_ref,
    b1_ref,
    w2_ref,
    b2_ref,
    regrid_ref,
    next_ref,
    slots_ref,
    tall,
    hidden,
    sums,
):
    row = lax.rem(pl.program_id(0), 16)
    rows, channels, cols = x_ref.shape
    mask_at = 76
    b1, b2 = column(b1_ref[...]), column(b2_ref[...])

    def first_conv(j):
        field = jnp.concatenate([tall[j], tall[j + 1], tall[j + 2]], axis=0)
        taps = jnp.dot(w1_ref[...], field, preferred_element_type=F32)
        mask = tall[j + 1, mask_at : mask_at + 1, :].astype(F32)
        hidden[j] = (silu(shifted_sum(taps) + b1) * mask).astype(BF16)

    @pl.when(row == 0)
    def _():
        lat = lax.axis_index("lat")
        lane = lax.broadcasted_iota(jnp.int32, (channels, 128), 1)
        tall[2 : 2 + rows, :, 0:cols] = x_ref[...]
        for tile in range(3):
            both = jnp.where(lane % 4 < 2, left_ref[tile], right_ref[tile]).astype(F32)
            for k in range(rows):
                j = (tile - 1) * rows + k + 2
                if j < 0 or j >= rows + 4:
                    continue
                side = pltpu.roll(both, (126 - 4 * k) % 128, 1).astype(BF16)
                if tile != 1:
                    inside = lat > 0 if tile == 0 else lat < lat_count - 1
                    main = top_ref[j] if tile == 0 else bottom_ref[j - rows - 2]
                    tall[j, :, 0:cols] = jnp.where(inside, main, jnp.zeros_like(main))
                    side = jnp.where(inside, side, jnp.zeros_like(side))
                tall[j, :, cols:] = side
        first_conv(0)
        first_conv(1)

    first_conv(lax.rem(row + 2, 16))
    field = jnp.concatenate([hidden[row], hidden[row + 1], hidden[row + 2]], axis=0)
    taps = jnp.dot(w2_ref[...], field, preferred_element_type=F32)
    mask = tall[row + 2, mask_at : mask_at + 1, :].astype(F32)
    result = ((shifted_sum(taps) + b2) * mask).astype(BF16)[:, :cols]
    next_ref[0] = result
    blocks = regrid_ref.shape[0]
    for q in range(blocks):
        field = result[:, q * 128 : (q + 1) * 128]
        both = lax.dot_general(
            field, regrid_ref[q], (((1,), (1,)), ((), ())), preferred_element_type=F32
        ).astype(BF16)
        for k in range(2):
            what = meta[0, k * (rows * blocks) + row * blocks + q]
            at = what // 2
            value = both[:, k * 128 : (k + 1) * 128].astype(F32)
            sums[at] = jnp.where(lax.rem(what, 2) == 1, value, sums[at] + value)

    @pl.when(row == rows - 1)
    def _():
        groups, slots, size = slots_ref.shape[:3]

        def rounded(i, carry):
            for g in range(groups):
                slots_ref[g, i] = sums[i, g * size : (g + 1) * size].astype(BF16)
            return carry

        lax.fori_loop(0, slots, rounded, 0)


def ocean_step(meta, x, top, bottom, left, right, w1, b1, w2, b2, regrid, lat_count):
    rows, channels, cols = x.shape
    wide = cols + 128
    out = w2.shape[0] // 3
    slots = meta.shape[1]

    def whole(array):
        zeros = (0,) * array.ndim
        return pl.BlockSpec(array.shape, lambda r, meta: zeros)

    blocks = regrid.shape[0] // rows
    return pl.pallas_call(
        functools.partial(ocean_kernel, lat_count),
        out_shape=(
            jax.ShapeDtypeStruct((rows, out, cols), BF16),
            jax.ShapeDtypeStruct((GROUPS, slots, out // GROUPS, 128), BF16),
        ),
        grid_spec=pltpu.PrefetchScalarGridSpec(
            num_scalar_prefetch=1,
            grid=(rows,),
            in_specs=[whole(a) for a in (x, top, bottom, left, right, w1, b1, w2, b2)]
            + [pl.BlockSpec((blocks, 256, 128), lambda r, meta: (r, 0, 0))],
            out_specs=[
                pl.BlockSpec((1, out, cols), lambda r, meta: (r, 0, 0)),
                pl.BlockSpec((GROUPS, slots, out // GROUPS, 128), lambda r, meta: (0, 0, 0, 0)),
            ],
            scratch_shapes=[
                pltpu.VMEM((rows + 4, channels, wide), BF16),
                pltpu.VMEM((rows + 2, out, wide), BF16),
                pltpu.VMEM((slots, out, 128), F32),
            ],
        ),
        compiler_params=pltpu.CompilerParams(vmem_limit_bytes=VMEM_LIMIT),
        name="ocean",
    )(meta, x, top, bottom, left, right, w1, b1, w2, b2, regrid)


def couple_kernel(
    lat_count,
    lon_count,
    count,
    edge_count,
    own_index,
    north_index,
    south_index,
    slots,
    atmos,
    overflow,
    first,
    top,
    bottom,
    left,
    right,
    overflow_of_all,
    *scratch,
):
    lat, lon = lax.axis_index("lat"), lax.axis_index("lon")
    west = lax.rem(lon + lon_count - 1, lon_count)
    east = lax.rem(lon + 1, lon_count)
    across = lax.rem(lon + 2, lon_count)
    beside = lon + 1 - 2 * lax.rem(lon, 2)
    beside_across = lax.rem(beside + 2, lon_count)
    up, down, always = lat > 0, lat < lat_count - 1, lat >= 0
    edge = jnp.logical_or(lat == 0, lat == lat_count - 1)
    partners = [(lat, there, always) for there in (west, east, across)]
    for there, ok in ((lat - 1, up), (lat + 1, down)):
        partners += [(there, side, ok) for side in (west, lon, east)]
    four, inner = lat // 4, lax.rem(lat, 4)
    fours = lat_count // 4
    rounds = [
        [(lat, lax.rem(lon + k, lon_count)) for k in range(1, lon_count)],
        [(four * 4 + lax.rem(inner + k, 4), lon) for k in range(1, 4)],
        [(lax.rem(four + k, fours) * 4 + inner, lon) for k in range(1, fours)],
    ]
    partners += [(a, b, always) for peers in rounds[1:] for a, b in peers]
    greet(partners)

    groups, total, size, cols = slots.shape
    rows, channels = first.shape[:2]
    own, north, south = (scratch[i * groups : (i + 1) * groups] for i in range(3))
    away, mine, from_core, to_z, from_z, edges = scratch[3 * groups : 3 * groups + 6]
    load_sem, y_send, y_recv, core_send, core_recv, z_send, z_recv, halo_send, halo_recv = scratch[
        3 * groups + 6 : 3 * groups + 15
    ]
    gathered, partial, max_send, max_recv = scratch[3 * groups + 15 :]
    held, waiting, small = overflow, [], []

    def send_maximum(number):
        begin = sum(len(peers) for peers in rounds[:number])
        for i, (a, b) in enumerate(rounds[number], begin):
            small.append(remote(held, gathered.at[i], max_send.at[i], max_recv.at[i], a, b))
            small[-1].start()
            waiting.append(i)

    def receive_maximum(target):
        value = held[...]
        for i in waiting:
            landed(gathered.at[i], max_recv.at[i]).wait()
            value = jnp.maximum(value, gathered[i])
        waiting.clear()
        target[...] = value
        return target

    everything = pl.ds(0, total)
    loads = []
    for g in range(groups):
        loads.append(
            pltpu.make_async_copy(slots.at[g], own[g].at[everything], load_sem.at[g])
        )
        loads[g].start()
    for buffer in (own, north, south):
        for g in range(groups):
            buffer[g][total] = jnp.zeros((size, cols), BF16)
    greeted(jnp.where(edge, 6, 9) + sum(len(peers) for peers in rounds[1:]))
    send_maximum(0)

    last = lat_count - 1
    lists = []
    for g in range(groups):
        lists.append([])
        for length, sends_down, sends_up, north_comes, south_comes in (
            (count, lat > 0, lat < last, lat > 1, lat < last - 1),
            (edge_count, lat == 0, lat == last, lat == 1, lat == last - 1),
        ):
            low, high = pl.ds(0, length), pl.ds(total - length, length)
            lists[g] += [
                (
                    remote(
                        slots.at[g, high],
                        north[g].at[high],
                        y_send.at[0, g],
                        y_recv.at[0, g],
                        lat + 1,
                        lon,
                    ),
                    landed(north[g].at[high], y_recv.at[0, g]),
                    jnp.logical_and(down, sends_down),
                    jnp.logical_and(up, north_comes),
                ),
                (
                    remote(
                        slots.at[g, low],
                        south[g].at[low],
                        y_send.at[1, g],
                        y_recv.at[1, g],
                        lat - 1,
                        lon,
                    ),
                    landed(south[g].at[low], y_recv.at[1, g]),
                    jnp.logical_and(up, sends_up),
                    jnp.logical_and(down, south_comes),
                ),
            ]
        for copy, _, sends, _ in lists[g]:
            pl.when(sends)(copy.start)

    def dense(g, lon_there, store):
        def row(t, carry):
            at = lon_there * rows + t
            i, j = at // 128, lax.rem(at, 128)
            a = own_index[1, i, j]
            b = jnp.where(up, north_index[i, j], total)
            c = jnp.where(down, south_index[i, j], total)
            value = own[g][a].astype(F32) + north[g][b].astype(F32) + south[g][c].astype(F32)
            store(t, value.astype(BF16))
            return carry

        lax.fori_loop(0, rows, row, 0, unroll=8)

    core_copies, z_copies = [], []
    for g in range(groups):
        loads[g].wait()
        for _, arrival, _, comes in lists[g]:
            pl.when(comes)(arrival.wait)
        for part, (theirs, ours) in enumerate(((beside_across, across), (beside, lon))):

            def put_away(t, value):
                away[part, g, t] = value

            def put_mine(t, value):
                mine[part, g, t] = value

            dense(g, theirs, put_away)
            copy = remote(
                away.at[part, g],
                from_core.at[part, g],
                core_send.at[part, g],
                core_recv.at[part, g],
                lat,
                beside,
            )
            copy.start()
            core_copies.append(copy)
            dense(g, ours, put_mine)
            if part == 0:
                landed(from_core.at[0, g], core_recv.at[0, g]).wait()
                to_z[g] = (mine[0, g].astype(F32) + from_core[0, g].astype(F32)).astype(BF16)
                copy = remote(
                    to_z.at[g], from_z.at[g], z_send.at[g], z_recv.at[g], lat, across
                )
                copy.start()
                z_copies.append(copy)
        if g < 2:
            held = receive_maximum(partial.at[g])
            send_maximum(g + 1)

    lane = lax.broadcasted_iota(jnp.int32, (size, cols), 1)
    tiles = edges.shape[0]
    for g in range(groups):
        landed(from_core.at[1, g], core_recv.at[1, g]).wait()
        landed(from_z.at[g], z_recv.at[g]).wait()
        part = pl.ds(g * size, size)
        for tile in range(tiles):
            edge = jnp.zeros((size, cols), F32)
            for k in range(32):
                r = tile * 32 + k
                flux = (
                    mine[1, g, r].astype(F32)
                    + from_core[1, g, r].astype(F32)
                    + from_z[g, r].astype(F32)
                )
                v = (atmos[r, part].astype(F32) + flux).astype(BF16)
                first[r, part] = v
                rolled = pltpu.roll(v.astype(F32), (4 * k + 2) % cols, 1)
                edge = jnp.where(lane // 4 == k, rolled, edge)
            edges[tile, part] = edge.astype(BF16)
    lo, hi = edges.at[0], edges.at[tiles - 1]
    moves = [
        (edges, right.at[pl.ds(1, tiles)], lat, west, always, always),
        (edges, left.at[pl.ds(1, tiles)], lat, east, always, always),
        (first.at[pl.ds(0, 2)], bottom, lat - 1, lon, up, down),
        (first.at[pl.ds(rows - 2, 2)], top, lat + 1, lon, down, up),
        (lo, right.at[tiles + 1], lat - 1, west, up, down),
        (lo, left.at[tiles + 1], lat - 1, east, up, down),
        (hi, right.at[0], lat + 1, west, down, up),
        (hi, left.at[0], lat + 1, east, down, up),
    ]
    copies = [
        remote(src, dst, halo_send.at[i], halo_recv.at[i], a, b)
        for i, (src, dst, a, b, _, _) in enumerate(moves)
    ]
    for copy, move in zip(copies, moves):
        pl.when(move[4])(copy.start)
    receive_maximum(overflow_of_all)
    for copy in core_copies + z_copies + small:
        copy.wait_send()
    for g in range(groups):
        for copy, _, sends, _ in lists[g]:
            pl.when(sends)(copy.wait_send)
    for i, (copy, move) in enumerate(zip(copies, moves)):
        pl.when(move[4])(copy.wait_send)
        pl.when(move[5])(landed(move[1], halo_recv.at[i]).wait)


def couple(operands, count, edge_count, collective_id, lat_count, lon_count):
    _, _, _, slots, atmos, overflow = operands
    groups, total, size, cols = slots.shape
    rows, channels, cols = atmos.shape
    tiles = rows // 32
    vmem = pl.BlockSpec(memory_space=pltpu.VMEM)
    smem = pl.BlockSpec(memory_space=pltpu.SMEM)
    dma = pltpu.SemaphoreType.DMA
    shapes = [(rows, channels, cols)] + [(2, channels, cols)] * 2 + [(tiles + 2, channels, cols)] * 2
    received = pltpu.VMEM((total + 1, size, cols), BF16)
    peers = lon_count - 1 + 3 + lat_count // 4 - 1
    one = pltpu.VMEM((groups, rows, size, cols), BF16)
    two = pltpu.VMEM((2, groups, rows, size, cols), BF16)
    return pl.pallas_call(
        functools.partial(couple_kernel, lat_count, lon_count, count, edge_count),
        out_shape=[jax.ShapeDtypeStruct(s, BF16) for s in shapes]
        + [jax.ShapeDtypeStruct(overflow.shape, jnp.int32)],
        in_specs=[smem] * 3 + whole_any(1) + [vmem] * 2,
        out_specs=[vmem] + whole_any(4) + [vmem],
        scratch_shapes=[received] * (3 * groups)
        + [two] * 3
        + [one] * 2
        + [pltpu.VMEM((tiles, channels, cols), BF16)]
        + [dma((groups,))]
        + [dma((2, groups))] * 4
        + [dma((groups,))] * 2
        + [dma((8,))] * 2
        + [pltpu.VMEM((peers,) + overflow.shape, jnp.int32)]
        + [pltpu.VMEM((2,) + overflow.shape, jnp.int32)]
        + [dma((peers,))] * 2,
        compiler_params=pltpu.CompilerParams(
            collective_id=collective_id, has_side_effects=True, vmem_limit_bytes=VMEM_LIMIT
        ),
        name="couple",
    )(*operands)


def atmos_kernel(
    lat_count, a_ref, top_ref, bottom_ref, left_ref, right_ref, w1_ref, b1_ref, w2_ref, b2_ref, out_ref, tall, second
):
    count, channels, cols = a_ref.shape
    lat = lax.axis_index("lat")
    b1, b2 = column(b1_ref[...]), column(b2_ref[...])

    tall[2 : 2 + count, :, 0:cols] = a_ref[...]
    lane = lax.broadcasted_iota(jnp.int32, (channels, cols), 1)
    for tile in range(count // 32 + 2):
        side = jnp.where(lane % 4 < 2, left_ref[tile], right_ref[tile]).astype(F32)
        for k in range(32):
            r = tile * 32 - 32 + k
            if r < -2 or r >= count + 2:
                continue
            v = pltpu.roll(side, (126 - 4 * k) % cols, 1).astype(BF16)
            if r < 0 or r >= count:
                inside = lat > 0 if r < 0 else lat < lat_count - 1
                main = top_ref[r + 2] if r < 0 else bottom_ref[r - count]
                tall[r + 2, :, 0:cols] = jnp.where(inside, main, jnp.zeros_like(main))
                v = jnp.where(inside, v, jnp.zeros_like(v))
            tall[r + 2, :, cols:] = v

    def conv(source, weight, start, group):
        fields = [
            jnp.concatenate([source[start + i + d] for d in range(3)], axis=0)
            for i in range(group)
        ]
        return jnp.dot(weight, jnp.concatenate(fields, axis=1), preferred_element_type=F32)

    def first(step, carry):
        group = FIRST_ROWS
        start = step * group
        taps = conv(tall, w1_ref[...], start, group)
        for i in range(group):
            j = start + i
            value = silu(shifted_sum(taps[:, i * 2 * cols : (i + 1) * 2 * cols]) + b1)
            outside = jnp.logical_or(
                jnp.logical_and(j == 0, lat == 0),
                jnp.logical_and(j == count + 1, lat == lat_count - 1),
            )
            second[j] = jnp.where(outside, 0.0, value).astype(BF16)
        return carry

    lax.fori_loop(0, (count + 2) // FIRST_ROWS, first, 0)

    def last(step, carry):
        group = LAST_ROWS
        start = step * group
        taps = conv(second, w2_ref[...], start, group)
        rows = []
        for i in range(group):
            value = shifted_sum(taps[:, i * 2 * cols : (i + 1) * 2 * cols])[:, :cols]
            rows.append(a_ref[start + i].astype(F32) + (value + b2))
        block = jnp.swapaxes(jnp.stack(rows), 0, 1).astype(BF16)
        out_ref[:, pl.ds(pl.multiple_of(start, group), group), :] = block
        return carry

    lax.fori_loop(0, count // LAST_ROWS, last, 0)


def atmos_step(a, top, bottom, left, right, w1, b1, w2, b2, lat_count):
    count, channels, cols = a.shape
    vmem = pl.BlockSpec(memory_space=pltpu.VMEM)
    return pl.pallas_call(
        functools.partial(atmos_kernel, lat_count),
        out_shape=jax.ShapeDtypeStruct((channels, count, cols), BF16),
        in_specs=[vmem] * 9,
        out_specs=vmem,
        scratch_shapes=[
            pltpu.VMEM((count + 4, channels, 2 * cols), BF16),
            pltpu.VMEM((count + 2, channels, 2 * cols), BF16),
        ],
        compiler_params=pltpu.CompilerParams(vmem_limit_bytes=VMEM_LIMIT),
        name="atmos",
    )(a, top, bottom, left, right, w1, b1, w2, b2)


def per_device(
    ocean_state,
    sea_mask,
    ocean_w1,
    ocean_b1,
    ocean_w2,
    ocean_b2,
    regrid_weight,
    route_dev,
    route_row,
    atmos_state,
    atmos_w1,
    atmos_b1,
    atmos_w2,
    atmos_b2,
):
    lat_count, lon_count = lax.axis_size("lat"), lax.axis_size("lon")
    atmos_rows = atmos_state.shape[1]

    field = jnp.concatenate(
        [
            ocean_state,
            sea_mask.astype(BF16)[None],
            jnp.zeros((3,) + sea_mask.shape, BF16),
        ],
        axis=0,
    ).transpose(1, 0, 2)
    count = route_dev.size
    weights = (ocean_w1, ocean_w2, atmos_w1, atmos_w2)
    top, bottom, left, right, index, north_index, south_index, meta, overflow, *weights = ocean_halo(
        field, route_dev, route_row, weights, lat_count, lon_count, atmos_rows
    )
    ocean_next, slots = ocean_step(
        meta,
        field,
        top,
        bottom,
        left,
        right,
        weights[0],
        ocean_b1[None, :],
        weights[1],
        ocean_b2[None, :],
        regrid_weight.reshape(-1, 256, 128),
        lat_count,
    )
    operands = (index, north_index, south_index, slots, atmos_state.transpose(1, 0, 2), overflow)
    *coupled, overflow = couple(operands, SHORT, EDGE_SHORT, 1, lat_count, lon_count)
    first, top, bottom, left, right = lax.cond(
        overflow[0, 0] > 0,
        lambda short, operands: tuple(couple(operands, count, count, 2, lat_count, lon_count)[:5]),
        lambda short, operands: short,
        tuple(coupled),
        operands,
    )
    atmos_next = atmos_step(
        first,
        top,
        bottom,
        left,
        right,
        weights[2],
        atmos_b1[None, :],
        weights[3],
        atmos_b2[None, :],
        lat_count,
    )
    return ocean_next.transpose(1, 0, 2), atmos_next


def solution(mesh):
    in_specs = (
        P(None, "lat", "lon"),
        P("lat", "lon"),
        P(),
        P(),
        P(),
        P(),
        P(("lat", "lon"), None, None, None),
        P(("lat", "lon"), None),
        P(("lat", "lon"), None),
        P(None, "lat", "lon"),
        P(),
        P(),
        P(),
        P(),
    )
    out_specs = (P(None, "lat", "lon"), P(None, "lat", "lon"))
    return jax.shard_map(
        per_device, mesh=mesh, in_specs=in_specs, out_specs=out_specs, check_vma=False
    )
```

```python
import functools

import jax
import jax.numpy as jnp
from jax import lax
from jax.experimental import pallas as pl
from jax.experimental.pallas import tpu as pltpu
from jax.sharding import PartitionSpec as P

MESH = pl.DeviceIdType.MESH
F32 = jnp.float32
BF16 = jnp.bfloat16
VMEM_LIMIT = 56 * 1024 * 1024
GROUPS = 4
MASK_AT = 76
FIRST_ROWS = 11
LAST_ROWS = 16
SHORT = 32
EDGE_SHORT = 48


def silu(v):
    return 0.5 * v * (1.0 + jnp.tanh(0.5 * v))


def shifted_sum(taps):
    out = taps.shape[0] // 3
    columns = taps.shape[1]
    return (
        pltpu.roll(taps[0:out], 1, 1)
        + taps[out : 2 * out]
        + pltpu.roll(taps[2 * out :], columns - 1, 1)
    )


def stack_weight(weight_ref, out_ref):
    out, inn = weight_ref.shape[2:]
    padded = out_ref.shape[1] // 3
    for dc in range(3):
        pieces = []
        for dr in range(3):
            pieces.append(weight_ref[dr, dc].astype(F32))
            if padded > inn:
                pieces.append(jnp.zeros((out, padded - inn), F32))
        out_ref[dc * out : (dc + 1) * out, :] = jnp.concatenate(pieces, axis=1).astype(BF16)


def column(bias):
    n = bias.shape[1]
    at = lax.broadcasted_iota(jnp.int32, (n, n), 0) == lax.broadcasted_iota(jnp.int32, (n, n), 1)
    return jnp.sum(jnp.where(at, bias, jnp.zeros_like(bias)), axis=1, keepdims=True)


def remote(src, dst, send_sem, recv_sem, lat, lon):
    return pltpu.make_async_remote_copy(
        src_ref=src,
        dst_ref=dst,
        send_sem=send_sem,
        recv_sem=recv_sem,
        device_id={"lat": lat, "lon": lon},
        device_id_type=MESH,
    )


def landed(ref, sem):
    return pltpu.make_async_copy(ref, ref, sem)


def greet(partners):
    barrier = pltpu.get_barrier_semaphore()
    for lat, lon, ok in partners:

        @pl.when(ok)
        def _():
            pl.semaphore_signal(
                barrier, inc=1, device_id={"lat": lat, "lon": lon}, device_id_type=MESH
            )


def greeted(waits):
    pl.semaphore_wait(pltpu.get_barrier_semaphore(), waits)


def whole_any(count):
    return [pl.BlockSpec(memory_space=pl.ANY)] * count


def ocean_halo_kernel(
    lat_count,
    lon_count,
    atmos_rows,
    field,
    dev_ref,
    row_ref,
    w1_ref,
    w2_ref,
    w3_ref,
    w4_ref,
    b1_ref,
    hidden,
    index,
    north_index,
    south_index,
    meta,
    overflow,
    w2_out,
    w3_out,
    w4_out,
    top,
    bottom,
    left,
    right,
    edges,
    tall,
    w1_out,
    send_sem,
    recv_sem,
):
    lat, lon = lax.axis_index("lat"), lax.axis_index("lon")
    rows, channels, cols = field.shape
    west = lax.rem(lon + lon_count - 1, lon_count)
    east = lax.rem(lon + 1, lon_count)
    up, down, always = lat > 0, lat < lat_count - 1, lat >= 0
    edge = jnp.logical_or(lat == 0, lat == lat_count - 1)
    partners = [(lat, west, always), (lat, east, always)]
    for there, ok in ((lat - 1, up), (lat + 1, down)):
        partners += [(there, side, ok) for side in (west, lon, east)]
    greet(partners)

    keys = (dev_ref[...] - (lat - 1) * lon_count) * atmos_rows + row_ref[...]
    key = jnp.concatenate([keys[k : k + 1] for k in range(keys.shape[0])], axis=1)
    count = key.shape[1]
    key_down = column(key)
    blocks = keys.shape[1]
    across = lax.broadcasted_iota(jnp.int32, (count, count), 1)
    across = lax.rem(across, blocks) * keys.shape[0] + lax.div(across, blocks)
    along = lax.broadcasted_iota(jnp.int32, (count, count), 0)
    along = lax.rem(along, blocks) * keys.shape[0] + lax.div(along, blocks)
    place = jnp.sum((key_down < key).astype(jnp.int32), axis=0, keepdims=True)
    again = jnp.logical_and(key_down == key, along < across).astype(jnp.int32)
    meta[...] = place * 2 + 1 - jnp.max(again, axis=0, keepdims=True)
    place_down = column(place)
    per_step = lon_count * atmos_rows
    lane = lax.broadcasted_iota(jnp.int32, (1, count), 1)
    for step in range(3):
        for row in range(8):
            if row * count < per_step:
                number = lane + (step * per_step + row * count)
                places = jnp.min(
                    jnp.where(key_down == number, place_down, count), axis=0, keepdims=True
                )
                index[step, row : row + 1, :] = places
            else:
                index[step, row : row + 1, :] = jnp.full((1, count), count, jnp.int32)
    low = jnp.sum((key < per_step).astype(jnp.int32), axis=1, keepdims=True)
    high = jnp.sum((key >= 2 * per_step).astype(jnp.int32), axis=1, keepdims=True)
    most = jnp.where(edge, EDGE_SHORT, SHORT)
    long = (jnp.maximum(low, high) > most).astype(jnp.int32)
    overflow[...] = jnp.broadcast_to(long, overflow.shape)

    lane = lax.broadcasted_iota(jnp.int32, (channels, 128), 1)
    tile = jnp.zeros((channels, 128), F32)
    for k in range(rows):
        both = jnp.where(lane < 64, field[k, :, 0:128], field[k, :, cols - 128 :]).astype(F32)
        tile = jnp.where(lane // 4 == k, pltpu.roll(both, (4 * k + 2) % 128, 1), tile)
    edges[...] = tile.astype(BF16)

    stack_weight(w1_ref, w1_out)
    b1 = column(b1_ref[...])
    tall[2 : 2 + rows, :, 0:cols] = field[...]

    greeted(jnp.where(edge, 5, 8))
    moves = [
        (edges, right.at[1], lat, west, always, always),
        (edges, left.at[1], lat, east, always, always),
        (edges, right.at[2], lat - 1, west, up, down),
        (edges, left.at[2], lat - 1, east, up, down),
        (edges, right.at[0], lat + 1, west, down, up),
        (edges, left.at[0], lat + 1, east, down, up),
        (index.at[0], south_index, lat - 1, lon, up, down),
        (index.at[2], north_index, lat + 1, lon, down, up),
        (field.at[pl.ds(0, 2)], bottom, lat - 1, lon, up, down),
        (field.at[pl.ds(rows - 2, 2)], top, lat + 1, lon, down, up),
    ]
    copies = [
        remote(src, dst, send_sem.at[i], recv_sem.at[i], a, b)
        for i, (src, dst, a, b, _, _) in enumerate(moves)
    ]
    for copy, move in zip(copies, moves):
        pl.when(move[4])(copy.start)
    for weight, out in ((w2_ref, w2_out), (w3_ref, w3_out), (w4_ref, w4_out)):
        stack_weight(weight, out)

    def arrive(numbers):
        for i in numbers:
            pl.when(moves[i][5])(landed(moves[i][1], recv_sem.at[i]).wait)

    def sides(tile, some):
        both = jnp.where(lane % 4 < 2, left[tile], right[tile]).astype(F32)
        for k in some:
            side = pltpu.roll(both, (126 - 4 * k) % 128, 1).astype(BF16)
            if tile != 1:
                inside = lat > 0 if tile == 0 else lat < lat_count - 1
                side = jnp.where(inside, side, jnp.zeros_like(side))
            tall[(tile - 1) * rows + k + 2, :, cols:] = side

    def conv(start):
        for i in range(2):
            j = start + i
            fields = jnp.concatenate([tall[j], tall[j + 1], tall[j + 2]], axis=0)
            taps = jnp.dot(w1_out[...], fields, preferred_element_type=F32)
            mask = tall[j + 1, MASK_AT : MASK_AT + 1, :].astype(F32)
            hidden[j] = (silu(shifted_sum(taps) + b1) * mask).astype(BF16)

    def inner(step, carry):
        conv(2 * step + 2)
        return carry

    def outer(step, carry):
        conv(step * rows)
        return carry

    arrive((0, 1))
    sides(1, range(rows))
    lax.fori_loop(0, rows // 2 - 1, inner, 0)
    arrive(range(2, len(moves)))
    sides(0, range(rows - 2, rows))
    sides(2, range(2))
    for i in range(2):
        tall[i, :, 0:cols] = jnp.where(up, top[i], jnp.zeros_like(top[i]))
        tall[rows + 2 + i, :, 0:cols] = jnp.where(down, bottom[i], jnp.zeros_like(bottom[i]))
    lax.fori_loop(0, 2, outer, 0)
    for copy, move in zip(copies, moves):
        pl.when(move[4])(copy.wait_send)


def ocean_halo(field, route_dev, route_row, weights, b1, lat_count, lon_count, atmos_rows):
    rows, channels, cols = field.shape
    count = route_dev.size
    weights = [w.transpose(2, 3, 0, 1) for w in weights]
    stacked = [
        jax.ShapeDtypeStruct((3 * w.shape[2], 3 * (-(-w.shape[3] // 16) * 16)), BF16) for w in weights
    ]
    table = jax.ShapeDtypeStruct((8, count), jnp.int32)
    vmem = pl.BlockSpec(memory_space=pltpu.VMEM)
    out = weights[0].shape[2]
    return pl.pallas_call(
        functools.partial(ocean_halo_kernel, lat_count, lon_count, atmos_rows),
        out_shape=[
            jax.ShapeDtypeStruct((rows + 2, out, cols + 128), BF16),
            jax.ShapeDtypeStruct((3,) + table.shape, jnp.int32),
            table,
            table,
            jax.ShapeDtypeStruct((1, count), jnp.int32),
            table,
        ]
        + stacked[1:],
        in_specs=[vmem] * 8,
        out_specs=[vmem] * 2 + whole_any(2) + [vmem] * 5,
        scratch_shapes=[
            pltpu.VMEM((2, channels, cols), BF16),
            pltpu.VMEM((2, channels, cols), BF16),
            pltpu.VMEM((3, channels, 128), BF16),
            pltpu.VMEM((3, channels, 128), BF16),
            pltpu.VMEM((channels, 128), BF16),
            pltpu.VMEM((rows + 4, channels, cols + 128), BF16),
            pltpu.VMEM(stacked[0].shape, BF16),
            pltpu.SemaphoreType.DMA((10,)),
            pltpu.SemaphoreType.DMA((10,)),
        ],
        compiler_params=pltpu.CompilerParams(
            collective_id=0, has_side_effects=True, vmem_limit_bytes=VMEM_LIMIT
        ),
        name="ocean_halo",
    )(field, route_dev.T, route_row.T, *weights, b1)


def ocean_kernel(
    meta, hidden, mask_ref, w2_ref, b2_ref, regrid_ref, next_ref, slots_ref, sums, before, kept
):
    step = lax.rem(pl.program_id(0), 16)
    rows = next_ref.shape[1]
    cols = next_ref.shape[2]
    row = jnp.minimum(step, rows - 1)
    done = jnp.maximum(step - 1, 0)
    blocks = regrid_ref.shape[0]

    previous = before[...]
    values = []
    for q in range(blocks):
        both = lax.dot_general(
            previous[:, q * 128 : (q + 1) * 128],
            regrid_ref[q],
            (((1,), (1,)), ((), ())),
            preferred_element_type=F32,
        ).astype(BF16)
        values += [both[:, 0:128], both[:, 128:256]]

    field = jnp.concatenate([hidden[row], hidden[row + 1], hidden[row + 2]], axis=0)
    taps = jnp.dot(w2_ref[...], field, preferred_element_type=F32)
    mask = mask_ref[pl.ds(row, 1), :].astype(F32)
    result = (shifted_sum(taps)[:, :cols] + column(b2_ref[...])) * mask
    before[...] = result.astype(BF16)
    kept[row] = result

    for q in range(blocks):
        for k in range(2):
            what = meta[0, k * (rows * blocks) + done * blocks + q]
            at = what // 2
            value = values[2 * q + k].astype(F32)
            sums[at] = jnp.where(lax.rem(what, 2) == 1, value, sums[at] + value)

    @pl.when(step == rows)
    def _():
        groups, slots, size = slots_ref.shape[:3]

        def rounded(i, carry):
            for g in range(groups):
                slots_ref[g, i] = sums[i, g * size : (g + 1) * size].astype(BF16)
            return carry

        lax.fori_loop(0, slots, rounded, 0, unroll=4)
        for q in range(cols // 128):
            part = slice(q * 128, (q + 1) * 128)
            block = jnp.stack([kept[r, :, part] for r in range(rows)])
            next_ref[:, :, part] = jnp.swapaxes(block, 0, 1).astype(BF16)


def ocean_step(meta, hidden, mask, w2, b2, regrid):
    rows, cols = mask.shape
    out = w2.shape[0] // 3
    slots = meta.shape[1]

    def whole(array):
        zeros = (0,) * array.ndim
        return pl.BlockSpec(array.shape, lambda r, meta: zeros)

    blocks = regrid.shape[0] // rows
    return pl.pallas_call(
        ocean_kernel,
        out_shape=(
            jax.ShapeDtypeStruct((out, rows, cols), BF16),
            jax.ShapeDtypeStruct((GROUPS, slots, out // GROUPS, 128), BF16),
        ),
        grid_spec=pltpu.PrefetchScalarGridSpec(
            num_scalar_prefetch=1,
            grid=(rows + 1,),
            in_specs=[whole(a) for a in (hidden, mask, w2, b2)]
            + [pl.BlockSpec((blocks, 256, 128), lambda r, meta: (jnp.maximum(r - 1, 0), 0, 0))],
            out_specs=[
                pl.BlockSpec((out, rows, cols), lambda r, meta: (0, 0, 0)),
                pl.BlockSpec((GROUPS, slots, out // GROUPS, 128), lambda r, meta: (0, 0, 0, 0)),
            ],
            scratch_shapes=[
                pltpu.VMEM((slots, out, 128), F32),
                pltpu.VMEM((out, cols), BF16),
                pltpu.VMEM((rows, out, cols), F32),
            ],
        ),
        compiler_params=pltpu.CompilerParams(vmem_limit_bytes=VMEM_LIMIT),
        name="ocean",
    )(meta, hidden, mask, w2, b2, regrid)


def couple_kernel(
    lat_count,
    lon_count,
    count,
    edge_count,
    own_index,
    north_index,
    south_index,
    slots,
    atmos,
    overflow,
    first,
    top,
    bottom,
    left,
    right,
    overflow_of_all,
    *scratch,
):
    lat, lon = lax.axis_index("lat"), lax.axis_index("lon")
    west = lax.rem(lon + lon_count - 1, lon_count)
    east = lax.rem(lon + 1, lon_count)
    across = lax.rem(lon + 2, lon_count)
    beside = lon + 1 - 2 * lax.rem(lon, 2)
    beside_across = lax.rem(beside + 2, lon_count)
    up, down, always = lat > 0, lat < lat_count - 1, lat >= 0
    edge = jnp.logical_or(lat == 0, lat == lat_count - 1)
    partners = [(lat, there, always) for there in (west, east, across)]
    for there, ok in ((lat - 1, up), (lat + 1, down)):
        partners += [(there, side, ok) for side in (west, lon, east)]
    four, inner = lat // 4, lax.rem(lat, 4)
    fours = lat_count // 4
    rounds = [
        [(lat, lax.rem(lon + k, lon_count)) for k in range(1, lon_count)],
        [(four * 4 + lax.rem(inner + k, 4), lon) for k in range(1, 4)],
        [(lax.rem(four + k, fours) * 4 + inner, lon) for k in range(1, fours)],
    ]
    partners += [(a, b, always) for peers in rounds[1:] for a, b in peers]
    greet(partners)

    groups, total, size, cols = slots.shape
    rows, channels = first.shape[:2]
    own, north, south = (scratch[i * groups : (i + 1) * groups] for i in range(3))
    away, mine, from_core, to_z, from_z, edges = scratch[3 * groups : 3 * groups + 6]
    load_sem, y_send, y_recv, core_send, core_recv, z_send, z_recv, halo_send, halo_recv = scratch[
        3 * groups + 6 : 3 * groups + 15
    ]
    gathered, partial, max_send, max_recv = scratch[3 * groups + 15 :]
    held, waiting, small = overflow, [], []

    def send_maximum(number):
        begin = sum(len(peers) for peers in rounds[:number])
        for i, (a, b) in enumerate(rounds[number], begin):
            small.append(remote(held, gathered.at[i], max_send.at[i], max_recv.at[i], a, b))
            small[-1].start()
            waiting.append(i)

    def receive_maximum(target):
        value = held[...]
        for i in waiting:
            landed(gathered.at[i], max_recv.at[i]).wait()
            value = jnp.maximum(value, gathered[i])
        waiting.clear()
        target[...] = value
        return target

    everything = pl.ds(0, total)
    loads = []
    for g in range(groups):
        loads.append(
            pltpu.make_async_copy(slots.at[g], own[g].at[everything], load_sem.at[g])
        )
        loads[g].start()
    for buffer in (own, north, south):
        for g in range(groups):
            buffer[g][total] = jnp.zeros((size, cols), BF16)
    greeted(jnp.where(edge, 6, 9) + sum(len(peers) for peers in rounds[1:]))
    send_maximum(0)

    last = lat_count - 1
    lists = []
    for g in range(groups):
        lists.append([])
        for length, sends_down, sends_up, north_comes, south_comes in (
            (count, lat > 0, lat < last, lat > 1, lat < last - 1),
            (edge_count, lat == 0, lat == last, lat == 1, lat == last - 1),
        ):
            low, high = pl.ds(0, length), pl.ds(total - length, length)
            lists[g] += [
                (
                    remote(
                        slots.at[g, high],
                        north[g].at[high],
                        y_send.at[0, g],
                        y_recv.at[0, g],
                        lat + 1,
                        lon,
                    ),
                    landed(north[g].at[high], y_recv.at[0, g]),
                    jnp.logical_and(down, sends_down),
                    jnp.logical_and(up, north_comes),
                ),
                (
                    remote(
                        slots.at[g, low],
                        south[g].at[low],
                        y_send.at[1, g],
                        y_recv.at[1, g],
                        lat - 1,
                        lon,
                    ),
                    landed(south[g].at[low], y_recv.at[1, g]),
                    jnp.logical_and(up, sends_up),
                    jnp.logical_and(down, south_comes),
                ),
            ]
        for copy, _, sends, _ in lists[g]:
            pl.when(sends)(copy.start)

    def dense(g, lon_there, store):
        def row(t, carry):
            at = lon_there * rows + t
            i, j = at // 128, lax.rem(at, 128)
            a = own_index[1, i, j]
            b = jnp.where(up, north_index[i, j], total)
            c = jnp.where(down, south_index[i, j], total)
            value = own[g][a].astype(F32) + north[g][b].astype(F32) + south[g][c].astype(F32)
            store(t, value.astype(BF16))
            return carry

        lax.fori_loop(0, rows, row, 0, unroll=8)

    core_copies, z_copies = [], []
    for g in range(groups):
        loads[g].wait()
        for _, arrival, _, comes in lists[g]:
            pl.when(comes)(arrival.wait)
        for part, (theirs, ours) in enumerate(((beside_across, across), (beside, lon))):

            def put_away(t, value):
                away[part, g, t] = value

            def put_mine(t, value):
                mine[part, g, t] = value

            dense(g, theirs, put_away)
            copy = remote(
                away.at[part, g],
                from_core.at[part, g],
                core_send.at[part, g],
                core_recv.at[part, g],
                lat,
                beside,
            )
            copy.start()
            core_copies.append(copy)
            dense(g, ours, put_mine)
            if part == 0:
                landed(from_core.at[0, g], core_recv.at[0, g]).wait()
                to_z[g] = (mine[0, g].astype(F32) + from_core[0, g].astype(F32)).astype(BF16)
                copy = remote(
                    to_z.at[g], from_z.at[g], z_send.at[g], z_recv.at[g], lat, across
                )
                copy.start()
                z_copies.append(copy)
        if g < 2:
            held = receive_maximum(partial.at[g])
            send_maximum(g + 1)

    lane = lax.broadcasted_iota(jnp.int32, (size, cols), 1)
    tiles = edges.shape[0]
    for g in range(groups):
        landed(from_core.at[1, g], core_recv.at[1, g]).wait()
        landed(from_z.at[g], z_recv.at[g]).wait()
        part = pl.ds(g * size, size)
        for tile in range(tiles):
            edge = jnp.zeros((size, cols), F32)
            for k in range(32):
                r = tile * 32 + k
                flux = (
                    mine[1, g, r].astype(F32)
                    + from_core[1, g, r].astype(F32)
                    + from_z[g, r].astype(F32)
                )
                v = (atmos[r, part].astype(F32) + flux).astype(BF16)
                first[r, part] = v
                rolled = pltpu.roll(v.astype(F32), (4 * k + 2) % cols, 1)
                edge = jnp.where(lane // 4 == k, rolled, edge)
            edges[tile, part] = edge.astype(BF16)
    lo, hi = edges.at[0], edges.at[tiles - 1]
    moves = [
        (edges, right.at[pl.ds(1, tiles)], lat, west, always, always),
        (edges, left.at[pl.ds(1, tiles)], lat, east, always, always),
        (first.at[pl.ds(0, 2)], bottom, lat - 1, lon, up, down),
        (first.at[pl.ds(rows - 2, 2)], top, lat + 1, lon, down, up),
        (lo, right.at[tiles + 1], lat - 1, west, up, down),
        (lo, left.at[tiles + 1], lat - 1, east, up, down),
        (hi, right.at[0], lat + 1, west, down, up),
        (hi, left.at[0], lat + 1, east, down, up),
    ]
    copies = [
        remote(src, dst, halo_send.at[i], halo_recv.at[i], a, b)
        for i, (src, dst, a, b, _, _) in enumerate(moves)
    ]
    for copy, move in zip(copies, moves):
        pl.when(move[4])(copy.start)
    receive_maximum(overflow_of_all)
    for copy in core_copies + z_copies + small:
        copy.wait_send()
    for g in range(groups):
        for copy, _, sends, _ in lists[g]:
            pl.when(sends)(copy.wait_send)
    for i, (copy, move) in enumerate(zip(copies, moves)):
        pl.when(move[4])(copy.wait_send)
        pl.when(move[5])(landed(move[1], halo_recv.at[i]).wait)


def couple(operands, count, edge_count, collective_id, lat_count, lon_count):
    _, _, _, slots, atmos, overflow = operands
    groups, total, size, cols = slots.shape
    rows, channels, cols = atmos.shape
    tiles = rows // 32
    vmem = pl.BlockSpec(memory_space=pltpu.VMEM)
    smem = pl.BlockSpec(memory_space=pltpu.SMEM)
    dma = pltpu.SemaphoreType.DMA
    shapes = [(rows, channels, cols)] + [(2, channels, cols)] * 2 + [(tiles + 2, channels, cols)] * 2
    received = pltpu.VMEM((total + 1, size, cols), BF16)
    peers = lon_count - 1 + 3 + lat_count // 4 - 1
    one = pltpu.VMEM((groups, rows, size, cols), BF16)
    two = pltpu.VMEM((2, groups, rows, size, cols), BF16)
    return pl.pallas_call(
        functools.partial(couple_kernel, lat_count, lon_count, count, edge_count),
        out_shape=[jax.ShapeDtypeStruct(s, BF16) for s in shapes]
        + [jax.ShapeDtypeStruct(overflow.shape, jnp.int32)],
        in_specs=[smem] * 3 + whole_any(1) + [vmem] * 2,
        out_specs=[vmem] + whole_any(4) + [vmem],
        scratch_shapes=[received] * (3 * groups)
        + [two] * 3
        + [one] * 2
        + [pltpu.VMEM((tiles, channels, cols), BF16)]
        + [dma((groups,))]
        + [dma((2, groups))] * 4
        + [dma((groups,))] * 2
        + [dma((8,))] * 2
        + [pltpu.VMEM((peers,) + overflow.shape, jnp.int32)]
        + [pltpu.VMEM((2,) + overflow.shape, jnp.int32)]
        + [dma((peers,))] * 2,
        compiler_params=pltpu.CompilerParams(
            collective_id=collective_id, has_side_effects=True, vmem_limit_bytes=VMEM_LIMIT
        ),
        name="couple",
    )(*operands)


def atmos_kernel(
    lat_count, a_ref, top_ref, bottom_ref, left_ref, right_ref, w1_ref, b1_ref, w2_ref, b2_ref, out_ref, tall, second
):
    count, channels, cols = a_ref.shape
    lat = lax.axis_index("lat")
    b1, b2 = column(b1_ref[...]), column(b2_ref[...])

    tall[2 : 2 + count, :, 0:cols] = a_ref[...]
    lane = lax.broadcasted_iota(jnp.int32, (channels, cols), 1)
    for tile in range(count // 32 + 2):
        side = jnp.where(lane % 4 < 2, left_ref[tile], right_ref[tile]).astype(F32)
        for k in range(32):
            r = tile * 32 - 32 + k
            if r < -2 or r >= count + 2:
                continue
            v = pltpu.roll(side, (126 - 4 * k) % cols, 1).astype(BF16)
            if r < 0 or r >= count:
                inside = lat > 0 if r < 0 else lat < lat_count - 1
                main = top_ref[r + 2] if r < 0 else bottom_ref[r - count]
                tall[r + 2, :, 0:cols] = jnp.where(inside, main, jnp.zeros_like(main))
                v = jnp.where(inside, v, jnp.zeros_like(v))
            tall[r + 2, :, cols:] = v

    def conv(source, weight, start, group):
        fields = [
            jnp.concatenate([source[start + i + d] for d in range(3)], axis=0)
            for i in range(group)
        ]
        return jnp.dot(weight, jnp.concatenate(fields, axis=1), preferred_element_type=F32)

    def first(step, carry):
        group = FIRST_ROWS
        start = step * group
        taps = conv(tall, w1_ref[...], start, group)
        for i in range(group):
            j = start + i
            value = silu(shifted_sum(taps[:, i * 2 * cols : (i + 1) * 2 * cols]) + b1)
            outside = jnp.logical_or(
                jnp.logical_and(j == 0, lat == 0),
                jnp.logical_and(j == count + 1, lat == lat_count - 1),
            )
            second[j] = jnp.where(outside, 0.0, value).astype(BF16)
        return carry

    lax.fori_loop(0, (count + 2) // FIRST_ROWS, first, 0)

    def last(step, carry):
        group = LAST_ROWS
        start = step * group
        taps = conv(second, w2_ref[...], start, group)
        rows = []
        for i in range(group):
            value = shifted_sum(taps[:, i * 2 * cols : (i + 1) * 2 * cols])[:, :cols]
            rows.append(a_ref[start + i].astype(F32) + (value + b2))
        block = jnp.swapaxes(jnp.stack(rows), 0, 1).astype(BF16)
        out_ref[:, pl.ds(pl.multiple_of(start, group), group), :] = block
        return carry

    lax.fori_loop(0, count // LAST_ROWS, last, 0)


def atmos_step(a, top, bottom, left, right, w1, b1, w2, b2, lat_count):
    count, channels, cols = a.shape
    vmem = pl.BlockSpec(memory_space=pltpu.VMEM)
    return pl.pallas_call(
        functools.partial(atmos_kernel, lat_count),
        out_shape=jax.ShapeDtypeStruct((channels, count, cols), BF16),
        in_specs=[vmem] * 9,
        out_specs=vmem,
        scratch_shapes=[
            pltpu.VMEM((count + 4, channels, 2 * cols), BF16),
            pltpu.VMEM((count + 2, channels, 2 * cols), BF16),
        ],
        compiler_params=pltpu.CompilerParams(vmem_limit_bytes=VMEM_LIMIT),
        name="atmos",
    )(a, top, bottom, left, right, w1, b1, w2, b2)


def per_device(
    ocean_state,
    sea_mask,
    ocean_w1,
    ocean_b1,
    ocean_w2,
    ocean_b2,
    regrid_weight,
    route_dev,
    route_row,
    atmos_state,
    atmos_w1,
    atmos_b1,
    atmos_w2,
    atmos_b2,
):
    lat_count, lon_count = lax.axis_size("lat"), lax.axis_size("lon")
    atmos_rows = atmos_state.shape[1]

    field = jnp.concatenate(
        [
            ocean_state,
            sea_mask.astype(BF16)[None],
            jnp.zeros((3,) + sea_mask.shape, BF16),
        ],
        axis=0,
    ).transpose(1, 0, 2)
    count = route_dev.size
    weights = (ocean_w1, ocean_w2, atmos_w1, atmos_w2)
    hidden, index, north_index, south_index, meta, overflow, *weights = ocean_halo(
        field, route_dev, route_row, weights, ocean_b1[None, :], lat_count, lon_count, atmos_rows
    )
    ocean_next, slots = ocean_step(
        meta,
        hidden,
        sea_mask,
        weights[0],
        ocean_b2[None, :],
        regrid_weight.reshape(-1, 256, 128),
    )
    operands = (index, north_index, south_index, slots, atmos_state.transpose(1, 0, 2), overflow)
    *coupled, overflow = couple(operands, SHORT, EDGE_SHORT, 1, lat_count, lon_count)
    first, top, bottom, left, right = lax.cond(
        overflow[0, 0] > 0,
        lambda short, operands: tuple(couple(operands, count, count, 2, lat_count, lon_count)[:5]),
        lambda short, operands: short,
        tuple(coupled),
        operands,
    )
    atmos_next = atmos_step(
        first,
        top,
        bottom,
        left,
        right,
        weights[1],
        atmos_b1[None, :],
        weights[2],
        atmos_b2[None, :],
        lat_count,
    )
    return ocean_next, atmos_next


def solution(mesh):
    in_specs = (
        P(None, "lat", "lon"),
        P("lat", "lon"),
        P(),
        P(),
        P(),
        P(),
        P(("lat", "lon"), None, None, None),
        P(("lat", "lon"), None),
        P(("lat", "lon"), None),
        P(None, "lat", "lon"),
        P(),
        P(),
        P(),
        P(),
    )
    out_specs = (P(None, "lat", "lon"), P(None, "lat", "lon"))
    return jax.shard_map(
        per_device, mesh=mesh, in_specs=in_specs, out_specs=out_specs, check_vma=False
    )
```

```python
import functools

import jax
import jax.numpy as jnp
from jax import lax
from jax.experimental import pallas as pl
from jax.experimental.pallas import tpu as pltpu
from jax.sharding import PartitionSpec as P

MESH = pl.DeviceIdType.MESH
F32 = jnp.float32
BF16 = jnp.bfloat16
VMEM_LIMIT = 56 * 1024 * 1024
GROUPS = 4
FIRST_ROWS = 11
LAST_ROWS = 16
SHORT = 32
EDGE_SHORT = 48


def silu(v):
    return 0.5 * v * (1.0 + jnp.tanh(0.5 * v))


def shifted_sum(taps):
    out = taps.shape[0] // 3
    columns = taps.shape[1]
    return (
        pltpu.roll(taps[0:out], 1, 1)
        + taps[out : 2 * out]
        + pltpu.roll(taps[2 * out :], columns - 1, 1)
    )


def stack_weight(weight_ref, out_ref):
    out, inn = weight_ref.shape[2:]
    padded = out_ref.shape[1] // 3
    for dc in range(3):
        pieces = []
        for dr in range(3):
            pieces.append(weight_ref[dr, dc].astype(F32))
            if padded > inn:
                pieces.append(jnp.zeros((out, padded - inn), F32))
        out_ref[dc * out : (dc + 1) * out, :] = jnp.concatenate(pieces, axis=1).astype(BF16)


def column(bias):
    n = bias.shape[1]
    at = lax.broadcasted_iota(jnp.int32, (n, n), 0) == lax.broadcasted_iota(jnp.int32, (n, n), 1)
    return jnp.sum(jnp.where(at, bias, jnp.zeros_like(bias)), axis=1, keepdims=True)


def remote(src, dst, send_sem, recv_sem, lat, lon):
    return pltpu.make_async_remote_copy(
        src_ref=src,
        dst_ref=dst,
        send_sem=send_sem,
        recv_sem=recv_sem,
        device_id={"lat": lat, "lon": lon},
        device_id_type=MESH,
    )


def landed(ref, sem):
    return pltpu.make_async_copy(ref, ref, sem)


def greet(partners):
    barrier = pltpu.get_barrier_semaphore()
    for lat, lon, ok in partners:

        @pl.when(ok)
        def _():
            pl.semaphore_signal(
                barrier, inc=1, device_id={"lat": lat, "lon": lon}, device_id_type=MESH
            )


def greeted(waits):
    pl.semaphore_wait(pltpu.get_barrier_semaphore(), waits)


def whole_any(count):
    return [pl.BlockSpec(memory_space=pl.ANY)] * count


def ocean_halo_kernel(
    lat_count,
    lon_count,
    atmos_rows,
    x_ref,
    mask_ref,
    dev_ref,
    row_ref,
    w1_ref,
    w2_ref,
    w3_ref,
    w4_ref,
    b1_ref,
    hidden,
    index,
    north_index,
    south_index,
    meta,
    overflow,
    w2_out,
    w3_out,
    w4_out,
    left,
    right,
    edges,
    tall,
    w1_out,
    send_sem,
    recv_sem,
):
    lat, lon = lax.axis_index("lat"), lax.axis_index("lon")
    rows, inputs, cols = x_ref.shape
    channels = tall.shape[1]
    west = lax.rem(lon + lon_count - 1, lon_count)
    east = lax.rem(lon + 1, lon_count)
    up, down, always = lat > 0, lat < lat_count - 1, lat >= 0
    edge = jnp.logical_or(lat == 0, lat == lat_count - 1)
    partners = [(lat, west, always), (lat, east, always)]
    for there, ok in ((lat - 1, up), (lat + 1, down)):
        partners += [(there, side, ok) for side in (west, lon, east)]
    greet(partners)

    keys = (dev_ref[...] - (lat - 1) * lon_count) * atmos_rows + row_ref[...]
    key = jnp.concatenate([keys[k : k + 1] for k in range(keys.shape[0])], axis=1)
    count = key.shape[1]
    key_down = column(key)
    blocks = keys.shape[1]
    across = lax.broadcasted_iota(jnp.int32, (count, count), 1)
    across = lax.rem(across, blocks) * keys.shape[0] + lax.div(across, blocks)
    along = lax.broadcasted_iota(jnp.int32, (count, count), 0)
    along = lax.rem(along, blocks) * keys.shape[0] + lax.div(along, blocks)
    again = jnp.logical_and(key_down == key, along < across).astype(jnp.int32)
    place = jnp.sum((key_down < key).astype(jnp.int32) + again, axis=0, keepdims=True)
    place_down = column(place)
    first_down = column(1 - jnp.max(again, axis=0, keepdims=True))
    lane = lax.broadcasted_iota(jnp.int32, (1, count), 1)
    meta[0:1, :] = place
    meta[1:2, :] = jnp.max(jnp.where(place_down == lane, first_down, 0), axis=0, keepdims=True)
    per_step = lon_count * atmos_rows
    for step in range(3):
        for row in range(8):
            if row * count < per_step:
                number = lane + (step * per_step + row * count)
                places = jnp.max(
                    jnp.where(key_down == number, place_down, -1), axis=0, keepdims=True
                )
                index[step, row : row + 1, :] = jnp.where(places < 0, count, places)
            else:
                index[step, row : row + 1, :] = jnp.full((1, count), count, jnp.int32)
    low = jnp.sum((key < per_step).astype(jnp.int32), axis=1, keepdims=True)
    high = jnp.sum((key >= 2 * per_step).astype(jnp.int32), axis=1, keepdims=True)
    most = jnp.where(edge, EDGE_SHORT, SHORT)
    long = (jnp.maximum(low, high) > most).astype(jnp.int32)
    overflow[...] = jnp.broadcast_to(long, overflow.shape)

    lane = lax.broadcasted_iota(jnp.int32, (channels, 128), 1)
    extra = lax.broadcasted_iota(jnp.int32, (channels - inputs, cols), 0)
    for k in range(rows):
        tall[k + 2, 0:inputs, 0:cols] = x_ref[k]
        mask = jnp.where(extra == 0, mask_ref[k : k + 1, :], 0).astype(F32).astype(BF16)
        tall[k + 2, inputs:, 0:cols] = mask
    tile = jnp.zeros((channels, 128), F32)
    for k in range(rows):
        low, high = tall[k + 2, :, 0:128], tall[k + 2, :, cols - 128 : cols]
        both = jnp.where(lane < 64, low, high).astype(F32)
        tile = jnp.where(lane // 4 == k, pltpu.roll(both, (4 * k + 2) % 128, 1), tile)
    edges[...] = tile.astype(BF16)

    stack_weight(w1_ref, w1_out)
    b1 = column(b1_ref[...])
    blank = jnp.zeros((2, channels, cols), BF16)

    @pl.when(jnp.logical_not(up))
    def _():
        tall[0:2, :, 0:cols] = blank

    @pl.when(jnp.logical_not(down))
    def _():
        tall[rows + 2 :, :, 0:cols] = blank

    greeted(jnp.where(edge, 5, 8))
    def two(start):
        return tall.at[pl.ds(start, 2), :, pl.ds(0, cols)]

    moves = [
        (edges, right.at[1], lat, west, always, always),
        (edges, left.at[1], lat, east, always, always),
        (edges, right.at[2], lat - 1, west, up, down),
        (edges, left.at[2], lat - 1, east, up, down),
        (edges, right.at[0], lat + 1, west, down, up),
        (edges, left.at[0], lat + 1, east, down, up),
        (index.at[0], south_index, lat - 1, lon, up, down),
        (index.at[2], north_index, lat + 1, lon, down, up),
        (two(2), two(rows + 2), lat - 1, lon, up, down),
        (two(rows), two(0), lat + 1, lon, down, up),
    ]
    copies = [
        remote(src, dst, send_sem.at[i], recv_sem.at[i], a, b)
        for i, (src, dst, a, b, _, _) in enumerate(moves)
    ]
    for copy, move in zip(copies, moves):
        pl.when(move[4])(copy.start)
    for weight, out in ((w2_ref, w2_out), (w3_ref, w3_out), (w4_ref, w4_out)):
        stack_weight(weight, out)

    def arrive(numbers):
        for i in numbers:
            pl.when(moves[i][5])(landed(moves[i][1], recv_sem.at[i]).wait)

    def sides(tile, some):
        both = jnp.where(lane % 4 < 2, left[tile], right[tile]).astype(F32)
        for k in some:
            side = pltpu.roll(both, (126 - 4 * k) % 128, 1).astype(BF16)
            if tile != 1:
                inside = lat > 0 if tile == 0 else lat < lat_count - 1
                side = jnp.where(inside, side, jnp.zeros_like(side))
            tall[(tile - 1) * rows + k + 2, :, cols:] = side

    def conv(start):
        for i in range(2):
            j = start + i
            fields = jnp.concatenate([tall[j], tall[j + 1], tall[j + 2]], axis=0)
            taps = jnp.dot(w1_out[...], fields, preferred_element_type=F32)
            mask = tall[j + 1, inputs : inputs + 1, :].astype(F32)
            hidden[j] = (silu(shifted_sum(taps) + b1) * mask).astype(BF16)

    def inner(step, carry):
        conv(2 * step + 2)
        return carry

    def outer(step, carry):
        conv(step * rows)
        return carry

    arrive((0, 1))
    sides(1, range(rows))
    lax.fori_loop(0, rows // 2 - 1, inner, 0)
    arrive(range(2, len(moves)))
    sides(0, range(rows - 2, rows))
    sides(2, range(2))
    lax.fori_loop(0, 2, outer, 0)
    for copy, move in zip(copies, moves):
        pl.when(move[4])(copy.wait_send)


def ocean_halo(x, sea_mask, route_dev, route_row, weights, b1, lat_count, lon_count, atmos_rows):
    rows, inputs, cols = x.shape
    channels = -(-(inputs + 1) // 16) * 16
    count = route_dev.size
    weights = [w.transpose(2, 3, 0, 1) for w in weights]
    stacked = [
        jax.ShapeDtypeStruct((3 * w.shape[2], 3 * (-(-w.shape[3] // 16) * 16)), BF16) for w in weights
    ]
    table = jax.ShapeDtypeStruct((8, count), jnp.int32)
    vmem = pl.BlockSpec(memory_space=pltpu.VMEM)
    out = weights[0].shape[2]
    return pl.pallas_call(
        functools.partial(ocean_halo_kernel, lat_count, lon_count, atmos_rows),
        out_shape=[
            jax.ShapeDtypeStruct((rows + 2, out, cols + 128), BF16),
            jax.ShapeDtypeStruct((3,) + table.shape, jnp.int32),
            table,
            table,
            jax.ShapeDtypeStruct((2, count), jnp.int32),
            table,
        ]
        + stacked[1:],
        in_specs=[vmem] * 9,
        out_specs=[vmem] * 2 + whole_any(2) + [vmem] * 5,
        scratch_shapes=[
            pltpu.VMEM((3, channels, 128), BF16),
            pltpu.VMEM((3, channels, 128), BF16),
            pltpu.VMEM((channels, 128), BF16),
            pltpu.VMEM((rows + 4, channels, cols + 128), BF16),
            pltpu.VMEM(stacked[0].shape, BF16),
            pltpu.SemaphoreType.DMA((10,)),
            pltpu.SemaphoreType.DMA((10,)),
        ],
        compiler_params=pltpu.CompilerParams(
            collective_id=0, has_side_effects=True, vmem_limit_bytes=VMEM_LIMIT
        ),
        name="ocean_halo",
    )(x, sea_mask, route_dev.T, route_row.T, *weights, b1)


def ocean_kernel(
    meta, hidden, mask_ref, w2_ref, b2_ref, regrid_ref, next_ref, slots_ref, listed, before, kept
):
    step = lax.rem(pl.program_id(0), 16)
    rows = next_ref.shape[1]
    cols = next_ref.shape[2]
    row = jnp.minimum(step, rows - 1)
    done = jnp.maximum(step - 1, 0)
    blocks = regrid_ref.shape[0]

    previous = before[...]
    values = []
    for q in range(blocks):
        both = lax.dot_general(
            previous[:, q * 128 : (q + 1) * 128],
            regrid_ref[q],
            (((1,), (1,)), ((), ())),
            preferred_element_type=F32,
        ).astype(BF16)
        values += [both[:, 0:128], both[:, 128:256]]

    field = jnp.concatenate([hidden[row], hidden[row + 1], hidden[row + 2]], axis=0)
    taps = jnp.dot(w2_ref[...], field, preferred_element_type=F32)
    mask = mask_ref[pl.ds(row, 1), :].astype(F32)
    result = (shifted_sum(taps)[:, :cols] + column(b2_ref[...])) * mask
    before[...] = result.astype(BF16)
    kept[row] = result

    for q in range(blocks):
        for k in range(2):
            place = meta[0, k * (rows * blocks) + done * blocks + q]
            listed[place] = values[2 * q + k]

    @pl.when(step == rows)
    def _():
        groups, slots, size = slots_ref.shape[:3]

        def add(i, run):
            value = listed[i].astype(F32)
            run = jnp.where(meta[1, i] == 1, value, run + value)
            for g in range(groups):
                slots_ref[g, i] = run[g * size : (g + 1) * size].astype(BF16)
            return run

        lax.fori_loop(0, slots, add, jnp.zeros(listed.shape[1:], F32), unroll=4)
        for q in range(cols // 128):
            part = slice(q * 128, (q + 1) * 128)
            block = jnp.stack([kept[r, :, part] for r in range(rows)])
            next_ref[:, :, part] = jnp.swapaxes(block, 0, 1).astype(BF16)


def ocean_step(meta, hidden, mask, w2, b2, regrid):
    rows, cols = mask.shape
    out = w2.shape[0] // 3
    slots = meta.shape[1]

    def whole(array):
        zeros = (0,) * array.ndim
        return pl.BlockSpec(array.shape, lambda r, meta: zeros)

    blocks = regrid.shape[0] // rows
    return pl.pallas_call(
        ocean_kernel,
        out_shape=(
            jax.ShapeDtypeStruct((out, rows, cols), BF16),
            jax.ShapeDtypeStruct((GROUPS, slots, out // GROUPS, 128), BF16),
        ),
        grid_spec=pltpu.PrefetchScalarGridSpec(
            num_scalar_prefetch=1,
            grid=(rows + 1,),
            in_specs=[whole(a) for a in (hidden, mask, w2, b2)]
            + [pl.BlockSpec((blocks, 256, 128), lambda r, meta: (jnp.maximum(r - 1, 0), 0, 0))],
            out_specs=[
                pl.BlockSpec((out, rows, cols), lambda r, meta: (0, 0, 0)),
                pl.BlockSpec((GROUPS, slots, out // GROUPS, 128), lambda r, meta: (0, 0, 0, 0)),
            ],
            scratch_shapes=[
                pltpu.VMEM((slots, out, 128), BF16),
                pltpu.VMEM((out, cols), BF16),
                pltpu.VMEM((rows, out, cols), F32),
            ],
        ),
        compiler_params=pltpu.CompilerParams(vmem_limit_bytes=VMEM_LIMIT),
        name="ocean",
    )(meta, hidden, mask, w2, b2, regrid)


def couple_kernel(
    lat_count,
    lon_count,
    count,
    edge_count,
    own_index,
    north_index,
    south_index,
    slots,
    atmos,
    overflow,
    first,
    top,
    bottom,
    left,
    right,
    overflow_of_all,
    *scratch,
):
    lat, lon = lax.axis_index("lat"), lax.axis_index("lon")
    west = lax.rem(lon + lon_count - 1, lon_count)
    east = lax.rem(lon + 1, lon_count)
    across = lax.rem(lon + 2, lon_count)
    beside = lon + 1 - 2 * lax.rem(lon, 2)
    beside_across = lax.rem(beside + 2, lon_count)
    up, down, always = lat > 0, lat < lat_count - 1, lat >= 0
    edge = jnp.logical_or(lat == 0, lat == lat_count - 1)
    partners = [(lat, there, always) for there in (west, east, across)]
    for there, ok in ((lat - 1, up), (lat + 1, down)):
        partners += [(there, side, ok) for side in (west, lon, east)]
    four, inner = lat // 4, lax.rem(lat, 4)
    fours = lat_count // 4
    rounds = [
        [(lat, lax.rem(lon + k, lon_count)) for k in range(1, lon_count)],
        [(four * 4 + lax.rem(inner + k, 4), lon) for k in range(1, 4)],
        [(lax.rem(four + k, fours) * 4 + inner, lon) for k in range(1, fours)],
    ]
    partners += [(a, b, always) for peers in rounds[1:] for a, b in peers]
    greet(partners)

    groups, total, size, cols = slots.shape
    rows, channels = first.shape[:2]
    own, north, south = (scratch[i * groups : (i + 1) * groups] for i in range(3))
    away, mine, from_core, to_z, from_z, edges = scratch[3 * groups : 3 * groups + 6]
    load_sem, y_send, y_recv, core_send, core_recv, z_send, z_recv, halo_send, halo_recv = scratch[
        3 * groups + 6 : 3 * groups + 15
    ]
    gathered, partial, max_send, max_recv = scratch[3 * groups + 15 :]
    held, waiting, small = overflow, [], []

    def send_maximum(number):
        begin = sum(len(peers) for peers in rounds[:number])
        for i, (a, b) in enumerate(rounds[number], begin):
            small.append(remote(held, gathered.at[i], max_send.at[i], max_recv.at[i], a, b))
            small[-1].start()
            waiting.append(i)

    def receive_maximum(target):
        value = held[...]
        for i in waiting:
            landed(gathered.at[i], max_recv.at[i]).wait()
            value = jnp.maximum(value, gathered[i])
        waiting.clear()
        if target is None:
            overflow_of_all[0] = jnp.max(value)
        else:
            target[...] = value
        return target

    everything = pl.ds(0, total)
    loads = []
    for g in range(groups):
        loads.append(
            pltpu.make_async_copy(slots.at[g], own[g].at[everything], load_sem.at[g])
        )
        loads[g].start()
    for buffer in (own, north, south):
        for g in range(groups):
            buffer[g][total] = jnp.zeros((size, cols), BF16)
    greeted(jnp.where(edge, 6, 9) + sum(len(peers) for peers in rounds[1:]))
    send_maximum(0)

    last = lat_count - 1
    lists = []
    for g in range(groups):
        lists.append([])
        for length, sends_down, sends_up, north_comes, south_comes in (
            (count, lat > 0, lat < last, lat > 1, lat < last - 1),
            (edge_count, lat == 0, lat == last, lat == 1, lat == last - 1),
        ):
            low, high = pl.ds(0, length), pl.ds(total - length, length)
            lists[g] += [
                (
                    remote(
                        slots.at[g, high],
                        north[g].at[high],
                        y_send.at[0, g],
                        y_recv.at[0, g],
                        lat + 1,
                        lon,
                    ),
                    landed(north[g].at[high], y_recv.at[0, g]),
                    jnp.logical_and(down, sends_down),
                    jnp.logical_and(up, north_comes),
                ),
                (
                    remote(
                        slots.at[g, low],
                        south[g].at[low],
                        y_send.at[1, g],
                        y_recv.at[1, g],
                        lat - 1,
                        lon,
                    ),
                    landed(south[g].at[low], y_recv.at[1, g]),
                    jnp.logical_and(up, sends_up),
                    jnp.logical_and(down, south_comes),
                ),
            ]
        for copy, _, sends, _ in lists[g]:
            pl.when(sends)(copy.start)

    def dense(g, lon_there, store):
        def row(t, carry):
            at = lon_there * rows + t
            i, j = at // 128, lax.rem(at, 128)
            a = own_index[1, i, j]
            b = jnp.where(up, north_index[i, j], total)
            c = jnp.where(down, south_index[i, j], total)
            value = own[g][a].astype(F32) + north[g][b].astype(F32) + south[g][c].astype(F32)
            store(t, value.astype(BF16))
            return carry

        lax.fori_loop(0, rows, row, 0, unroll=8)

    core_copies, z_copies = [], []
    for g in range(groups):
        loads[g].wait()
        for _, arrival, _, comes in lists[g]:
            pl.when(comes)(arrival.wait)
        for part, (theirs, ours) in enumerate(((beside_across, across), (beside, lon))):

            def put_away(t, value):
                away[part, g, t] = value

            def put_mine(t, value):
                mine[part, g, t] = value

            dense(g, theirs, put_away)
            copy = remote(
                away.at[part, g],
                from_core.at[part, g],
                core_send.at[part, g],
                core_recv.at[part, g],
                lat,
                beside,
            )
            copy.start()
            core_copies.append(copy)
            dense(g, ours, put_mine)
            if part == 0:
                landed(from_core.at[0, g], core_recv.at[0, g]).wait()
                to_z[g] = (mine[0, g].astype(F32) + from_core[0, g].astype(F32)).astype(BF16)
                copy = remote(
                    to_z.at[g], from_z.at[g], z_send.at[g], z_recv.at[g], lat, across
                )
                copy.start()
                z_copies.append(copy)
        if g < 2:
            held = receive_maximum(partial.at[g])
            send_maximum(g + 1)

    lane = lax.broadcasted_iota(jnp.int32, (size, cols), 1)
    tiles = edges.shape[0]
    for g in range(groups):
        landed(from_core.at[1, g], core_recv.at[1, g]).wait()
        landed(from_z.at[g], z_recv.at[g]).wait()
        part = pl.ds(g * size, size)
        for tile in range(tiles):
            edge = jnp.zeros((size, cols), F32)
            for k in range(32):
                r = tile * 32 + k
                flux = (
                    mine[1, g, r].astype(F32)
                    + from_core[1, g, r].astype(F32)
                    + from_z[g, r].astype(F32)
                )
                v = (atmos[r, part].astype(F32) + flux).astype(BF16)
                first[r, part] = v
                rolled = pltpu.roll(v.astype(F32), (4 * k + 2) % cols, 1)
                edge = jnp.where(lane // 4 == k, rolled, edge)
            edges[tile, part] = edge.astype(BF16)
    lo, hi = edges.at[0], edges.at[tiles - 1]
    moves = [
        (edges, right.at[pl.ds(1, tiles)], lat, west, always, always),
        (edges, left.at[pl.ds(1, tiles)], lat, east, always, always),
        (first.at[pl.ds(0, 2)], bottom, lat - 1, lon, up, down),
        (first.at[pl.ds(rows - 2, 2)], top, lat + 1, lon, down, up),
        (lo, right.at[tiles + 1], lat - 1, west, up, down),
        (lo, left.at[tiles + 1], lat - 1, east, up, down),
        (hi, right.at[0], lat + 1, west, down, up),
        (hi, left.at[0], lat + 1, east, down, up),
    ]
    copies = [
        remote(src, dst, halo_send.at[i], halo_recv.at[i], a, b)
        for i, (src, dst, a, b, _, _) in enumerate(moves)
    ]
    for copy, move in zip(copies, moves):
        pl.when(move[4])(copy.start)
    receive_maximum(None)
    for copy in core_copies + z_copies + small:
        copy.wait_send()
    for g in range(groups):
        for copy, _, sends, _ in lists[g]:
            pl.when(sends)(copy.wait_send)
    for i, (copy, move) in enumerate(zip(copies, moves)):
        pl.when(move[4])(copy.wait_send)
        pl.when(move[5])(landed(move[1], halo_recv.at[i]).wait)


def couple(operands, count, edge_count, collective_id, lat_count, lon_count):
    _, _, _, slots, atmos, overflow = operands
    groups, total, size, cols = slots.shape
    rows, channels, cols = atmos.shape
    tiles = rows // 32
    vmem = pl.BlockSpec(memory_space=pltpu.VMEM)
    smem = pl.BlockSpec(memory_space=pltpu.SMEM)
    dma = pltpu.SemaphoreType.DMA
    shapes = [(rows, channels, cols)] + [(2, channels, cols)] * 2 + [(tiles + 2, channels, cols)] * 2
    received = pltpu.VMEM((total + 1, size, cols), BF16)
    peers = lon_count - 1 + 3 + lat_count // 4 - 1
    one = pltpu.VMEM((groups, rows, size, cols), BF16)
    two = pltpu.VMEM((2, groups, rows, size, cols), BF16)
    return pl.pallas_call(
        functools.partial(couple_kernel, lat_count, lon_count, count, edge_count),
        out_shape=[jax.ShapeDtypeStruct(s, BF16) for s in shapes]
        + [jax.ShapeDtypeStruct((1,), jnp.int32)],
        in_specs=[smem] * 3 + whole_any(1) + [vmem] * 2,
        out_specs=[vmem] + whole_any(4) + [smem],
        scratch_shapes=[received] * (3 * groups)
        + [two] * 3
        + [one] * 2
        + [pltpu.VMEM((tiles, channels, cols), BF16)]
        + [dma((groups,))]
        + [dma((2, groups))] * 4
        + [dma((groups,))] * 2
        + [dma((8,))] * 2
        + [pltpu.VMEM((peers,) + overflow.shape, jnp.int32)]
        + [pltpu.VMEM((2,) + overflow.shape, jnp.int32)]
        + [dma((peers,))] * 2,
        compiler_params=pltpu.CompilerParams(
            collective_id=collective_id, has_side_effects=True, vmem_limit_bytes=VMEM_LIMIT
        ),
        name="couple",
    )(*operands)


def atmos_kernel(
    lat_count, a_ref, top_ref, bottom_ref, left_ref, right_ref, w1_ref, b1_ref, w2_ref, b2_ref, out_ref, tall, second
):
    count, channels, cols = a_ref.shape
    lat = lax.axis_index("lat")
    b1, b2 = column(b1_ref[...]), column(b2_ref[...])

    tall[2 : 2 + count, :, 0:cols] = a_ref[...]
    lane = lax.broadcasted_iota(jnp.int32, (channels, cols), 1)
    for tile in range(count // 32 + 2):
        side = jnp.where(lane % 4 < 2, left_ref[tile], right_ref[tile]).astype(F32)
        for k in range(32):
            r = tile * 32 - 32 + k
            if r < -2 or r >= count + 2:
                continue
            v = pltpu.roll(side, (126 - 4 * k) % cols, 1).astype(BF16)
            if r < 0 or r >= count:
                inside = lat > 0 if r < 0 else lat < lat_count - 1
                main = top_ref[r + 2] if r < 0 else bottom_ref[r - count]
                tall[r + 2, :, 0:cols] = jnp.where(inside, main, jnp.zeros_like(main))
                v = jnp.where(inside, v, jnp.zeros_like(v))
            tall[r + 2, :, cols:] = v

    def conv(source, weight, start, group):
        fields = [
            jnp.concatenate([source[start + i + d] for d in range(3)], axis=0)
            for i in range(group)
        ]
        return jnp.dot(weight, jnp.concatenate(fields, axis=1), preferred_element_type=F32)

    def first(step, carry):
        group = FIRST_ROWS
        start = step * group
        taps = conv(tall, w1_ref[...], start, group)
        for i in range(group):
            j = start + i
            value = silu(shifted_sum(taps[:, i * 2 * cols : (i + 1) * 2 * cols]) + b1)
            outside = jnp.logical_or(
                jnp.logical_and(j == 0, lat == 0),
                jnp.logical_and(j == count + 1, lat == lat_count - 1),
            )
            second[j] = jnp.where(outside, 0.0, value).astype(BF16)
        return carry

    lax.fori_loop(0, (count + 2) // FIRST_ROWS, first, 0)

    def last(step, carry):
        group = LAST_ROWS
        start = step * group
        taps = conv(second, w2_ref[...], start, group)
        rows = []
        for i in range(group):
            value = shifted_sum(taps[:, i * 2 * cols : (i + 1) * 2 * cols])[:, :cols]
            rows.append(a_ref[start + i].astype(F32) + (value + b2))
        block = jnp.swapaxes(jnp.stack(rows), 0, 1).astype(BF16)
        out_ref[:, pl.ds(pl.multiple_of(start, group), group), :] = block
        return carry

    lax.fori_loop(0, count // LAST_ROWS, last, 0)


def atmos_step(a, top, bottom, left, right, w1, b1, w2, b2, lat_count):
    count, channels, cols = a.shape
    vmem = pl.BlockSpec(memory_space=pltpu.VMEM)
    return pl.pallas_call(
        functools.partial(atmos_kernel, lat_count),
        out_shape=jax.ShapeDtypeStruct((channels, count, cols), BF16),
        in_specs=[vmem] * 9,
        out_specs=vmem,
        scratch_shapes=[
            pltpu.VMEM((count + 4, channels, 2 * cols), BF16),
            pltpu.VMEM((count + 2, channels, 2 * cols), BF16),
        ],
        compiler_params=pltpu.CompilerParams(vmem_limit_bytes=VMEM_LIMIT),
        name="atmos",
    )(a, top, bottom, left, right, w1, b1, w2, b2)


def per_device(
    ocean_state,
    sea_mask,
    ocean_w1,
    ocean_b1,
    ocean_w2,
    ocean_b2,
    regrid_weight,
    route_dev,
    route_row,
    atmos_state,
    atmos_w1,
    atmos_b1,
    atmos_w2,
    atmos_b2,
):
    lat_count, lon_count = lax.axis_size("lat"), lax.axis_size("lon")
    atmos_rows = atmos_state.shape[1]

    count = route_dev.size
    weights = (ocean_w1, ocean_w2, atmos_w1, atmos_w2)
    hidden, index, north_index, south_index, meta, overflow, *weights = ocean_halo(
        ocean_state.transpose(1, 0, 2),
        sea_mask,
        route_dev,
        route_row,
        weights,
        ocean_b1[None, :],
        lat_count,
        lon_count,
        atmos_rows,
    )
    ocean_next, slots = ocean_step(
        meta,
        hidden,
        sea_mask,
        weights[0],
        ocean_b2[None, :],
        regrid_weight.reshape(-1, 256, 128),
    )
    operands = (index, north_index, south_index, slots, atmos_state.transpose(1, 0, 2), overflow)
    *coupled, overflow = couple(operands, SHORT, EDGE_SHORT, 1, lat_count, lon_count)
    first, top, bottom, left, right = lax.cond(
        overflow[0] > 0,
        lambda short, operands: tuple(couple(operands, count, count, 2, lat_count, lon_count)[:5]),
        lambda short, operands: short,
        tuple(coupled),
        operands,
    )
    atmos_next = atmos_step(
        first,
        top,
        bottom,
        left,
        right,
        weights[1],
        atmos_b1[None, :],
        weights[2],
        atmos_b2[None, :],
        lat_count,
    )
    return ocean_next, atmos_next


def solution(mesh):
    in_specs = (
        P(None, "lat", "lon"),
        P("lat", "lon"),
        P(),
        P(),
        P(),
        P(),
        P(("lat", "lon"), None, None, None),
        P(("lat", "lon"), None),
        P(("lat", "lon"), None),
        P(None, "lat", "lon"),
        P(),
        P(),
        P(),
        P(),
    )
    out_specs = (P(None, "lat", "lon"), P(None, "lat", "lon"))
    return jax.shard_map(
        per_device, mesh=mesh, in_specs=in_specs, out_specs=out_specs, check_vma=False
    )
```

```python
import functools

import jax
import jax.numpy as jnp
from jax import lax
from jax.experimental import pallas as pl
from jax.experimental.pallas import tpu as pltpu
from jax.sharding import PartitionSpec as P

MESH = pl.DeviceIdType.MESH
F32 = jnp.float32
BF16 = jnp.bfloat16
VMEM_LIMIT = 56 * 1024 * 1024
GROUPS = 4
FIRST_ROWS = 22
LAST_ROWS = 32
SHORT = 32
EDGE_SHORT = 48


def silu(v):
    return 0.5 * v * (1.0 + jnp.tanh(0.5 * v))


def shifted_sum(taps):
    out = taps.shape[0] // 3
    columns = taps.shape[1]
    return (
        pltpu.roll(taps[0:out], 1, 1)
        + taps[out : 2 * out]
        + pltpu.roll(taps[2 * out :], columns - 1, 1)
    )


def stack_weight(weight_ref, out_ref):
    out, inn = weight_ref.shape[2:]
    padded = out_ref.shape[1] // 3
    for dc in range(3):
        pieces = []
        for dr in range(3):
            pieces.append(weight_ref[dr, dc].astype(F32))
            if padded > inn:
                pieces.append(jnp.zeros((out, padded - inn), F32))
        out_ref[dc * out : (dc + 1) * out, :] = jnp.concatenate(pieces, axis=1).astype(BF16)


def column(bias):
    n = bias.shape[1]
    at = lax.broadcasted_iota(jnp.int32, (n, n), 0) == lax.broadcasted_iota(jnp.int32, (n, n), 1)
    return jnp.sum(jnp.where(at, bias, jnp.zeros_like(bias)), axis=1, keepdims=True)


def remote(src, dst, send_sem, recv_sem, lat, lon):
    return pltpu.make_async_remote_copy(
        src_ref=src,
        dst_ref=dst,
        send_sem=send_sem,
        recv_sem=recv_sem,
        device_id={"lat": lat, "lon": lon},
        device_id_type=MESH,
    )


def landed(ref, sem):
    return pltpu.make_async_copy(ref, ref, sem)


def list_lons(lat, lon):
    across = lax.rem(lon + 2, 4)
    odd = lax.rem(lon, 2) == 1
    up = jnp.where(jnp.logical_and(odd, lax.rem(lat, 4) == 0), across, lon)
    down = jnp.where(jnp.logical_and(odd, lax.rem(lat, 4) == 3), across, lon)
    return up, down


def greet(partners):
    barrier = pltpu.get_barrier_semaphore()
    for lat, lon, ok in partners:

        @pl.when(ok)
        def _():
            pl.semaphore_signal(
                barrier, inc=1, device_id={"lat": lat, "lon": lon}, device_id_type=MESH
            )


def greeted(waits):
    pl.semaphore_wait(pltpu.get_barrier_semaphore(), waits)


def whole_any(count):
    return [pl.BlockSpec(memory_space=pl.ANY)] * count


def ocean_halo_kernel(
    lat_count,
    lon_count,
    atmos_rows,
    x_ref,
    mask_ref,
    dev_ref,
    row_ref,
    w1_ref,
    w2_ref,
    w3_ref,
    w4_ref,
    b1_ref,
    hidden,
    index,
    north_index,
    south_index,
    meta,
    overflow,
    w2_out,
    w3_out,
    w4_out,
    left,
    right,
    edges,
    tall,
    w1_out,
    send_sem,
    recv_sem,
):
    lat, lon = lax.axis_index("lat"), lax.axis_index("lon")
    rows, inputs, cols = x_ref.shape
    channels = tall.shape[1]
    west = lax.rem(lon + lon_count - 1, lon_count)
    east = lax.rem(lon + 1, lon_count)
    up, down, always = lat > 0, lat < lat_count - 1, lat >= 0
    edge = jnp.logical_or(lat == 0, lat == lat_count - 1)
    partners = [(lat, west, always), (lat, east, always)]
    for there, ok in ((lat - 1, up), (lat + 1, down)):
        partners += [(there, side, ok) for side in (west, lon, east)]
    up_lon, down_lon = list_lons(lat, lon)
    partners += [(lat - 1, up_lon, up), (lat + 1, down_lon, down)]
    greet(partners)

    keys = (dev_ref[...] - (lat - 1) * lon_count) * atmos_rows + row_ref[...]
    key = jnp.concatenate([keys[k : k + 1] for k in range(keys.shape[0])], axis=1)
    count = key.shape[1]
    key_down = column(key)
    blocks = keys.shape[1]
    across = lax.broadcasted_iota(jnp.int32, (count, count), 1)
    across = lax.rem(across, blocks) * keys.shape[0] + lax.div(across, blocks)
    along = lax.broadcasted_iota(jnp.int32, (count, count), 0)
    along = lax.rem(along, blocks) * keys.shape[0] + lax.div(along, blocks)
    again = jnp.logical_and(key_down == key, along < across).astype(jnp.int32)
    place = jnp.sum((key_down < key).astype(jnp.int32) + again, axis=0, keepdims=True)
    place_down = column(place)
    first_down = column(1 - jnp.max(again, axis=0, keepdims=True))
    lane = lax.broadcasted_iota(jnp.int32, (1, count), 1)
    meta[0:1, :] = place
    meta[1:2, :] = jnp.max(jnp.where(place_down == lane, first_down, 0), axis=0, keepdims=True)
    per_step = lon_count * atmos_rows
    for step in range(3):
        for row in range(8):
            if row * count < per_step:
                number = lane + (step * per_step + row * count)
                places = jnp.max(
                    jnp.where(key_down == number, place_down, -1), axis=0, keepdims=True
                )
                index[step, row : row + 1, :] = jnp.where(places < 0, count, places)
            else:
                index[step, row : row + 1, :] = jnp.full((1, count), count, jnp.int32)
    low = jnp.sum((key < per_step).astype(jnp.int32), axis=1, keepdims=True)
    high = jnp.sum((key >= 2 * per_step).astype(jnp.int32), axis=1, keepdims=True)
    most = jnp.where(edge, EDGE_SHORT, SHORT)
    long = (jnp.maximum(low, high) > most).astype(jnp.int32)
    overflow[...] = jnp.broadcast_to(long, overflow.shape)

    lane = lax.broadcasted_iota(jnp.int32, (channels, 128), 1)
    extra = lax.broadcasted_iota(jnp.int32, (channels - inputs, cols), 0)
    for k in range(rows):
        tall[k + 2, 0:inputs, 0:cols] = x_ref[k]
        mask = jnp.where(extra == 0, mask_ref[k : k + 1, :], 0).astype(F32).astype(BF16)
        tall[k + 2, inputs:, 0:cols] = mask
    tile = jnp.zeros((channels, 128), F32)
    for k in range(rows):
        low, high = tall[k + 2, :, 0:128], tall[k + 2, :, cols - 128 : cols]
        both = jnp.where(lane < 64, low, high).astype(F32)
        tile = jnp.where(lane // 4 == k, pltpu.roll(both, (4 * k + 2) % 128, 1), tile)
    edges[...] = tile.astype(BF16)

    stack_weight(w1_ref, w1_out)
    b1 = column(b1_ref[...])
    blank = jnp.zeros((2, channels, cols), BF16)

    @pl.when(jnp.logical_not(up))
    def _():
        tall[0:2, :, 0:cols] = blank

    @pl.when(jnp.logical_not(down))
    def _():
        tall[rows + 2 :, :, 0:cols] = blank

    greeted(jnp.where(edge, 6, 10))
    def two(start):
        return tall.at[pl.ds(start, 2), :, pl.ds(0, cols)]

    moves = [
        (edges, right.at[1], lat, west, always, always),
        (edges, left.at[1], lat, east, always, always),
        (edges, right.at[2], lat - 1, west, up, down),
        (edges, left.at[2], lat - 1, east, up, down),
        (edges, right.at[0], lat + 1, west, down, up),
        (edges, left.at[0], lat + 1, east, down, up),
        (index.at[0], south_index, lat - 1, up_lon, up, down),
        (index.at[2], north_index, lat + 1, down_lon, down, up),
        (two(2), two(rows + 2), lat - 1, lon, up, down),
        (two(rows), two(0), lat + 1, lon, down, up),
    ]
    copies = [
        remote(src, dst, send_sem.at[i], recv_sem.at[i], a, b)
        for i, (src, dst, a, b, _, _) in enumerate(moves)
    ]
    for copy, move in zip(copies, moves):
        pl.when(move[4])(copy.start)
    for weight, out in ((w2_ref, w2_out), (w3_ref, w3_out), (w4_ref, w4_out)):
        stack_weight(weight, out)

    def arrive(numbers):
        for i in numbers:
            pl.when(moves[i][5])(landed(moves[i][1], recv_sem.at[i]).wait)

    def sides(tile, some):
        both = jnp.where(lane % 4 < 2, left[tile], right[tile]).astype(F32)
        for k in some:
            side = pltpu.roll(both, (126 - 4 * k) % 128, 1).astype(BF16)
            if tile != 1:
                inside = lat > 0 if tile == 0 else lat < lat_count - 1
                side = jnp.where(inside, side, jnp.zeros_like(side))
            tall[(tile - 1) * rows + k + 2, :, cols:] = side

    def conv(some):
        for j in some:
            fields = jnp.concatenate([tall[j], tall[j + 1], tall[j + 2]], axis=0)
            taps = jnp.dot(w1_out[...], fields, preferred_element_type=F32)
            mask = tall[j + 1, inputs : inputs + 1, :].astype(F32)
            hidden[j] = (silu(shifted_sum(taps) + b1) * mask).astype(BF16)

    arrive((0, 1))
    sides(1, range(rows))
    conv(range(2, rows))
    arrive(range(2, len(moves)))
    sides(0, range(rows - 2, rows))
    sides(2, range(2))
    conv((0, 1, rows, rows + 1))
    for copy, move in zip(copies, moves):
        pl.when(move[4])(copy.wait_send)


def ocean_halo(x, sea_mask, route_dev, route_row, weights, b1, lat_count, lon_count, atmos_rows):
    rows, inputs, cols = x.shape
    channels = -(-(inputs + 1) // 16) * 16
    count = route_dev.size
    weights = [w.transpose(2, 3, 0, 1) for w in weights]
    stacked = [
        jax.ShapeDtypeStruct((3 * w.shape[2], 3 * (-(-w.shape[3] // 16) * 16)), BF16) for w in weights
    ]
    table = jax.ShapeDtypeStruct((8, count), jnp.int32)
    vmem = pl.BlockSpec(memory_space=pltpu.VMEM)
    out = weights[0].shape[2]
    return pl.pallas_call(
        functools.partial(ocean_halo_kernel, lat_count, lon_count, atmos_rows),
        out_shape=[
            jax.ShapeDtypeStruct((rows + 2, out, cols + 128), BF16),
            jax.ShapeDtypeStruct((3,) + table.shape, jnp.int32),
            table,
            table,
            jax.ShapeDtypeStruct((2, count), jnp.int32),
            table,
        ]
        + stacked[1:],
        in_specs=[vmem] * 9,
        out_specs=[vmem] * 2 + whole_any(2) + [vmem] * 5,
        scratch_shapes=[
            pltpu.VMEM((3, channels, 128), BF16),
            pltpu.VMEM((3, channels, 128), BF16),
            pltpu.VMEM((channels, 128), BF16),
            pltpu.VMEM((rows + 4, channels, cols + 128), BF16),
            pltpu.VMEM(stacked[0].shape, BF16),
            pltpu.SemaphoreType.DMA((10,)),
            pltpu.SemaphoreType.DMA((10,)),
        ],
        compiler_params=pltpu.CompilerParams(
            collective_id=0, has_side_effects=True, vmem_limit_bytes=VMEM_LIMIT
        ),
        name="ocean_halo",
    )(x, sea_mask, route_dev.T, route_row.T, *weights, b1)


def ocean_kernel(
    meta, hidden, mask_ref, w2_ref, b2_ref, regrid, next_ref, slots_ref, listed, weights, kept, sem
):
    rows, cols = mask_ref.shape
    blocks = regrid.shape[0] // rows
    copies = []
    for r in range(rows):
        some = pl.ds(r * blocks, blocks)
        copies.append(pltpu.make_async_copy(regrid.at[some], weights.at[some], sem.at[r]))
        copies[r].start()
    b2 = column(b2_ref[...])
    for r in range(rows):
        field = jnp.concatenate([hidden[r], hidden[r + 1], hidden[r + 2]], axis=0)
        taps = jnp.dot(w2_ref[...], field, preferred_element_type=F32)
        result = (shifted_sum(taps)[:, :cols] + b2) * mask_ref[r : r + 1, :].astype(F32)
        kept[r] = result
        result = result.astype(BF16)
        copies[r].wait()
        for q in range(blocks):
            both = lax.dot_general(
                result[:, q * 128 : (q + 1) * 128],
                weights[r * blocks + q],
                (((1,), (1,)), ((), ())),
                preferred_element_type=F32,
            ).astype(BF16)
            for k in range(2):
                place = meta[0, k * (rows * blocks) + r * blocks + q]
                listed[place] = both[:, k * 128 : (k + 1) * 128]

    groups, slots, size = slots_ref.shape[:3]

    def add(i, run):
        value = listed[i].astype(F32)
        run = jnp.where(meta[1, i] == 1, value, run + value)
        for g in range(groups):
            slots_ref[g, i] = run[g * size : (g + 1) * size].astype(BF16)
        return run

    lax.fori_loop(0, slots, add, jnp.zeros(listed.shape[1:], F32), unroll=8)
    for q in range(cols // 128):
        part = slice(q * 128, (q + 1) * 128)
        block = jnp.stack([kept[r, :, part] for r in range(rows)])
        next_ref[:, :, part] = jnp.swapaxes(block, 0, 1).astype(BF16)


def ocean_step(meta, hidden, mask, w2, b2, regrid):
    rows, cols = mask.shape
    out = w2.shape[0] // 3
    slots = meta.shape[1]
    vmem = pl.BlockSpec(memory_space=pltpu.VMEM)
    return pl.pallas_call(
        ocean_kernel,
        out_shape=(
            jax.ShapeDtypeStruct((out, rows, cols), BF16),
            jax.ShapeDtypeStruct((GROUPS, slots, out // GROUPS, 128), BF16),
        ),
        in_specs=[pl.BlockSpec(memory_space=pltpu.SMEM)] + [vmem] * 4 + whole_any(1),
        out_specs=[vmem] * 2,
        scratch_shapes=[
            pltpu.VMEM((slots, out, 128), BF16),
            pltpu.VMEM(regrid.shape, BF16),
            pltpu.VMEM((rows, out, cols), F32),
            pltpu.SemaphoreType.DMA((rows,)),
        ],
        compiler_params=pltpu.CompilerParams(vmem_limit_bytes=VMEM_LIMIT),
        name="ocean",
    )(meta, hidden, mask, w2, b2, regrid)


def couple_kernel(
    lat_count,
    lon_count,
    count,
    edge_count,
    own_index,
    north_index,
    south_index,
    slots,
    atmos,
    overflow,
    first,
    top,
    bottom,
    left,
    right,
    overflow_of_all,
    *scratch,
):
    lat, lon = lax.axis_index("lat"), lax.axis_index("lon")
    west = lax.rem(lon + lon_count - 1, lon_count)
    east = lax.rem(lon + 1, lon_count)
    across = lax.rem(lon + 2, lon_count)
    beside = lon + 1 - 2 * lax.rem(lon, 2)
    beside_across = lax.rem(beside + 2, lon_count)
    up, down, always = lat > 0, lat < lat_count - 1, lat >= 0
    edge = jnp.logical_or(lat == 0, lat == lat_count - 1)
    partners = [(lat, there, always) for there in (west, east, across)]
    for there, ok in ((lat - 1, up), (lat + 1, down)):
        partners += [(there, side, ok) for side in (west, lon, east)]
    four, inner = lat // 4, lax.rem(lat, 4)
    fours = lat_count // 4
    rounds = [
        [(lat, lax.rem(lon + k, lon_count)) for k in range(1, lon_count)],
        [(four * 4 + lax.rem(inner + k, 4), lon) for k in range(1, 4)],
        [(lax.rem(four + k, fours) * 4 + inner, lon) for k in range(1, fours)],
    ]
    partners += [(a, b, always) for peers in rounds[1:] for a, b in peers]
    up_lon, down_lon = list_lons(lat, lon)
    partners += [(lat - 1, up_lon, up), (lat + 1, down_lon, down)]
    greet(partners)

    groups, total, size, cols = slots.shape
    rows, channels = first.shape[:2]
    own, north, south = (scratch[i * groups : (i + 1) * groups] for i in range(3))
    away, mine, from_core, to_z, from_z, edges = scratch[3 * groups : 3 * groups + 6]
    load_sem, y_send, y_recv, core_send, core_recv, z_send, z_recv, halo_send, halo_recv = scratch[
        3 * groups + 6 : 3 * groups + 15
    ]
    gathered, partial, max_send, max_recv = scratch[3 * groups + 15 :]
    held, waiting, small = overflow, [], []

    def send_maximum(number):
        begin = sum(len(peers) for peers in rounds[:number])
        for i, (a, b) in enumerate(rounds[number], begin):
            small.append(remote(held, gathered.at[i], max_send.at[i], max_recv.at[i], a, b))
            small[-1].start()
            waiting.append(i)

    def receive_maximum(target):
        value = held[...]
        for i in waiting:
            landed(gathered.at[i], max_recv.at[i]).wait()
            value = jnp.maximum(value, gathered[i])
        waiting.clear()
        if target is None:
            overflow_of_all[0] = jnp.max(value)
        else:
            target[...] = value
        return target

    everything = pl.ds(0, total)
    loads = []
    for g in range(groups):
        loads.append(
            pltpu.make_async_copy(slots.at[g], own[g].at[everything], load_sem.at[g])
        )
        loads[g].start()
    for buffer in (own, north, south):
        for g in range(groups):
            buffer[g][total] = jnp.zeros((size, cols), BF16)
    greeted(jnp.where(edge, 7, 11) + sum(len(peers) for peers in rounds[1:]))
    send_maximum(0)

    last = lat_count - 1
    lists = []
    for g in range(groups):
        lists.append([])
        for length, sends_down, sends_up, north_comes, south_comes in (
            (count, lat > 0, lat < last, lat > 1, lat < last - 1),
            (edge_count, lat == 0, lat == last, lat == 1, lat == last - 1),
        ):
            low, high = pl.ds(0, length), pl.ds(total - length, length)
            lists[g] += [
                (
                    remote(
                        slots.at[g, high],
                        north[g].at[high],
                        y_send.at[0, g],
                        y_recv.at[0, g],
                        lat + 1,
                        down_lon,
                    ),
                    landed(north[g].at[high], y_recv.at[0, g]),
                    jnp.logical_and(down, sends_down),
                    jnp.logical_and(up, north_comes),
                ),
                (
                    remote(
                        slots.at[g, low],
                        south[g].at[low],
                        y_send.at[1, g],
                        y_recv.at[1, g],
                        lat - 1,
                        up_lon,
                    ),
                    landed(south[g].at[low], y_recv.at[1, g]),
                    jnp.logical_and(up, sends_up),
                    jnp.logical_and(down, south_comes),
                ),
            ]
        for copy, _, sends, _ in lists[g]:
            pl.when(sends)(copy.start)

    def dense(g, lon_there, store):
        def row(t, carry):
            at = lon_there * rows + t
            i, j = at // 128, lax.rem(at, 128)
            a = own_index[1, i, j]
            b = jnp.where(up, north_index[i, j], total)
            c = jnp.where(down, south_index[i, j], total)
            value = own[g][a].astype(F32) + north[g][b].astype(F32) + south[g][c].astype(F32)
            store(t, value.astype(BF16))
            return carry

        lax.fori_loop(0, rows, row, 0, unroll=8)

    core_copies, z_copies = [], []
    for g in range(groups):
        loads[g].wait()
        for _, arrival, _, comes in lists[g]:
            pl.when(comes)(arrival.wait)
        for part, (theirs, ours) in enumerate(((beside_across, across), (beside, lon))):

            def put_away(t, value):
                away[part, g, t] = value

            def put_mine(t, value):
                mine[part, g, t] = value

            dense(g, theirs, put_away)
            copy = remote(
                away.at[part, g],
                from_core.at[part, g],
                core_send.at[part, g],
                core_recv.at[part, g],
                lat,
                beside,
            )
            copy.start()
            core_copies.append(copy)
            dense(g, ours, put_mine)
            if part == 0:
                landed(from_core.at[0, g], core_recv.at[0, g]).wait()
                to_z[g] = (mine[0, g].astype(F32) + from_core[0, g].astype(F32)).astype(BF16)
                copy = remote(
                    to_z.at[g], from_z.at[g], z_send.at[g], z_recv.at[g], lat, across
                )
                copy.start()
                z_copies.append(copy)
        if g < 2:
            held = receive_maximum(partial.at[g])
            send_maximum(g + 1)

    lane = lax.broadcasted_iota(jnp.int32, (size, cols), 1)
    tiles = edges.shape[0]
    for g in range(groups):
        landed(from_core.at[1, g], core_recv.at[1, g]).wait()
        landed(from_z.at[g], z_recv.at[g]).wait()
        part = pl.ds(g * size, size)
        for tile in range(tiles):
            edge = jnp.zeros((size, cols), F32)
            for k in range(32):
                r = tile * 32 + k
                flux = (
                    mine[1, g, r].astype(F32)
                    + from_core[1, g, r].astype(F32)
                    + from_z[g, r].astype(F32)
                )
                v = (atmos[r, part].astype(F32) + flux).astype(BF16)
                first[r, part] = v
                rolled = pltpu.roll(v.astype(F32), (4 * k + 2) % cols, 1)
                edge = jnp.where(lane // 4 == k, rolled, edge)
            edges[tile, part] = edge.astype(BF16)
    lo, hi = edges.at[0], edges.at[tiles - 1]
    moves = [
        (edges, right.at[pl.ds(1, tiles)], lat, west, always, always),
        (edges, left.at[pl.ds(1, tiles)], lat, east, always, always),
        (first.at[pl.ds(0, 2)], bottom, lat - 1, lon, up, down),
        (first.at[pl.ds(rows - 2, 2)], top, lat + 1, lon, down, up),
        (lo, right.at[tiles + 1], lat - 1, west, up, down),
        (lo, left.at[tiles + 1], lat - 1, east, up, down),
        (hi, right.at[0], lat + 1, west, down, up),
        (hi, left.at[0], lat + 1, east, down, up),
    ]
    copies = [
        remote(src, dst, halo_send.at[i], halo_recv.at[i], a, b)
        for i, (src, dst, a, b, _, _) in enumerate(moves)
    ]
    for copy, move in zip(copies, moves):
        pl.when(move[4])(copy.start)
    receive_maximum(None)
    for copy in core_copies + z_copies + small:
        copy.wait_send()
    for g in range(groups):
        for copy, _, sends, _ in lists[g]:
            pl.when(sends)(copy.wait_send)
    for i, (copy, move) in enumerate(zip(copies, moves)):
        pl.when(move[4])(copy.wait_send)
        pl.when(move[5])(landed(move[1], halo_recv.at[i]).wait)


def couple(operands, count, edge_count, collective_id, lat_count, lon_count):
    _, _, _, slots, atmos, overflow = operands
    groups, total, size, cols = slots.shape
    rows, channels, cols = atmos.shape
    tiles = rows // 32
    vmem = pl.BlockSpec(memory_space=pltpu.VMEM)
    smem = pl.BlockSpec(memory_space=pltpu.SMEM)
    dma = pltpu.SemaphoreType.DMA
    shapes = [(rows, channels, cols)] + [(2, channels, cols)] * 2 + [(tiles + 2, channels, cols)] * 2
    received = pltpu.VMEM((total + 1, size, cols), BF16)
    peers = lon_count - 1 + 3 + lat_count // 4 - 1
    one = pltpu.VMEM((groups, rows, size, cols), BF16)
    two = pltpu.VMEM((2, groups, rows, size, cols), BF16)
    return pl.pallas_call(
        functools.partial(couple_kernel, lat_count, lon_count, count, edge_count),
        out_shape=[jax.ShapeDtypeStruct(s, BF16) for s in shapes]
        + [jax.ShapeDtypeStruct((1,), jnp.int32)],
        in_specs=[smem] * 3 + whole_any(1) + [vmem] * 2,
        out_specs=[vmem] + whole_any(4) + [smem],
        scratch_shapes=[received] * (3 * groups)
        + [two] * 3
        + [one] * 2
        + [pltpu.VMEM((tiles, channels, cols), BF16)]
        + [dma((groups,))]
        + [dma((2, groups))] * 4
        + [dma((groups,))] * 2
        + [dma((8,))] * 2
        + [pltpu.VMEM((peers,) + overflow.shape, jnp.int32)]
        + [pltpu.VMEM((2,) + overflow.shape, jnp.int32)]
        + [dma((peers,))] * 2,
        compiler_params=pltpu.CompilerParams(
            collective_id=collective_id, has_side_effects=True, vmem_limit_bytes=VMEM_LIMIT
        ),
        name="couple",
    )(*operands)


def atmos_kernel(
    lat_count, a_ref, top_ref, bottom_ref, left_ref, right_ref, w1_ref, b1_ref, w2_ref, b2_ref, out_ref, tall, second
):
    count, channels, cols = a_ref.shape
    lat = lax.axis_index("lat")
    b1, b2 = column(b1_ref[...]), column(b2_ref[...])

    tall[2 : 2 + count, :, 0:cols] = a_ref[...]
    lane = lax.broadcasted_iota(jnp.int32, (channels, cols), 1)
    for tile in range(count // 32 + 2):
        side = jnp.where(lane % 4 < 2, left_ref[tile], right_ref[tile]).astype(F32)
        for k in range(32):
            r = tile * 32 - 32 + k
            if r < -2 or r >= count + 2:
                continue
            v = pltpu.roll(side, (126 - 4 * k) % cols, 1).astype(BF16)
            if r < 0 or r >= count:
                inside = lat > 0 if r < 0 else lat < lat_count - 1
                main = top_ref[r + 2] if r < 0 else bottom_ref[r - count]
                tall[r + 2, :, 0:cols] = jnp.where(inside, main, jnp.zeros_like(main))
                v = jnp.where(inside, v, jnp.zeros_like(v))
            tall[r + 2, :, cols:] = v

    def conv(source, weight, start, group):
        fields = [
            jnp.concatenate([source[start + i + d] for d in range(3)], axis=0)
            for i in range(group)
        ]
        return jnp.dot(weight, jnp.concatenate(fields, axis=1), preferred_element_type=F32)

    def first(step, carry):
        group = FIRST_ROWS
        start = step * group
        taps = conv(tall, w1_ref[...], start, group)
        for i in range(group):
            j = start + i
            value = silu(shifted_sum(taps[:, i * 2 * cols : (i + 1) * 2 * cols]) + b1)
            outside = jnp.logical_or(
                jnp.logical_and(j == 0, lat == 0),
                jnp.logical_and(j == count + 1, lat == lat_count - 1),
            )
            second[j] = jnp.where(outside, 0.0, value).astype(BF16)
        return carry

    lax.fori_loop(0, (count + 2) // FIRST_ROWS, first, 0)

    def last(step, carry):
        group = LAST_ROWS
        start = step * group
        taps = conv(second, w2_ref[...], start, group)
        rows = []
        for i in range(group):
            value = shifted_sum(taps[:, i * 2 * cols : (i + 1) * 2 * cols])[:, :cols]
            rows.append(a_ref[start + i].astype(F32) + (value + b2))
        block = jnp.swapaxes(jnp.stack(rows), 0, 1).astype(BF16)
        out_ref[:, pl.ds(pl.multiple_of(start, group), group), :] = block
        return carry

    lax.fori_loop(0, count // LAST_ROWS, last, 0)


def atmos_step(a, top, bottom, left, right, w1, b1, w2, b2, lat_count):
    count, channels, cols = a.shape
    vmem = pl.BlockSpec(memory_space=pltpu.VMEM)
    return pl.pallas_call(
        functools.partial(atmos_kernel, lat_count),
        out_shape=jax.ShapeDtypeStruct((channels, count, cols), BF16),
        in_specs=[vmem] * 9,
        out_specs=vmem,
        scratch_shapes=[
            pltpu.VMEM((count + 4, channels, 2 * cols), BF16),
            pltpu.VMEM((count + 2, channels, 2 * cols), BF16),
        ],
        compiler_params=pltpu.CompilerParams(vmem_limit_bytes=VMEM_LIMIT),
        name="atmos",
    )(a, top, bottom, left, right, w1, b1, w2, b2)


def per_device(
    ocean_state,
    sea_mask,
    ocean_w1,
    ocean_b1,
    ocean_w2,
    ocean_b2,
    regrid_weight,
    route_dev,
    route_row,
    atmos_state,
    atmos_w1,
    atmos_b1,
    atmos_w2,
    atmos_b2,
):
    lat_count, lon_count = lax.axis_size("lat"), lax.axis_size("lon")
    atmos_rows = atmos_state.shape[1]

    count = route_dev.size
    weights = (ocean_w1, ocean_w2, atmos_w1, atmos_w2)
    hidden, index, north_index, south_index, meta, overflow, *weights = ocean_halo(
        ocean_state.transpose(1, 0, 2),
        sea_mask,
        route_dev,
        route_row,
        weights,
        ocean_b1[None, :],
        lat_count,
        lon_count,
        atmos_rows,
    )
    ocean_next, slots = ocean_step(
        meta,
        hidden,
        sea_mask,
        weights[0],
        ocean_b2[None, :],
        regrid_weight.reshape(-1, 256, 128),
    )
    operands = (index, north_index, south_index, slots, atmos_state.transpose(1, 0, 2), overflow)
    *coupled, overflow = couple(operands, SHORT, EDGE_SHORT, 1, lat_count, lon_count)
    first, top, bottom, left, right = lax.cond(
        overflow[0] > 0,
        lambda short, operands: tuple(couple(operands, count, count, 2, lat_count, lon_count)[:5]),
        lambda short, operands: short,
        tuple(coupled),
        operands,
    )
    atmos_next = atmos_step(
        first,
        top,
        bottom,
        left,
        right,
        weights[1],
        atmos_b1[None, :],
        weights[2],
        atmos_b2[None, :],
        lat_count,
    )
    return ocean_next, atmos_next


def solution(mesh):
    in_specs = (
        P(None, "lat", "lon"),
        P("lat", "lon"),
        P(),
        P(),
        P(),
        P(),
        P(("lat", "lon"), None, None, None),
        P(("lat", "lon"), None),
        P(("lat", "lon"), None),
        P(None, "lat", "lon"),
        P(),
        P(),
        P(),
        P(),
    )
    out_specs = (P(None, "lat", "lon"), P(None, "lat", "lon"))
    return jax.shard_map(
        per_device, mesh=mesh, in_specs=in_specs, out_specs=out_specs, check_vma=False
    )
```

```python
import functools

import jax
import jax.numpy as jnp
from jax import lax
from jax.experimental import pallas as pl
from jax.experimental.pallas import tpu as pltpu
from jax.sharding import PartitionSpec as P

MESH = pl.DeviceIdType.MESH
F32 = jnp.float32
BF16 = jnp.bfloat16
VMEM_LIMIT = 56 * 1024 * 1024
GROUPS = 4
FIRST_ROWS = 22
LAST_ROWS = 32
SHORT = 32
EDGE_SHORT = 48


def silu(v):
    return 0.5 * v * (1.0 + jnp.tanh(0.5 * v))


def shifted_sum(taps):
    out = taps.shape[0] // 3
    columns = taps.shape[1]
    return (
        pltpu.roll(taps[0:out], 1, 1)
        + taps[out : 2 * out]
        + pltpu.roll(taps[2 * out :], columns - 1, 1)
    )


def stack_weight(weight_ref, out_ref):
    out, inn = weight_ref.shape[2:]
    padded = out_ref.shape[1] // 3
    for dc in range(3):
        pieces = []
        for dr in range(3):
            pieces.append(weight_ref[dr, dc].astype(F32))
            if padded > inn:
                pieces.append(jnp.zeros((out, padded - inn), F32))
        out_ref[dc * out : (dc + 1) * out, :] = jnp.concatenate(pieces, axis=1).astype(BF16)


def column(bias):
    n = bias.shape[1]
    at = lax.broadcasted_iota(jnp.int32, (n, n), 0) == lax.broadcasted_iota(jnp.int32, (n, n), 1)
    return jnp.sum(jnp.where(at, bias, jnp.zeros_like(bias)), axis=1, keepdims=True)


def remote(src, dst, send_sem, recv_sem, lat, lon):
    return pltpu.make_async_remote_copy(
        src_ref=src,
        dst_ref=dst,
        send_sem=send_sem,
        recv_sem=recv_sem,
        device_id={"lat": lat, "lon": lon},
        device_id_type=MESH,
    )


def landed(ref, sem):
    return pltpu.make_async_copy(ref, ref, sem)


def list_lons(lat, lon):
    across = lax.rem(lon + 2, 4)
    odd = lax.rem(lon, 2) == 1
    up = jnp.where(jnp.logical_and(odd, lax.rem(lat, 4) == 0), across, lon)
    down = jnp.where(jnp.logical_and(odd, lax.rem(lat, 4) == 3), across, lon)
    return up, down


def greet(partners):
    barrier = pltpu.get_barrier_semaphore()
    for lat, lon, ok in partners:

        @pl.when(ok)
        def _():
            pl.semaphore_signal(
                barrier, inc=1, device_id={"lat": lat, "lon": lon}, device_id_type=MESH
            )


def greeted(waits):
    pl.semaphore_wait(pltpu.get_barrier_semaphore(), waits)


def whole_any(count):
    return [pl.BlockSpec(memory_space=pl.ANY)] * count


def ocean_halo_kernel(
    lat_count,
    lon_count,
    atmos_rows,
    x_ref,
    mask_ref,
    dev_ref,
    row_ref,
    w1_ref,
    w2_ref,
    w3_ref,
    w4_ref,
    b1_ref,
    hidden,
    index,
    north_index,
    south_index,
    meta,
    overflow,
    w2_out,
    w3_out,
    w4_out,
    left,
    right,
    edges,
    tall,
    w1_out,
    send_sem,
    recv_sem,
):
    lat, lon = lax.axis_index("lat"), lax.axis_index("lon")
    inputs, rows, cols = x_ref.shape
    channels = tall.shape[1]
    west = lax.rem(lon + lon_count - 1, lon_count)
    east = lax.rem(lon + 1, lon_count)
    up, down, always = lat > 0, lat < lat_count - 1, lat >= 0
    edge = jnp.logical_or(lat == 0, lat == lat_count - 1)
    partners = [(lat, west, always), (lat, east, always)]
    for there, ok in ((lat - 1, up), (lat + 1, down)):
        partners += [(there, side, ok) for side in (west, lon, east)]
    up_lon, down_lon = list_lons(lat, lon)
    partners += [(lat - 1, up_lon, up), (lat + 1, down_lon, down)]
    greet(partners)

    keys = (dev_ref[...] - (lat - 1) * lon_count) * atmos_rows + row_ref[...]
    key = jnp.concatenate([keys[k : k + 1] for k in range(keys.shape[0])], axis=1)
    count = key.shape[1]
    key_down = column(key)
    blocks = keys.shape[1]
    across = lax.broadcasted_iota(jnp.int32, (count, count), 1)
    across = lax.rem(across, blocks) * keys.shape[0] + lax.div(across, blocks)
    along = lax.broadcasted_iota(jnp.int32, (count, count), 0)
    along = lax.rem(along, blocks) * keys.shape[0] + lax.div(along, blocks)
    again = jnp.logical_and(key_down == key, along < across).astype(jnp.int32)
    place = jnp.sum((key_down < key).astype(jnp.int32) + again, axis=0, keepdims=True)
    place_down = column(place)
    first_down = column(1 - jnp.max(again, axis=0, keepdims=True))
    lane = lax.broadcasted_iota(jnp.int32, (1, count), 1)
    meta[0:1, :] = place
    meta[1:2, :] = jnp.max(jnp.where(place_down == lane, first_down, 0), axis=0, keepdims=True)
    per_step = lon_count * atmos_rows
    for step in range(3):
        for row in range(8):
            if row * count < per_step:
                number = lane + (step * per_step + row * count)
                places = jnp.max(
                    jnp.where(key_down == number, place_down, -1), axis=0, keepdims=True
                )
                index[step, row : row + 1, :] = jnp.where(places < 0, count, places)
            else:
                index[step, row : row + 1, :] = jnp.full((1, count), count, jnp.int32)
    low = jnp.sum((key < per_step).astype(jnp.int32), axis=1, keepdims=True)
    high = jnp.sum((key >= 2 * per_step).astype(jnp.int32), axis=1, keepdims=True)
    most = jnp.where(edge, EDGE_SHORT, SHORT)
    long = (jnp.maximum(low, high) > most).astype(jnp.int32)
    overflow[...] = jnp.broadcast_to(long, overflow.shape)

    lane = lax.broadcasted_iota(jnp.int32, (channels, 128), 1)
    for q in range(cols // 128):
        part = slice(q * 128, (q + 1) * 128)
        block = jnp.concatenate(
            [
                x_ref[:, :, part].astype(F32),
                mask_ref[:, part].astype(F32)[None],
                jnp.zeros((channels - inputs - 1, rows, 128), F32),
            ],
            axis=0,
        )
        tall[2 : 2 + rows, :, part] = jnp.swapaxes(block, 0, 1).astype(BF16)
    tile = jnp.zeros((channels, 128), F32)
    for k in range(rows):
        low, high = tall[k + 2, :, 0:128], tall[k + 2, :, cols - 128 : cols]
        both = jnp.where(lane < 64, low, high).astype(F32)
        tile = jnp.where(lane // 4 == k, pltpu.roll(both, (4 * k + 2) % 128, 1), tile)
    edges[...] = tile.astype(BF16)

    stack_weight(w1_ref, w1_out)
    b1 = column(b1_ref[...])
    blank = jnp.zeros((2, channels, cols), BF16)

    @pl.when(jnp.logical_not(up))
    def _():
        tall[0:2, :, 0:cols] = blank

    @pl.when(jnp.logical_not(down))
    def _():
        tall[rows + 2 :, :, 0:cols] = blank

    greeted(jnp.where(edge, 6, 10))
    def two(start):
        return tall.at[pl.ds(start, 2), :, pl.ds(0, cols)]

    moves = [
        (edges, right.at[1], lat, west, always, always),
        (edges, left.at[1], lat, east, always, always),
        (edges, right.at[2], lat - 1, west, up, down),
        (edges, left.at[2], lat - 1, east, up, down),
        (edges, right.at[0], lat + 1, west, down, up),
        (edges, left.at[0], lat + 1, east, down, up),
        (index.at[0], south_index, lat - 1, up_lon, up, down),
        (index.at[2], north_index, lat + 1, down_lon, down, up),
        (two(2), two(rows + 2), lat - 1, lon, up, down),
        (two(rows), two(0), lat + 1, lon, down, up),
    ]
    copies = [
        remote(src, dst, send_sem.at[i], recv_sem.at[i], a, b)
        for i, (src, dst, a, b, _, _) in enumerate(moves)
    ]
    for copy, move in zip(copies, moves):
        pl.when(move[4])(copy.start)
    for weight, out in ((w2_ref, w2_out), (w3_ref, w3_out), (w4_ref, w4_out)):
        stack_weight(weight, out)

    def arrive(numbers):
        for i in numbers:
            pl.when(moves[i][5])(landed(moves[i][1], recv_sem.at[i]).wait)

    def sides(tile, some):
        both = jnp.where(lane % 4 < 2, left[tile], right[tile]).astype(F32)
        for k in some:
            side = pltpu.roll(both, (126 - 4 * k) % 128, 1).astype(BF16)
            if tile != 1:
                inside = lat > 0 if tile == 0 else lat < lat_count - 1
                side = jnp.where(inside, side, jnp.zeros_like(side))
            tall[(tile - 1) * rows + k + 2, :, cols:] = side

    def conv(some):
        for j in some:
            fields = jnp.concatenate([tall[j], tall[j + 1], tall[j + 2]], axis=0)
            taps = jnp.dot(w1_out[...], fields, preferred_element_type=F32)
            mask = tall[j + 1, inputs : inputs + 1, :].astype(F32)
            hidden[j] = (silu(shifted_sum(taps) + b1) * mask).astype(BF16)

    arrive((0, 1))
    sides(1, range(rows))
    conv(range(2, rows))
    arrive(range(2, len(moves)))
    sides(0, range(rows - 2, rows))
    sides(2, range(2))
    conv((0, 1, rows, rows + 1))
    for copy, move in zip(copies, moves):
        pl.when(move[4])(copy.wait_send)


def ocean_halo(x, sea_mask, route_dev, route_row, weights, b1, lat_count, lon_count, atmos_rows):
    inputs, rows, cols = x.shape
    channels = -(-(inputs + 1) // 16) * 16
    count = route_dev.size
    weights = [w.transpose(2, 3, 0, 1) for w in weights]
    stacked = [
        jax.ShapeDtypeStruct((3 * w.shape[2], 3 * (-(-w.shape[3] // 16) * 16)), BF16) for w in weights
    ]
    table = jax.ShapeDtypeStruct((8, count), jnp.int32)
    vmem = pl.BlockSpec(memory_space=pltpu.VMEM)
    out = weights[0].shape[2]
    return pl.pallas_call(
        functools.partial(ocean_halo_kernel, lat_count, lon_count, atmos_rows),
        out_shape=[
            jax.ShapeDtypeStruct((rows + 2, out, cols + 128), BF16),
            jax.ShapeDtypeStruct((3,) + table.shape, jnp.int32),
            table,
            table,
            jax.ShapeDtypeStruct((2, count), jnp.int32),
            table,
        ]
        + stacked[1:],
        in_specs=[vmem] * 9,
        out_specs=[vmem] * 2 + whole_any(2) + [vmem] * 5,
        scratch_shapes=[
            pltpu.VMEM((3, channels, 128), BF16),
            pltpu.VMEM((3, channels, 128), BF16),
            pltpu.VMEM((channels, 128), BF16),
            pltpu.VMEM((rows + 4, channels, cols + 128), BF16),
            pltpu.VMEM(stacked[0].shape, BF16),
            pltpu.SemaphoreType.DMA((10,)),
            pltpu.SemaphoreType.DMA((10,)),
        ],
        compiler_params=pltpu.CompilerParams(
            collective_id=0, has_side_effects=True, vmem_limit_bytes=VMEM_LIMIT
        ),
        name="ocean_halo",
    )(x, sea_mask, route_dev.T, route_row.T, *weights, b1)


def ocean_kernel(
    meta, hidden, mask_ref, w2_ref, b2_ref, regrid, next_ref, slots_ref, listed, weights, kept, sem
):
    rows, cols = mask_ref.shape
    blocks = regrid.shape[0] // rows
    copies = []
    for r in range(rows):
        some = pl.ds(r * blocks, blocks)
        copies.append(pltpu.make_async_copy(regrid.at[some], weights.at[some], sem.at[r]))
        copies[r].start()
    b2 = column(b2_ref[...])
    for r in range(rows):
        field = jnp.concatenate([hidden[r], hidden[r + 1], hidden[r + 2]], axis=0)
        taps = jnp.dot(w2_ref[...], field, preferred_element_type=F32)
        result = (shifted_sum(taps)[:, :cols] + b2) * mask_ref[r : r + 1, :].astype(F32)
        kept[r] = result
        result = result.astype(BF16)
        copies[r].wait()
        for q in range(blocks):
            both = lax.dot_general(
                result[:, q * 128 : (q + 1) * 128],
                weights[r * blocks + q],
                (((1,), (1,)), ((), ())),
                preferred_element_type=F32,
            ).astype(BF16)
            for k in range(2):
                place = meta[0, k * (rows * blocks) + r * blocks + q]
                listed[place] = both[:, k * 128 : (k + 1) * 128]

    groups, slots, size = slots_ref.shape[:3]

    def add(i, run):
        value = listed[i].astype(F32)
        run = jnp.where(meta[1, i] == 1, value, run + value)
        for g in range(groups):
            slots_ref[g, i] = run[g * size : (g + 1) * size].astype(BF16)
        return run

    lax.fori_loop(0, slots, add, jnp.zeros(listed.shape[1:], F32), unroll=8)
    for q in range(cols // 128):
        part = slice(q * 128, (q + 1) * 128)
        block = jnp.stack([kept[r, :, part] for r in range(rows)])
        next_ref[:, :, part] = jnp.swapaxes(block, 0, 1).astype(BF16)


def ocean_step(meta, hidden, mask, w2, b2, regrid):
    rows, cols = mask.shape
    out = w2.shape[0] // 3
    slots = meta.shape[1]
    vmem = pl.BlockSpec(memory_space=pltpu.VMEM)
    return pl.pallas_call(
        ocean_kernel,
        out_shape=(
            jax.ShapeDtypeStruct((out, rows, cols), BF16),
            jax.ShapeDtypeStruct((GROUPS, slots, out // GROUPS, 128), BF16),
        ),
        in_specs=[pl.BlockSpec(memory_space=pltpu.SMEM)] + [vmem] * 4 + whole_any(1),
        out_specs=[vmem] * 2,
        scratch_shapes=[
            pltpu.VMEM((slots, out, 128), BF16),
            pltpu.VMEM(regrid.shape, BF16),
            pltpu.VMEM((rows, out, cols), F32),
            pltpu.SemaphoreType.DMA((rows,)),
        ],
        compiler_params=pltpu.CompilerParams(vmem_limit_bytes=VMEM_LIMIT),
        name="ocean",
    )(meta, hidden, mask, w2, b2, regrid)


def couple_kernel(
    lat_count,
    lon_count,
    count,
    edge_count,
    own_index,
    north_index,
    south_index,
    slots,
    atmos,
    overflow,
    first,
    top,
    bottom,
    left,
    right,
    overflow_of_all,
    *scratch,
):
    lat, lon = lax.axis_index("lat"), lax.axis_index("lon")
    west = lax.rem(lon + lon_count - 1, lon_count)
    east = lax.rem(lon + 1, lon_count)
    across = lax.rem(lon + 2, lon_count)
    beside = lon + 1 - 2 * lax.rem(lon, 2)
    beside_across = lax.rem(beside + 2, lon_count)
    up, down, always = lat > 0, lat < lat_count - 1, lat >= 0
    edge = jnp.logical_or(lat == 0, lat == lat_count - 1)
    partners = [(lat, there, always) for there in (west, east, across)]
    for there, ok in ((lat - 1, up), (lat + 1, down)):
        partners += [(there, side, ok) for side in (west, lon, east)]
    four, inner = lat // 4, lax.rem(lat, 4)
    fours = lat_count // 4
    rounds = [
        [(lat, lax.rem(lon + k, lon_count)) for k in range(1, lon_count)],
        [(four * 4 + lax.rem(inner + k, 4), lon) for k in range(1, 4)],
        [(lax.rem(four + k, fours) * 4 + inner, lon) for k in range(1, fours)],
    ]
    partners += [(a, b, always) for peers in rounds[1:] for a, b in peers]
    up_lon, down_lon = list_lons(lat, lon)
    partners += [(lat - 1, up_lon, up), (lat + 1, down_lon, down)]
    greet(partners)

    groups, total, size, cols = slots.shape
    rows, channels = first.shape[:2]
    own, north, south = (scratch[i * groups : (i + 1) * groups] for i in range(3))
    away, mine, from_core, to_z, from_z, edges = scratch[3 * groups : 3 * groups + 6]
    load_sem, y_send, y_recv, core_send, core_recv, z_send, z_recv, halo_send, halo_recv = scratch[
        3 * groups + 6 : 3 * groups + 15
    ]
    gathered, partial, max_send, max_recv, base = scratch[3 * groups + 15 :]
    held, waiting, small = overflow, [], []

    def send_maximum(number):
        begin = sum(len(peers) for peers in rounds[:number])
        for i, (a, b) in enumerate(rounds[number], begin):
            small.append(remote(held, gathered.at[i], max_send.at[i], max_recv.at[i], a, b))
            small[-1].start()
            waiting.append(i)

    def receive_maximum(target):
        value = held[...]
        for i in waiting:
            landed(gathered.at[i], max_recv.at[i]).wait()
            value = jnp.maximum(value, gathered[i])
        waiting.clear()
        if target is None:
            overflow_of_all[0] = jnp.max(value)
        else:
            target[...] = value
        return target

    everything = pl.ds(0, total)
    loads = []
    for g in range(groups):
        loads.append(
            pltpu.make_async_copy(slots.at[g], own[g].at[everything], load_sem.at[g])
        )
        loads[g].start()
    for buffer in (own, north, south):
        for g in range(groups):
            buffer[g][total] = jnp.zeros((size, cols), BF16)
    for at in range(0, rows, 16):
        block = atmos[:, at : at + 16, :].astype(F32)
        base[at : at + 16] = jnp.swapaxes(block, 0, 1).astype(BF16)
    greeted(jnp.where(edge, 7, 11) + sum(len(peers) for peers in rounds[1:]))
    send_maximum(0)

    last = lat_count - 1
    lists = []
    for g in range(groups):
        lists.append([])
        for length, sends_down, sends_up, north_comes, south_comes in (
            (count, lat > 0, lat < last, lat > 1, lat < last - 1),
            (edge_count, lat == 0, lat == last, lat == 1, lat == last - 1),
        ):
            low, high = pl.ds(0, length), pl.ds(total - length, length)
            lists[g] += [
                (
                    remote(
                        slots.at[g, high],
                        north[g].at[high],
                        y_send.at[0, g],
                        y_recv.at[0, g],
                        lat + 1,
                        down_lon,
                    ),
                    landed(north[g].at[high], y_recv.at[0, g]),
                    jnp.logical_and(down, sends_down),
                    jnp.logical_and(up, north_comes),
                ),
                (
                    remote(
                        slots.at[g, low],
                        south[g].at[low],
                        y_send.at[1, g],
                        y_recv.at[1, g],
                        lat - 1,
                        up_lon,
                    ),
                    landed(south[g].at[low], y_recv.at[1, g]),
                    jnp.logical_and(up, sends_up),
                    jnp.logical_and(down, south_comes),
                ),
            ]
        for copy, _, sends, _ in lists[g]:
            pl.when(sends)(copy.start)

    def dense(g, lon_there, store):
        def row(t, carry):
            at = lon_there * rows + t
            i, j = at // 128, lax.rem(at, 128)
            a = own_index[1, i, j]
            b = jnp.where(up, north_index[i, j], total)
            c = jnp.where(down, south_index[i, j], total)
            value = own[g][a].astype(F32) + north[g][b].astype(F32) + south[g][c].astype(F32)
            store(t, value.astype(BF16))
            return carry

        lax.fori_loop(0, rows, row, 0, unroll=8)

    core_copies, z_copies = [], []
    for g in range(groups):
        loads[g].wait()
        for _, arrival, _, comes in lists[g]:
            pl.when(comes)(arrival.wait)
        for part, (theirs, ours) in enumerate(((beside_across, across), (beside, lon))):

            def put_away(t, value):
                away[part, g, t] = value

            def put_mine(t, value):
                mine[part, g, t] = value

            dense(g, theirs, put_away)
            copy = remote(
                away.at[part, g],
                from_core.at[part, g],
                core_send.at[part, g],
                core_recv.at[part, g],
                lat,
                beside,
            )
            copy.start()
            core_copies.append(copy)
            dense(g, ours, put_mine)
            if part == 0:
                landed(from_core.at[0, g], core_recv.at[0, g]).wait()
                to_z[g] = (mine[0, g].astype(F32) + from_core[0, g].astype(F32)).astype(BF16)
                copy = remote(
                    to_z.at[g], from_z.at[g], z_send.at[g], z_recv.at[g], lat, across
                )
                copy.start()
                z_copies.append(copy)
        if g < 2:
            held = receive_maximum(partial.at[g])
            send_maximum(g + 1)

    lane = lax.broadcasted_iota(jnp.int32, (size, cols), 1)
    tiles = edges.shape[0]
    for g in range(groups):
        landed(from_core.at[1, g], core_recv.at[1, g]).wait()
        landed(from_z.at[g], z_recv.at[g]).wait()
        part = pl.ds(g * size, size)
        for tile in range(tiles):
            edge = jnp.zeros((size, cols), F32)
            for k in range(32):
                r = tile * 32 + k
                flux = (
                    mine[1, g, r].astype(F32)
                    + from_core[1, g, r].astype(F32)
                    + from_z[g, r].astype(F32)
                )
                v = (base[r, part].astype(F32) + flux).astype(BF16)
                first[r, part] = v
                rolled = pltpu.roll(v.astype(F32), (4 * k + 2) % cols, 1)
                edge = jnp.where(lane // 4 == k, rolled, edge)
            edges[tile, part] = edge.astype(BF16)
    lo, hi = edges.at[0], edges.at[tiles - 1]
    moves = [
        (edges, right.at[pl.ds(1, tiles)], lat, west, always, always),
        (edges, left.at[pl.ds(1, tiles)], lat, east, always, always),
        (first.at[pl.ds(0, 2)], bottom, lat - 1, lon, up, down),
        (first.at[pl.ds(rows - 2, 2)], top, lat + 1, lon, down, up),
        (lo, right.at[tiles + 1], lat - 1, west, up, down),
        (lo, left.at[tiles + 1], lat - 1, east, up, down),
        (hi, right.at[0], lat + 1, west, down, up),
        (hi, left.at[0], lat + 1, east, down, up),
    ]
    copies = [
        remote(src, dst, halo_send.at[i], halo_recv.at[i], a, b)
        for i, (src, dst, a, b, _, _) in enumerate(moves)
    ]
    for copy, move in zip(copies, moves):
        pl.when(move[4])(copy.start)
    receive_maximum(None)
    for copy in core_copies + z_copies + small:
        copy.wait_send()
    for g in range(groups):
        for copy, _, sends, _ in lists[g]:
            pl.when(sends)(copy.wait_send)
    for i, (copy, move) in enumerate(zip(copies, moves)):
        pl.when(move[4])(copy.wait_send)
        pl.when(move[5])(landed(move[1], halo_recv.at[i]).wait)


def couple(operands, count, edge_count, collective_id, lat_count, lon_count):
    _, _, _, slots, atmos, overflow = operands
    groups, total, size, cols = slots.shape
    channels, rows, cols = atmos.shape
    tiles = rows // 32
    vmem = pl.BlockSpec(memory_space=pltpu.VMEM)
    smem = pl.BlockSpec(memory_space=pltpu.SMEM)
    dma = pltpu.SemaphoreType.DMA
    shapes = [(rows, channels, cols)] + [(2, channels, cols)] * 2 + [(tiles + 2, channels, cols)] * 2
    received = pltpu.VMEM((total + 1, size, cols), BF16)
    peers = lon_count - 1 + 3 + lat_count // 4 - 1
    one = pltpu.VMEM((groups, rows, size, cols), BF16)
    two = pltpu.VMEM((2, groups, rows, size, cols), BF16)
    return pl.pallas_call(
        functools.partial(couple_kernel, lat_count, lon_count, count, edge_count),
        out_shape=[jax.ShapeDtypeStruct(s, BF16) for s in shapes]
        + [jax.ShapeDtypeStruct((1,), jnp.int32)],
        in_specs=[smem] * 3 + whole_any(1) + [vmem] * 2,
        out_specs=[vmem] + whole_any(4) + [smem],
        scratch_shapes=[received] * (3 * groups)
        + [two] * 3
        + [one] * 2
        + [pltpu.VMEM((tiles, channels, cols), BF16)]
        + [dma((groups,))]
        + [dma((2, groups))] * 4
        + [dma((groups,))] * 2
        + [dma((8,))] * 2
        + [pltpu.VMEM((peers,) + overflow.shape, jnp.int32)]
        + [pltpu.VMEM((2,) + overflow.shape, jnp.int32)]
        + [dma((peers,))] * 2
        + [pltpu.VMEM((rows, channels, cols), BF16)],
        compiler_params=pltpu.CompilerParams(
            collective_id=collective_id, has_side_effects=True, vmem_limit_bytes=VMEM_LIMIT
        ),
        name="couple",
    )(*operands)


def atmos_kernel(
    lat_count, a_ref, top_ref, bottom_ref, left_ref, right_ref, w1_ref, b1_ref, w2_ref, b2_ref, out_ref, tall, second
):
    count, channels, cols = a_ref.shape
    lat = lax.axis_index("lat")
    b1, b2 = column(b1_ref[...]), column(b2_ref[...])

    tall[2 : 2 + count, :, 0:cols] = a_ref[...]
    lane = lax.broadcasted_iota(jnp.int32, (channels, cols), 1)
    for tile in range(count // 32 + 2):
        side = jnp.where(lane % 4 < 2, left_ref[tile], right_ref[tile]).astype(F32)
        for k in range(32):
            r = tile * 32 - 32 + k
            if r < -2 or r >= count + 2:
                continue
            v = pltpu.roll(side, (126 - 4 * k) % cols, 1).astype(BF16)
            if r < 0 or r >= count:
                inside = lat > 0 if r < 0 else lat < lat_count - 1
                main = top_ref[r + 2] if r < 0 else bottom_ref[r - count]
                tall[r + 2, :, 0:cols] = jnp.where(inside, main, jnp.zeros_like(main))
                v = jnp.where(inside, v, jnp.zeros_like(v))
            tall[r + 2, :, cols:] = v

    def conv(source, weight, start, group):
        fields = [
            jnp.concatenate([source[start + i + d] for d in range(3)], axis=0)
            for i in range(group)
        ]
        return jnp.dot(weight, jnp.concatenate(fields, axis=1), preferred_element_type=F32)

    def first(step, carry):
        group = FIRST_ROWS
        start = step * group
        taps = conv(tall, w1_ref[...], start, group)
        for i in range(group):
            j = start + i
            value = silu(shifted_sum(taps[:, i * 2 * cols : (i + 1) * 2 * cols]) + b1)
            outside = jnp.logical_or(
                jnp.logical_and(j == 0, lat == 0),
                jnp.logical_and(j == count + 1, lat == lat_count - 1),
            )
            second[j] = jnp.where(outside, 0.0, value).astype(BF16)
        return carry

    lax.fori_loop(0, (count + 2) // FIRST_ROWS, first, 0)

    def last(step, carry):
        group = LAST_ROWS
        start = step * group
        taps = conv(second, w2_ref[...], start, group)
        rows = []
        for i in range(group):
            value = shifted_sum(taps[:, i * 2 * cols : (i + 1) * 2 * cols])[:, :cols]
            rows.append(a_ref[start + i].astype(F32) + (value + b2))
        block = jnp.swapaxes(jnp.stack(rows), 0, 1).astype(BF16)
        out_ref[:, pl.ds(pl.multiple_of(start, group), group), :] = block
        return carry

    lax.fori_loop(0, count // LAST_ROWS, last, 0)


def atmos_step(a, top, bottom, left, right, w1, b1, w2, b2, lat_count):
    count, channels, cols = a.shape
    vmem = pl.BlockSpec(memory_space=pltpu.VMEM)
    return pl.pallas_call(
        functools.partial(atmos_kernel, lat_count),
        out_shape=jax.ShapeDtypeStruct((channels, count, cols), BF16),
        in_specs=[vmem] * 9,
        out_specs=vmem,
        scratch_shapes=[
            pltpu.VMEM((count + 4, channels, 2 * cols), BF16),
            pltpu.VMEM((count + 2, channels, 2 * cols), BF16),
        ],
        compiler_params=pltpu.CompilerParams(vmem_limit_bytes=VMEM_LIMIT),
        name="atmos",
    )(a, top, bottom, left, right, w1, b1, w2, b2)


def per_device(
    ocean_state,
    sea_mask,
    ocean_w1,
    ocean_b1,
    ocean_w2,
    ocean_b2,
    regrid_weight,
    route_dev,
    route_row,
    atmos_state,
    atmos_w1,
    atmos_b1,
    atmos_w2,
    atmos_b2,
):
    lat_count, lon_count = lax.axis_size("lat"), lax.axis_size("lon")
    atmos_rows = atmos_state.shape[1]

    count = route_dev.size
    weights = (ocean_w1, ocean_w2, atmos_w1, atmos_w2)
    hidden, index, north_index, south_index, meta, overflow, *weights = ocean_halo(
        ocean_state,
        sea_mask,
        route_dev,
        route_row,
        weights,
        ocean_b1[None, :],
        lat_count,
        lon_count,
        atmos_rows,
    )
    ocean_next, slots = ocean_step(
        meta,
        hidden,
        sea_mask,
        weights[0],
        ocean_b2[None, :],
        regrid_weight.reshape(-1, 256, 128),
    )
    operands = (index, north_index, south_index, slots, atmos_state, overflow)
    *coupled, overflow = couple(operands, SHORT, EDGE_SHORT, 1, lat_count, lon_count)
    first, top, bottom, left, right = lax.cond(
        overflow[0] > 0,
        lambda short, operands: tuple(couple(operands, count, count, 2, lat_count, lon_count)[:5]),
        lambda short, operands: short,
        tuple(coupled),
        operands,
    )
    atmos_next = atmos_step(
        first,
        top,
        bottom,
        left,
        right,
        weights[1],
        atmos_b1[None, :],
        weights[2],
        atmos_b2[None, :],
        lat_count,
    )
    return ocean_next, atmos_next


def solution(mesh):
    in_specs = (
        P(None, "lat", "lon"),
        P("lat", "lon"),
        P(),
        P(),
        P(),
        P(),
        P(("lat", "lon"), None, None, None),
        P(("lat", "lon"), None),
        P(("lat", "lon"), None),
        P(None, "lat", "lon"),
        P(),
        P(),
        P(),
        P(),
    )
    out_specs = (P(None, "lat", "lon"), P(None, "lat", "lon"))
    return jax.shard_map(
        per_device, mesh=mesh, in_specs=in_specs, out_specs=out_specs, check_vma=False
    )
```

```python
import functools

import jax
import jax.numpy as jnp
from jax import lax
from jax.experimental import pallas as pl
from jax.experimental.pallas import tpu as pltpu
from jax.sharding import PartitionSpec as P

MESH = pl.DeviceIdType.MESH
F32 = jnp.float32
BF16 = jnp.bfloat16
GROUPS = 4
FIRST_ROWS = 22
LAST_ROWS = 32
SHORT = 32
EDGE_SHORT = 48


def silu(v):
    return 0.5 * v * (1.0 + jnp.tanh(0.5 * v))


def shifted_sum(taps):
    out = taps.shape[0] // 3
    columns = taps.shape[1]
    return (
        pltpu.roll(taps[0:out], 1, 1)
        + taps[out : 2 * out]
        + pltpu.roll(taps[2 * out :], columns - 1, 1)
    )


def stack_weight(weight_ref, out_ref):
    out, inn = weight_ref.shape[2:]
    padded = out_ref.shape[1] // 3
    for dc in range(3):
        pieces = []
        for dr in range(3):
            pieces.append(weight_ref[dr, dc].astype(F32))
            if padded > inn:
                pieces.append(jnp.zeros((out, padded - inn), F32))
        out_ref[dc * out : (dc + 1) * out, :] = jnp.concatenate(pieces, axis=1).astype(BF16)


def column(bias):
    n = bias.shape[1]
    at = lax.broadcasted_iota(jnp.int32, (n, n), 0) == lax.broadcasted_iota(jnp.int32, (n, n), 1)
    return jnp.sum(jnp.where(at, bias, jnp.zeros_like(bias)), axis=1, keepdims=True)


def remote(src, dst, send_sem, recv_sem, lat, lon):
    return pltpu.make_async_remote_copy(
        src_ref=src,
        dst_ref=dst,
        send_sem=send_sem,
        recv_sem=recv_sem,
        device_id={"lat": lat, "lon": lon},
        device_id_type=MESH,
    )


def landed(ref, sem):
    return pltpu.make_async_copy(ref, ref, sem)


def list_lons(lat, lon):
    across = lax.rem(lon + 2, 4)
    odd = lax.rem(lon, 2) == 1
    up = jnp.where(jnp.logical_and(odd, lax.rem(lat, 4) == 0), across, lon)
    down = jnp.where(jnp.logical_and(odd, lax.rem(lat, 4) == 3), across, lon)
    return up, down


def greet(partners):
    barrier = pltpu.get_barrier_semaphore()
    for lat, lon, ok in partners:

        @pl.when(ok)
        def _():
            pl.semaphore_signal(
                barrier, inc=1, device_id={"lat": lat, "lon": lon}, device_id_type=MESH
            )


def greeted(waits):
    pl.semaphore_wait(pltpu.get_barrier_semaphore(), waits)


def whole_any(count):
    return [pl.BlockSpec(memory_space=pl.ANY)] * count


def ocean_halo_kernel(
    lat_count,
    lon_count,
    atmos_rows,
    x_ref,
    mask_ref,
    dev_ref,
    row_ref,
    w1_ref,
    w2_ref,
    w3_ref,
    w4_ref,
    b1_ref,
    hidden,
    index,
    north_index,
    south_index,
    meta,
    overflow,
    w2_out,
    w3_out,
    w4_out,
    left,
    right,
    edges,
    tall,
    w1_out,
    send_sem,
    recv_sem,
):
    lat, lon = lax.axis_index("lat"), lax.axis_index("lon")
    inputs, rows, cols = x_ref.shape
    channels = tall.shape[1]
    west = lax.rem(lon + lon_count - 1, lon_count)
    east = lax.rem(lon + 1, lon_count)
    up, down, always = lat > 0, lat < lat_count - 1, lat >= 0
    edge = jnp.logical_or(lat == 0, lat == lat_count - 1)
    partners = [(lat, west, always), (lat, east, always)]
    for there, ok in ((lat - 1, up), (lat + 1, down)):
        partners += [(there, side, ok) for side in (west, lon, east)]
    up_lon, down_lon = list_lons(lat, lon)
    partners += [(lat - 1, up_lon, up), (lat + 1, down_lon, down)]
    greet(partners)

    keys = (dev_ref[...] - (lat - 1) * lon_count) * atmos_rows + row_ref[...]
    key = jnp.concatenate([keys[k : k + 1] for k in range(keys.shape[0])], axis=1)
    count = key.shape[1]
    key_down = column(key)
    blocks = keys.shape[1]
    across = lax.broadcasted_iota(jnp.int32, (count, count), 1)
    across = lax.rem(across, blocks) * keys.shape[0] + lax.div(across, blocks)
    along = lax.broadcasted_iota(jnp.int32, (count, count), 0)
    along = lax.rem(along, blocks) * keys.shape[0] + lax.div(along, blocks)
    again = jnp.logical_and(key_down == key, along < across).astype(jnp.int32)
    place = jnp.sum((key_down < key).astype(jnp.int32) + again, axis=0, keepdims=True)
    place_down = column(place)
    first_down = column(1 - jnp.max(again, axis=0, keepdims=True))
    lane = lax.broadcasted_iota(jnp.int32, (1, count), 1)
    meta[0:1, :] = place
    meta[1:2, :] = jnp.max(jnp.where(place_down == lane, first_down, 0), axis=0, keepdims=True)
    per_step = lon_count * atmos_rows
    for step in range(3):
        for row in range(8):
            if row * count < per_step:
                number = lane + (step * per_step + row * count)
                places = jnp.max(
                    jnp.where(key_down == number, place_down, -1), axis=0, keepdims=True
                )
                index[step, row : row + 1, :] = jnp.where(places < 0, count, places)
            else:
                index[step, row : row + 1, :] = jnp.full((1, count), count, jnp.int32)
    low = jnp.sum((key < per_step).astype(jnp.int32), axis=1, keepdims=True)
    high = jnp.sum((key >= 2 * per_step).astype(jnp.int32), axis=1, keepdims=True)
    most = jnp.where(edge, EDGE_SHORT, SHORT)
    long = (jnp.maximum(low, high) > most).astype(jnp.int32)
    overflow[...] = jnp.broadcast_to(long, overflow.shape)

    lane = lax.broadcasted_iota(jnp.int32, (channels, 128), 1)
    for q in range(cols // 128):
        part = slice(q * 128, (q + 1) * 128)
        block = jnp.concatenate(
            [
                x_ref[:, :, part].astype(F32),
                mask_ref[:, part].astype(F32)[None],
                jnp.zeros((channels - inputs - 1, rows, 128), F32),
            ],
            axis=0,
        )
        tall[2 : 2 + rows, :, part] = jnp.swapaxes(block, 0, 1).astype(BF16)
    tile = jnp.zeros((channels, 128), F32)
    for k in range(rows):
        low, high = tall[k + 2, :, 0:128], tall[k + 2, :, cols - 128 : cols]
        both = jnp.where(lane < 64, low, high).astype(F32)
        tile = jnp.where(lane // 4 == k, pltpu.roll(both, (4 * k + 2) % 128, 1), tile)
    edges[...] = tile.astype(BF16)

    stack_weight(w1_ref, w1_out)
    b1 = column(b1_ref[...])
    blank = jnp.zeros((2, channels, cols), BF16)

    @pl.when(jnp.logical_not(up))
    def _():
        tall[0:2, :, 0:cols] = blank

    @pl.when(jnp.logical_not(down))
    def _():
        tall[rows + 2 :, :, 0:cols] = blank

    greeted(jnp.where(edge, 6, 10))
    def two(start):
        return tall.at[pl.ds(start, 2), :, pl.ds(0, cols)]

    moves = [
        (edges, right.at[1], lat, west, always, always),
        (edges, left.at[1], lat, east, always, always),
        (edges, right.at[2], lat - 1, west, up, down),
        (edges, left.at[2], lat - 1, east, up, down),
        (edges, right.at[0], lat + 1, west, down, up),
        (edges, left.at[0], lat + 1, east, down, up),
        (index.at[0], south_index, lat - 1, up_lon, up, down),
        (index.at[2], north_index, lat + 1, down_lon, down, up),
        (two(2), two(rows + 2), lat - 1, lon, up, down),
        (two(rows), two(0), lat + 1, lon, down, up),
    ]
    copies = [
        remote(src, dst, send_sem.at[i], recv_sem.at[i], a, b)
        for i, (src, dst, a, b, _, _) in enumerate(moves)
    ]
    for copy, move in zip(copies, moves):
        pl.when(move[4])(copy.start)
    for weight, out in ((w2_ref, w2_out), (w3_ref, w3_out), (w4_ref, w4_out)):
        stack_weight(weight, out)

    def arrive(numbers):
        for i in numbers:
            pl.when(moves[i][5])(landed(moves[i][1], recv_sem.at[i]).wait)

    def sides(tile, some):
        both = jnp.where(lane % 4 < 2, left[tile], right[tile]).astype(F32)
        for k in some:
            side = pltpu.roll(both, (126 - 4 * k) % 128, 1).astype(BF16)
            if tile != 1:
                inside = lat > 0 if tile == 0 else lat < lat_count - 1
                side = jnp.where(inside, side, jnp.zeros_like(side))
            tall[(tile - 1) * rows + k + 2, :, cols:] = side

    def conv(some):
        for j in some:
            fields = jnp.concatenate([tall[j], tall[j + 1], tall[j + 2]], axis=0)
            taps = jnp.dot(w1_out[...], fields, preferred_element_type=F32)
            mask = tall[j + 1, inputs : inputs + 1, :].astype(F32)
            hidden[j] = (silu(shifted_sum(taps) + b1) * mask).astype(BF16)

    arrive((0, 1))
    sides(1, range(rows))
    conv(range(2, rows))
    arrive(range(2, len(moves)))
    sides(0, range(rows - 2, rows))
    sides(2, range(2))
    conv((0, 1, rows, rows + 1))
    for copy, move in zip(copies, moves):
        pl.when(move[4])(copy.wait_send)


def ocean_halo(x, sea_mask, route_dev, route_row, weights, b1, lat_count, lon_count, atmos_rows):
    inputs, rows, cols = x.shape
    channels = -(-(inputs + 1) // 16) * 16
    count = route_dev.size
    weights = [w.transpose(2, 3, 0, 1) for w in weights]
    stacked = [
        jax.ShapeDtypeStruct((3 * w.shape[2], 3 * (-(-w.shape[3] // 16) * 16)), BF16) for w in weights
    ]
    table = jax.ShapeDtypeStruct((8, count), jnp.int32)
    vmem = pl.BlockSpec(memory_space=pltpu.VMEM)
    out = weights[0].shape[2]
    return pl.pallas_call(
        functools.partial(ocean_halo_kernel, lat_count, lon_count, atmos_rows),
        out_shape=[
            jax.ShapeDtypeStruct((rows + 2, out, cols + 128), BF16),
            jax.ShapeDtypeStruct((3,) + table.shape, jnp.int32),
            table,
            table,
            jax.ShapeDtypeStruct((2, count), jnp.int32),
            table,
        ]
        + stacked[1:],
        in_specs=[vmem] * 9,
        out_specs=[vmem] * 2 + whole_any(2) + [vmem] * 5,
        scratch_shapes=[
            pltpu.VMEM((3, channels, 128), BF16),
            pltpu.VMEM((3, channels, 128), BF16),
            pltpu.VMEM((channels, 128), BF16),
            pltpu.VMEM((rows + 4, channels, cols + 128), BF16),
            pltpu.VMEM(stacked[0].shape, BF16),
            pltpu.SemaphoreType.DMA((10,)),
            pltpu.SemaphoreType.DMA((10,)),
        ],
        compiler_params=pltpu.CompilerParams(
            collective_id=0, has_side_effects=True, vmem_limit_bytes=24 * 1024 * 1024
        ),
        name="ocean_halo",
    )(x, sea_mask, route_dev.T, route_row.T, *weights, b1)


def ocean_kernel(
    meta, hidden, mask_ref, w2_ref, b2_ref, regrid, next_ref, slots_ref, listed, weights, kept, sem
):
    rows, cols = mask_ref.shape
    blocks = regrid.shape[0] // rows
    copies = []
    for r in range(rows):
        some = pl.ds(r * blocks, blocks)
        copies.append(pltpu.make_async_copy(regrid.at[some], weights.at[some], sem.at[r]))
        copies[r].start()
    b2 = column(b2_ref[...])
    for r in range(rows):
        field = jnp.concatenate([hidden[r], hidden[r + 1], hidden[r + 2]], axis=0)
        taps = jnp.dot(w2_ref[...], field, preferred_element_type=F32)
        result = (shifted_sum(taps)[:, :cols] + b2) * mask_ref[r : r + 1, :].astype(F32)
        kept[r] = result
        result = result.astype(BF16)
        copies[r].wait()
        for q in range(blocks):
            both = lax.dot_general(
                result[:, q * 128 : (q + 1) * 128],
                weights[r * blocks + q],
                (((1,), (1,)), ((), ())),
                preferred_element_type=F32,
            ).astype(BF16)
            for k in range(2):
                place = meta[0, k * (rows * blocks) + r * blocks + q]
                listed[place] = both[:, k * 128 : (k + 1) * 128]

    groups, slots, size = slots_ref.shape[:3]

    def add(i, run):
        value = listed[i].astype(F32)
        run = jnp.where(meta[1, i] == 1, value, run + value)
        for g in range(groups):
            slots_ref[g, i] = run[g * size : (g + 1) * size].astype(BF16)
        return run

    lax.fori_loop(0, slots, add, jnp.zeros(listed.shape[1:], F32), unroll=8)
    for q in range(cols // 128):
        part = slice(q * 128, (q + 1) * 128)
        block = jnp.stack([kept[r, :, part] for r in range(rows)])
        next_ref[:, :, part] = jnp.swapaxes(block, 0, 1).astype(BF16)


def ocean_step(meta, hidden, mask, w2, b2, regrid):
    rows, cols = mask.shape
    out = w2.shape[0] // 3
    slots = meta.shape[1]
    vmem = pl.BlockSpec(memory_space=pltpu.VMEM)
    return pl.pallas_call(
        ocean_kernel,
        out_shape=(
            jax.ShapeDtypeStruct((out, rows, cols), BF16),
            jax.ShapeDtypeStruct((GROUPS, slots, out // GROUPS, 128), BF16),
        ),
        in_specs=[pl.BlockSpec(memory_space=pltpu.SMEM)] + [vmem] * 4 + whole_any(1),
        out_specs=[vmem] * 2,
        scratch_shapes=[
            pltpu.VMEM((slots, out, 128), BF16),
            pltpu.VMEM(regrid.shape, BF16),
            pltpu.VMEM((rows, out, cols), F32),
            pltpu.SemaphoreType.DMA((rows,)),
        ],
        compiler_params=pltpu.CompilerParams(vmem_limit_bytes=52 * 1024 * 1024),
        name="ocean",
    )(meta, hidden, mask, w2, b2, regrid)


def couple_kernel(
    lat_count,
    lon_count,
    count,
    edge_count,
    own_index,
    north_index,
    south_index,
    slots,
    atmos,
    overflow,
    first,
    top,
    bottom,
    left,
    right,
    overflow_of_all,
    *scratch,
):
    lat, lon = lax.axis_index("lat"), lax.axis_index("lon")
    west = lax.rem(lon + lon_count - 1, lon_count)
    east = lax.rem(lon + 1, lon_count)
    across = lax.rem(lon + 2, lon_count)
    beside = lon + 1 - 2 * lax.rem(lon, 2)
    beside_across = lax.rem(beside + 2, lon_count)
    up, down, always = lat > 0, lat < lat_count - 1, lat >= 0
    edge = jnp.logical_or(lat == 0, lat == lat_count - 1)
    partners = [(lat, there, always) for there in (west, east, across)]
    for there, ok in ((lat - 1, up), (lat + 1, down)):
        partners += [(there, side, ok) for side in (west, lon, east)]
    four, inner = lat // 4, lax.rem(lat, 4)
    fours = lat_count // 4
    rounds = [
        [(lat, lax.rem(lon + k, lon_count)) for k in range(1, lon_count)],
        [(four * 4 + lax.rem(inner + k, 4), lon) for k in range(1, 4)],
        [(lax.rem(four + k, fours) * 4 + inner, lon) for k in range(1, fours)],
    ]
    partners += [(a, b, always) for peers in rounds[1:] for a, b in peers]
    up_lon, down_lon = list_lons(lat, lon)
    partners += [(lat - 1, up_lon, up), (lat + 1, down_lon, down)]
    greet(partners)

    groups, total, size, cols = slots.shape
    rows, channels = first.shape[:2]
    own, north, south = (scratch[i * groups : (i + 1) * groups] for i in range(3))
    away, mine, from_core, to_z, from_z, edges = scratch[3 * groups : 3 * groups + 6]
    load_sem, y_send, y_recv, core_send, core_recv, z_send, z_recv, halo_send, halo_recv = scratch[
        3 * groups + 6 : 3 * groups + 15
    ]
    gathered, partial, max_send, max_recv, base = scratch[3 * groups + 15 :]
    held, waiting, small = overflow, [], []

    def send_maximum(number):
        begin = sum(len(peers) for peers in rounds[:number])
        for i, (a, b) in enumerate(rounds[number], begin):
            small.append(remote(held, gathered.at[i], max_send.at[i], max_recv.at[i], a, b))
            small[-1].start()
            waiting.append(i)

    def receive_maximum(target):
        value = held[...]
        for i in waiting:
            landed(gathered.at[i], max_recv.at[i]).wait()
            value = jnp.maximum(value, gathered[i])
        waiting.clear()
        if target is None:
            overflow_of_all[0] = jnp.max(value)
        else:
            target[...] = value
        return target

    everything = pl.ds(0, total)
    loads = []
    for g in range(groups):
        loads.append(
            pltpu.make_async_copy(slots.at[g], own[g].at[everything], load_sem.at[g])
        )
        loads[g].start()
    for buffer in (own, north, south):
        for g in range(groups):
            buffer[g][total] = jnp.zeros((size, cols), BF16)
    for at in range(0, rows, 16):
        block = atmos[:, at : at + 16, :].astype(F32)
        base[at : at + 16] = jnp.swapaxes(block, 0, 1).astype(BF16)
    greeted(jnp.where(edge, 7, 11) + sum(len(peers) for peers in rounds[1:]))
    send_maximum(0)

    last = lat_count - 1
    lists = []
    for g in range(groups):
        lists.append([])
        for length, sends_down, sends_up, north_comes, south_comes in (
            (count, lat > 0, lat < last, lat > 1, lat < last - 1),
            (edge_count, lat == 0, lat == last, lat == 1, lat == last - 1),
        ):
            low, high = pl.ds(0, length), pl.ds(total - length, length)
            lists[g] += [
                (
                    remote(
                        slots.at[g, high],
                        north[g].at[high],
                        y_send.at[0, g],
                        y_recv.at[0, g],
                        lat + 1,
                        down_lon,
                    ),
                    landed(north[g].at[high], y_recv.at[0, g]),
                    jnp.logical_and(down, sends_down),
                    jnp.logical_and(up, north_comes),
                ),
                (
                    remote(
                        slots.at[g, low],
                        south[g].at[low],
                        y_send.at[1, g],
                        y_recv.at[1, g],
                        lat - 1,
                        up_lon,
                    ),
                    landed(south[g].at[low], y_recv.at[1, g]),
                    jnp.logical_and(up, sends_up),
                    jnp.logical_and(down, south_comes),
                ),
            ]
        for copy, _, sends, _ in lists[g]:
            pl.when(sends)(copy.start)

    def dense(g, lon_there, store):
        def row(t, carry):
            at = lon_there * rows + t
            i, j = at // 128, lax.rem(at, 128)
            a = own_index[1, i, j]
            b = jnp.where(up, north_index[i, j], total)
            c = jnp.where(down, south_index[i, j], total)
            value = own[g][a].astype(F32) + north[g][b].astype(F32) + south[g][c].astype(F32)
            store(t, value.astype(BF16))
            return carry

        lax.fori_loop(0, rows, row, 0, unroll=8)

    core_copies, z_copies = [], []
    for g in range(groups):
        loads[g].wait()
        for _, arrival, _, comes in lists[g]:
            pl.when(comes)(arrival.wait)
        for part, (theirs, ours) in enumerate(((beside_across, across), (beside, lon))):

            def put_away(t, value):
                away[part, g, t] = value

            def put_mine(t, value):
                mine[part, g, t] = value

            dense(g, theirs, put_away)
            copy = remote(
                away.at[part, g],
                from_core.at[part, g],
                core_send.at[part, g],
                core_recv.at[part, g],
                lat,
                beside,
            )
            copy.start()
            core_copies.append(copy)
            dense(g, ours, put_mine)
            if part == 0:
                landed(from_core.at[0, g], core_recv.at[0, g]).wait()
                to_z[g] = (mine[0, g].astype(F32) + from_core[0, g].astype(F32)).astype(BF16)
                copy = remote(
                    to_z.at[g], from_z.at[g], z_send.at[g], z_recv.at[g], lat, across
                )
                copy.start()
                z_copies.append(copy)
        if g < 2:
            held = receive_maximum(partial.at[g])
            send_maximum(g + 1)

    lane = lax.broadcasted_iota(jnp.int32, (size, cols), 1)
    tiles = edges.shape[0]
    for g in range(groups):
        landed(from_core.at[1, g], core_recv.at[1, g]).wait()
        landed(from_z.at[g], z_recv.at[g]).wait()
        part = pl.ds(g * size, size)
        for tile in range(tiles):
            edge = jnp.zeros((size, cols), F32)
            for k in range(32):
                r = tile * 32 + k
                flux = (
                    mine[1, g, r].astype(F32)
                    + from_core[1, g, r].astype(F32)
                    + from_z[g, r].astype(F32)
                )
                v = (base[r, part].astype(F32) + flux).astype(BF16)
                first[r, part] = v
                rolled = pltpu.roll(v.astype(F32), (4 * k + 2) % cols, 1)
                edge = jnp.where(lane // 4 == k, rolled, edge)
            edges[tile, part] = edge.astype(BF16)
    lo, hi = edges.at[0], edges.at[tiles - 1]
    moves = [
        (edges, right.at[pl.ds(1, tiles)], lat, west, always, always),
        (edges, left.at[pl.ds(1, tiles)], lat, east, always, always),
        (first.at[pl.ds(0, 2)], bottom, lat - 1, lon, up, down),
        (first.at[pl.ds(rows - 2, 2)], top, lat + 1, lon, down, up),
        (lo, right.at[tiles + 1], lat - 1, west, up, down),
        (lo, left.at[tiles + 1], lat - 1, east, up, down),
        (hi, right.at[0], lat + 1, west, down, up),
        (hi, left.at[0], lat + 1, east, down, up),
    ]
    copies = [
        remote(src, dst, halo_send.at[i], halo_recv.at[i], a, b)
        for i, (src, dst, a, b, _, _) in enumerate(moves)
    ]
    for copy, move in zip(copies, moves):
        pl.when(move[4])(copy.start)
    receive_maximum(None)
    for copy in core_copies + z_copies + small:
        copy.wait_send()
    for g in range(groups):
        for copy, _, sends, _ in lists[g]:
            pl.when(sends)(copy.wait_send)
    for i, (copy, move) in enumerate(zip(copies, moves)):
        pl.when(move[4])(copy.wait_send)
        pl.when(move[5])(landed(move[1], halo_recv.at[i]).wait)


def couple(operands, count, edge_count, collective_id, lat_count, lon_count):
    _, _, _, slots, atmos, overflow = operands
    groups, total, size, cols = slots.shape
    channels, rows, cols = atmos.shape
    tiles = rows // 32
    vmem = pl.BlockSpec(memory_space=pltpu.VMEM)
    smem = pl.BlockSpec(memory_space=pltpu.SMEM)
    dma = pltpu.SemaphoreType.DMA
    shapes = [(rows, channels, cols)] + [(2, channels, cols)] * 2 + [(tiles + 2, channels, cols)] * 2
    received = pltpu.VMEM((total + 1, size, cols), BF16)
    peers = lon_count - 1 + 3 + lat_count // 4 - 1
    one = pltpu.VMEM((groups, rows, size, cols), BF16)
    two = pltpu.VMEM((2, groups, rows, size, cols), BF16)
    return pl.pallas_call(
        functools.partial(couple_kernel, lat_count, lon_count, count, edge_count),
        out_shape=[jax.ShapeDtypeStruct(s, BF16) for s in shapes]
        + [jax.ShapeDtypeStruct((1,), jnp.int32)],
        in_specs=[smem] * 3 + whole_any(1) + [vmem] * 2,
        out_specs=[vmem] + whole_any(4) + [smem],
        scratch_shapes=[received] * (3 * groups)
        + [two] * 3
        + [one] * 2
        + [pltpu.VMEM((tiles, channels, cols), BF16)]
        + [dma((groups,))]
        + [dma((2, groups))] * 4
        + [dma((groups,))] * 2
        + [dma((8,))] * 2
        + [pltpu.VMEM((peers,) + overflow.shape, jnp.int32)]
        + [pltpu.VMEM((2,) + overflow.shape, jnp.int32)]
        + [dma((peers,))] * 2
        + [pltpu.VMEM((rows, channels, cols), BF16)],
        compiler_params=pltpu.CompilerParams(
            collective_id=collective_id, has_side_effects=True, vmem_limit_bytes=40 * 1024 * 1024
        ),
        name="couple",
    )(*operands)


def atmos_kernel(
    lat_count, a_ref, top_ref, bottom_ref, left_ref, right_ref, w1_ref, b1_ref, w2_ref, b2_ref, out_ref, tall, second
):
    count, channels, cols = a_ref.shape
    lat = lax.axis_index("lat")
    b1, b2 = column(b1_ref[...]), column(b2_ref[...])

    tall[2 : 2 + count, :, 0:cols] = a_ref[...]
    lane = lax.broadcasted_iota(jnp.int32, (channels, cols), 1)
    for tile in range(count // 32 + 2):
        side = jnp.where(lane % 4 < 2, left_ref[tile], right_ref[tile]).astype(F32)
        for k in range(32):
            r = tile * 32 - 32 + k
            if r < -2 or r >= count + 2:
                continue
            v = pltpu.roll(side, (126 - 4 * k) % cols, 1).astype(BF16)
            if r < 0 or r >= count:
                inside = lat > 0 if r < 0 else lat < lat_count - 1
                main = top_ref[r + 2] if r < 0 else bottom_ref[r - count]
                tall[r + 2, :, 0:cols] = jnp.where(inside, main, jnp.zeros_like(main))
                v = jnp.where(inside, v, jnp.zeros_like(v))
            tall[r + 2, :, cols:] = v

    def conv(source, weight, start, group):
        fields = [
            jnp.concatenate([source[start + i + d] for d in range(3)], axis=0)
            for i in range(group)
        ]
        return jnp.dot(weight, jnp.concatenate(fields, axis=1), preferred_element_type=F32)

    def first(step, carry):
        group = FIRST_ROWS
        start = step * group
        taps = conv(tall, w1_ref[...], start, group)
        for i in range(group):
            j = start + i
            value = silu(shifted_sum(taps[:, i * 2 * cols : (i + 1) * 2 * cols]) + b1)
            outside = jnp.logical_or(
                jnp.logical_and(j == 0, lat == 0),
                jnp.logical_and(j == count + 1, lat == lat_count - 1),
            )
            second[j] = jnp.where(outside, 0.0, value).astype(BF16)
        return carry

    lax.fori_loop(0, (count + 2) // FIRST_ROWS, first, 0)

    def last(step, carry):
        group = LAST_ROWS
        start = step * group
        taps = conv(second, w2_ref[...], start, group)
        rows = []
        for i in range(group):
            value = shifted_sum(taps[:, i * 2 * cols : (i + 1) * 2 * cols])[:, :cols]
            rows.append(a_ref[start + i].astype(F32) + (value + b2))
        block = jnp.swapaxes(jnp.stack(rows), 0, 1).astype(BF16)
        out_ref[:, pl.ds(pl.multiple_of(start, group), group), :] = block
        return carry

    lax.fori_loop(0, count // LAST_ROWS, last, 0)


def atmos_step(a, top, bottom, left, right, w1, b1, w2, b2, lat_count):
    count, channels, cols = a.shape
    vmem = pl.BlockSpec(memory_space=pltpu.VMEM)
    return pl.pallas_call(
        functools.partial(atmos_kernel, lat_count),
        out_shape=jax.ShapeDtypeStruct((channels, count, cols), BF16),
        in_specs=[vmem] * 9,
        out_specs=vmem,
        scratch_shapes=[
            pltpu.VMEM((count + 4, channels, 2 * cols), BF16),
            pltpu.VMEM((count + 2, channels, 2 * cols), BF16),
        ],
        compiler_params=pltpu.CompilerParams(vmem_limit_bytes=40 * 1024 * 1024),
        name="atmos",
    )(a, top, bottom, left, right, w1, b1, w2, b2)


def per_device(
    ocean_state,
    sea_mask,
    ocean_w1,
    ocean_b1,
    ocean_w2,
    ocean_b2,
    regrid_weight,
    route_dev,
    route_row,
    atmos_state,
    atmos_w1,
    atmos_b1,
    atmos_w2,
    atmos_b2,
):
    lat_count, lon_count = lax.axis_size("lat"), lax.axis_size("lon")
    atmos_rows = atmos_state.shape[1]

    count = route_dev.size
    weights = (ocean_w1, ocean_w2, atmos_w1, atmos_w2)
    hidden, index, north_index, south_index, meta, overflow, *weights = ocean_halo(
        ocean_state,
        sea_mask,
        route_dev,
        route_row,
        weights,
        ocean_b1[None, :],
        lat_count,
        lon_count,
        atmos_rows,
    )
    ocean_next, slots = ocean_step(
        meta,
        hidden,
        sea_mask,
        weights[0],
        ocean_b2[None, :],
        regrid_weight.reshape(-1, 256, 128),
    )
    operands = (index, north_index, south_index, slots, atmos_state, overflow)
    *coupled, overflow = couple(operands, SHORT, EDGE_SHORT, 1, lat_count, lon_count)
    first, top, bottom, left, right = lax.cond(
        overflow[0] > 0,
        lambda short, operands: tuple(couple(operands, count, count, 2, lat_count, lon_count)[:5]),
        lambda short, operands: short,
        tuple(coupled),
        operands,
    )
    atmos_next = atmos_step(
        first,
        top,
        bottom,
        left,
        right,
        weights[1],
        atmos_b1[None, :],
        weights[2],
        atmos_b2[None, :],
        lat_count,
    )
    return ocean_next, atmos_next


def solution(mesh):
    in_specs = (
        P(None, "lat", "lon"),
        P("lat", "lon"),
        P(),
        P(),
        P(),
        P(),
        P(("lat", "lon"), None, None, None),
        P(("lat", "lon"), None),
        P(("lat", "lon"), None),
        P(None, "lat", "lon"),
        P(),
        P(),
        P(),
        P(),
    )
    out_specs = (P(None, "lat", "lon"), P(None, "lat", "lon"))
    return jax.shard_map(
        per_device, mesh=mesh, in_specs=in_specs, out_specs=out_specs, check_vma=False
    )
```

```python
import functools

import jax
import jax.numpy as jnp
from jax import lax
from jax.experimental import pallas as pl
from jax.experimental.pallas import tpu as pltpu
from jax.sharding import PartitionSpec as P

MESH = pl.DeviceIdType.MESH
F32 = jnp.float32
BF16 = jnp.bfloat16
VMEM_LIMIT = 56 * 1024 * 1024
GROUPS = 4
FIRST_ROWS = 22
LAST_ROWS = 32
SHORT = 32
EDGE_SHORT = 48


def silu(v):
    return 0.5 * v * (1.0 + jnp.tanh(0.5 * v))


def shifted_sum(taps):
    out = taps.shape[0] // 3
    columns = taps.shape[1]
    return (
        pltpu.roll(taps[0:out], 1, 1)
        + taps[out : 2 * out]
        + pltpu.roll(taps[2 * out :], columns - 1, 1)
    )


def stack_weight(weight_ref, out_ref):
    out, inn = weight_ref.shape[2:]
    padded = out_ref.shape[1] // 3
    for dc in range(3):
        pieces = []
        for dr in range(3):
            pieces.append(weight_ref[dr, dc].astype(F32))
            if padded > inn:
                pieces.append(jnp.zeros((out, padded - inn), F32))
        out_ref[dc * out : (dc + 1) * out, :] = jnp.concatenate(pieces, axis=1).astype(BF16)


def column(bias):
    n = bias.shape[1]
    at = lax.broadcasted_iota(jnp.int32, (n, n), 0) == lax.broadcasted_iota(jnp.int32, (n, n), 1)
    return jnp.sum(jnp.where(at, bias, jnp.zeros_like(bias)), axis=1, keepdims=True)


def remote(src, dst, send_sem, recv_sem, lat, lon):
    return pltpu.make_async_remote_copy(
        src_ref=src,
        dst_ref=dst,
        send_sem=send_sem,
        recv_sem=recv_sem,
        device_id={"lat": lat, "lon": lon},
        device_id_type=MESH,
    )


def landed(ref, sem):
    return pltpu.make_async_copy(ref, ref, sem)


def list_lons(lat, lon):
    across = lax.rem(lon + 2, 4)
    odd = lax.rem(lon, 2) == 1
    up = jnp.where(jnp.logical_and(odd, lax.rem(lat, 4) == 0), across, lon)
    down = jnp.where(jnp.logical_and(odd, lax.rem(lat, 4) == 3), across, lon)
    return up, down


def greet(partners):
    barrier = pltpu.get_barrier_semaphore()
    for lat, lon, ok in partners:

        @pl.when(ok)
        def _():
            pl.semaphore_signal(
                barrier, inc=1, device_id={"lat": lat, "lon": lon}, device_id_type=MESH
            )


def greeted(waits):
    pl.semaphore_wait(pltpu.get_barrier_semaphore(), waits)


def whole_any(count):
    return [pl.BlockSpec(memory_space=pl.ANY)] * count


def ocean_halo_kernel(
    lat_count,
    lon_count,
    atmos_rows,
    x_hbm,
    mask_hbm,
    w1_hbm,
    w2_hbm,
    w3_hbm,
    w4_hbm,
    dev_ref,
    row_ref,
    b1_ref,
    hidden,
    index,
    north_index,
    south_index,
    meta,
    overflow,
    w2_out,
    w3_out,
    w4_out,
    left,
    right,
    edges,
    tall,
    w1_out,
    x_ref,
    mask_ref,
    w1_ref,
    w2_ref,
    w3_ref,
    w4_ref,
    load_sem,
    send_sem,
    recv_sem,
):
    lat, lon = lax.axis_index("lat"), lax.axis_index("lon")
    inputs, rows, cols = x_ref.shape
    channels = tall.shape[1]
    west = lax.rem(lon + lon_count - 1, lon_count)
    east = lax.rem(lon + 1, lon_count)
    up, down, always = lat > 0, lat < lat_count - 1, lat >= 0
    edge = jnp.logical_or(lat == 0, lat == lat_count - 1)
    partners = [(lat, west, always), (lat, east, always)]
    for there, ok in ((lat - 1, up), (lat + 1, down)):
        partners += [(there, side, ok) for side in (west, lon, east)]
    up_lon, down_lon = list_lons(lat, lon)
    partners += [(lat - 1, up_lon, up), (lat + 1, down_lon, down)]
    greet(partners)
    loads = []
    for src, dst in (
        (x_hbm, x_ref),
        (mask_hbm, mask_ref),
        (w1_hbm, w1_ref),
        (w2_hbm, w2_ref),
        (w3_hbm, w3_ref),
        (w4_hbm, w4_ref),
    ):
        loads.append(pltpu.make_async_copy(src, dst, load_sem.at[len(loads)]))
        loads[-1].start()

    keys = (dev_ref[...] - (lat - 1) * lon_count) * atmos_rows + row_ref[...]
    key = jnp.concatenate([keys[k : k + 1] for k in range(keys.shape[0])], axis=1)
    count = key.shape[1]
    key_down = column(key)
    blocks = keys.shape[1]
    across = lax.broadcasted_iota(jnp.int32, (count, count), 1)
    across = lax.rem(across, blocks) * keys.shape[0] + lax.div(across, blocks)
    along = lax.broadcasted_iota(jnp.int32, (count, count), 0)
    along = lax.rem(along, blocks) * keys.shape[0] + lax.div(along, blocks)
    again = jnp.logical_and(key_down == key, along < across).astype(jnp.int32)
    place = jnp.sum((key_down < key).astype(jnp.int32) + again, axis=0, keepdims=True)
    place_down = column(place)
    first_down = column(1 - jnp.max(again, axis=0, keepdims=True))
    lane = lax.broadcasted_iota(jnp.int32, (1, count), 1)
    meta[0:1, :] = place
    meta[1:2, :] = jnp.max(jnp.where(place_down == lane, first_down, 0), axis=0, keepdims=True)
    per_step = lon_count * atmos_rows
    for step in range(3):
        for row in range(8):
            if row * count < per_step:
                number = lane + (step * per_step + row * count)
                places = jnp.max(
                    jnp.where(key_down == number, place_down, -1), axis=0, keepdims=True
                )
                index[step, row : row + 1, :] = jnp.where(places < 0, count, places)
            else:
                index[step, row : row + 1, :] = jnp.full((1, count), count, jnp.int32)
    low = jnp.sum((key < per_step).astype(jnp.int32), axis=1, keepdims=True)
    high = jnp.sum((key >= 2 * per_step).astype(jnp.int32), axis=1, keepdims=True)
    most = jnp.where(edge, EDGE_SHORT, SHORT)
    long = (jnp.maximum(low, high) > most).astype(jnp.int32)
    overflow[...] = jnp.broadcast_to(long, overflow.shape)

    lane = lax.broadcasted_iota(jnp.int32, (channels, 128), 1)
    loads[0].wait()
    loads[1].wait()
    for q in range(cols // 128):
        part = slice(q * 128, (q + 1) * 128)
        block = jnp.concatenate(
            [
                x_ref[:, :, part].astype(F32),
                mask_ref[:, part].astype(F32)[None],
                jnp.zeros((channels - inputs - 1, rows, 128), F32),
            ],
            axis=0,
        )
        tall[2 : 2 + rows, :, part] = jnp.swapaxes(block, 0, 1).astype(BF16)
    tile = jnp.zeros((channels, 128), F32)
    for k in range(rows):
        low, high = tall[k + 2, :, 0:128], tall[k + 2, :, cols - 128 : cols]
        both = jnp.where(lane < 64, low, high).astype(F32)
        tile = jnp.where(lane // 4 == k, pltpu.roll(both, (4 * k + 2) % 128, 1), tile)
    edges[...] = tile.astype(BF16)

    loads[2].wait()
    stack_weight(w1_ref, w1_out)
    b1 = column(b1_ref[...])
    blank = jnp.zeros((2, channels, cols), BF16)

    @pl.when(jnp.logical_not(up))
    def _():
        tall[0:2, :, 0:cols] = blank

    @pl.when(jnp.logical_not(down))
    def _():
        tall[rows + 2 :, :, 0:cols] = blank

    greeted(jnp.where(edge, 6, 10))
    def two(start):
        return tall.at[pl.ds(start, 2), :, pl.ds(0, cols)]

    moves = [
        (edges, right.at[1], lat, west, always, always),
        (edges, left.at[1], lat, east, always, always),
        (edges, right.at[2], lat - 1, west, up, down),
        (edges, left.at[2], lat - 1, east, up, down),
        (edges, right.at[0], lat + 1, west, down, up),
        (edges, left.at[0], lat + 1, east, down, up),
        (index.at[0], south_index, lat - 1, up_lon, up, down),
        (index.at[2], north_index, lat + 1, down_lon, down, up),
        (two(2), two(rows + 2), lat - 1, lon, up, down),
        (two(rows), two(0), lat + 1, lon, down, up),
    ]
    copies = [
        remote(src, dst, send_sem.at[i], recv_sem.at[i], a, b)
        for i, (src, dst, a, b, _, _) in enumerate(moves)
    ]
    for copy, move in zip(copies, moves):
        pl.when(move[4])(copy.start)
    for load in loads[3:]:
        load.wait()
    for weight, out in ((w2_ref, w2_out), (w3_ref, w3_out), (w4_ref, w4_out)):
        stack_weight(weight, out)

    def arrive(numbers):
        for i in numbers:
            pl.when(moves[i][5])(landed(moves[i][1], recv_sem.at[i]).wait)

    def sides(tile, some):
        both = jnp.where(lane % 4 < 2, left[tile], right[tile]).astype(F32)
        for k in some:
            side = pltpu.roll(both, (126 - 4 * k) % 128, 1).astype(BF16)
            if tile != 1:
                inside = lat > 0 if tile == 0 else lat < lat_count - 1
                side = jnp.where(inside, side, jnp.zeros_like(side))
            tall[(tile - 1) * rows + k + 2, :, cols:] = side

    def conv(some):
        for j in some:
            fields = jnp.concatenate([tall[j], tall[j + 1], tall[j + 2]], axis=0)
            taps = jnp.dot(w1_out[...], fields, preferred_element_type=F32)
            mask = tall[j + 1, inputs : inputs + 1, :].astype(F32)
            hidden[j] = (silu(shifted_sum(taps) + b1) * mask).astype(BF16)

    arrive((0, 1))
    sides(1, range(rows))
    conv(range(2, rows))
    arrive(range(2, len(moves)))
    sides(0, range(rows - 2, rows))
    sides(2, range(2))
    conv((0, 1, rows, rows + 1))
    for copy, move in zip(copies, moves):
        pl.when(move[4])(copy.wait_send)


def ocean_halo(x, sea_mask, route_dev, route_row, weights, b1, lat_count, lon_count, atmos_rows):
    inputs, rows, cols = x.shape
    channels = -(-(inputs + 1) // 16) * 16
    count = route_dev.size
    weights = [w.transpose(2, 3, 0, 1) for w in weights]
    stacked = [
        jax.ShapeDtypeStruct((3 * w.shape[2], 3 * (-(-w.shape[3] // 16) * 16)), BF16) for w in weights
    ]
    table = jax.ShapeDtypeStruct((8, count), jnp.int32)
    vmem = pl.BlockSpec(memory_space=pltpu.VMEM)
    out = weights[0].shape[2]
    return pl.pallas_call(
        functools.partial(ocean_halo_kernel, lat_count, lon_count, atmos_rows),
        out_shape=[
            jax.ShapeDtypeStruct((rows + 2, out, cols + 128), BF16),
            jax.ShapeDtypeStruct((3,) + table.shape, jnp.int32),
            table,
            table,
            jax.ShapeDtypeStruct((2, count), jnp.int32),
            table,
        ]
        + stacked[1:],
        in_specs=whole_any(6) + [vmem] * 3,
        out_specs=[vmem] * 2 + whole_any(2) + [vmem] * 5,
        scratch_shapes=[
            pltpu.VMEM((3, channels, 128), BF16),
            pltpu.VMEM((3, channels, 128), BF16),
            pltpu.VMEM((channels, 128), BF16),
            pltpu.VMEM((rows + 4, channels, cols + 128), BF16),
            pltpu.VMEM(stacked[0].shape, BF16),
            pltpu.VMEM(x.shape, BF16),
            pltpu.VMEM(sea_mask.shape, jnp.int32),
            *[pltpu.VMEM(w.shape, BF16) for w in weights],
            pltpu.SemaphoreType.DMA((6,)),
            pltpu.SemaphoreType.DMA((10,)),
            pltpu.SemaphoreType.DMA((10,)),
        ],
        compiler_params=pltpu.CompilerParams(
            collective_id=0, has_side_effects=True, vmem_limit_bytes=VMEM_LIMIT
        ),
        name="ocean_halo",
    )(x, sea_mask, *weights, route_dev.T, route_row.T, b1)


def ocean_kernel(
    meta, hidden, mask_ref, w2_ref, b2_ref, regrid, next_ref, slots_ref, listed, weights, kept, sem
):
    rows, cols = mask_ref.shape
    blocks = regrid.shape[0] // rows
    copies = []
    for r in range(rows):
        some = pl.ds(r * blocks, blocks)
        copies.append(pltpu.make_async_copy(regrid.at[some], weights.at[some], sem.at[r]))
        copies[r].start()
    b2 = column(b2_ref[...])
    for r in range(rows):
        field = jnp.concatenate([hidden[r], hidden[r + 1], hidden[r + 2]], axis=0)
        taps = jnp.dot(w2_ref[...], field, preferred_element_type=F32)
        result = (shifted_sum(taps)[:, :cols] + b2) * mask_ref[r : r + 1, :].astype(F32)
        kept[r] = result
        result = result.astype(BF16)
        copies[r].wait()
        for q in range(blocks):
            both = lax.dot_general(
                result[:, q * 128 : (q + 1) * 128],
                weights[r * blocks + q],
                (((1,), (1,)), ((), ())),
                preferred_element_type=F32,
            ).astype(BF16)
            for k in range(2):
                place = meta[0, k * (rows * blocks) + r * blocks + q]
                listed[place] = both[:, k * 128 : (k + 1) * 128]

    groups, slots, size = slots_ref.shape[:3]

    def add(i, run):
        value = listed[i].astype(F32)
        run = jnp.where(meta[1, i] == 1, value, run + value)
        for g in range(groups):
            slots_ref[g, i] = run[g * size : (g + 1) * size].astype(BF16)
        return run

    lax.fori_loop(0, slots, add, jnp.zeros(listed.shape[1:], F32), unroll=8)
    for q in range(cols // 128):
        part = slice(q * 128, (q + 1) * 128)
        block = jnp.stack([kept[r, :, part] for r in range(rows)])
        next_ref[:, :, part] = jnp.swapaxes(block, 0, 1).astype(BF16)


def ocean_step(meta, hidden, mask, w2, b2, regrid):
    rows, cols = mask.shape
    out = w2.shape[0] // 3
    slots = meta.shape[1]
    vmem = pl.BlockSpec(memory_space=pltpu.VMEM)
    return pl.pallas_call(
        ocean_kernel,
        out_shape=(
            jax.ShapeDtypeStruct((out, rows, cols), BF16),
            jax.ShapeDtypeStruct((GROUPS, slots, out // GROUPS, 128), BF16),
        ),
        in_specs=[pl.BlockSpec(memory_space=pltpu.SMEM)] + [vmem] * 4 + whole_any(1),
        out_specs=[vmem] * 2,
        scratch_shapes=[
            pltpu.VMEM((slots, out, 128), BF16),
            pltpu.VMEM(regrid.shape, BF16),
            pltpu.VMEM((rows, out, cols), F32),
            pltpu.SemaphoreType.DMA((rows,)),
        ],
        compiler_params=pltpu.CompilerParams(vmem_limit_bytes=VMEM_LIMIT),
        name="ocean",
    )(meta, hidden, mask, w2, b2, regrid)


def couple_kernel(
    lat_count,
    lon_count,
    count,
    edge_count,
    own_index,
    north_index,
    south_index,
    slots,
    atmos_hbm,
    overflow_hbm,
    first,
    top,
    bottom,
    left,
    right,
    overflow_of_all,
    *scratch,
):
    lat, lon = lax.axis_index("lat"), lax.axis_index("lon")
    west = lax.rem(lon + lon_count - 1, lon_count)
    east = lax.rem(lon + 1, lon_count)
    across = lax.rem(lon + 2, lon_count)
    beside = lon + 1 - 2 * lax.rem(lon, 2)
    beside_across = lax.rem(beside + 2, lon_count)
    up, down, always = lat > 0, lat < lat_count - 1, lat >= 0
    edge = jnp.logical_or(lat == 0, lat == lat_count - 1)
    partners = [(lat, there, always) for there in (west, east, across)]
    for there, ok in ((lat - 1, up), (lat + 1, down)):
        partners += [(there, side, ok) for side in (west, lon, east)]
    four, inner = lat // 4, lax.rem(lat, 4)
    fours = lat_count // 4
    rounds = [
        [(lat, lax.rem(lon + k, lon_count)) for k in range(1, lon_count)],
        [(four * 4 + lax.rem(inner + k, 4), lon) for k in range(1, 4)],
        [(lax.rem(four + k, fours) * 4 + inner, lon) for k in range(1, fours)],
    ]
    partners += [(a, b, always) for peers in rounds[1:] for a, b in peers]
    up_lon, down_lon = list_lons(lat, lon)
    partners += [(lat - 1, up_lon, up), (lat + 1, down_lon, down)]
    greet(partners)

    groups, total, size, cols = slots.shape
    rows, channels = first.shape[:2]
    own, north, south = (scratch[i * groups : (i + 1) * groups] for i in range(3))
    away, mine, from_core, to_z, from_z, edges = scratch[3 * groups : 3 * groups + 6]
    load_sem, y_send, y_recv, core_send, core_recv, z_send, z_recv, halo_send, halo_recv = scratch[
        3 * groups + 6 : 3 * groups + 15
    ]
    gathered, partial, max_send, max_recv, base = scratch[3 * groups + 15 : 3 * groups + 20]
    atmos, overflow, more_sem = scratch[3 * groups + 20 :]
    atmos_load = pltpu.make_async_copy(atmos_hbm, atmos, more_sem.at[0])
    overflow_load = pltpu.make_async_copy(overflow_hbm, overflow, more_sem.at[1])
    atmos_load.start()
    overflow_load.start()
    held, waiting, small = overflow, [], []

    def send_maximum(number):
        begin = sum(len(peers) for peers in rounds[:number])
        for i, (a, b) in enumerate(rounds[number], begin):
            small.append(remote(held, gathered.at[i], max_send.at[i], max_recv.at[i], a, b))
            small[-1].start()
            waiting.append(i)

    def receive_maximum(target):
        value = held[...]
        for i in waiting:
            landed(gathered.at[i], max_recv.at[i]).wait()
            value = jnp.maximum(value, gathered[i])
        waiting.clear()
        if target is None:
            overflow_of_all[0] = jnp.max(value)
        else:
            target[...] = value
        return target

    everything = pl.ds(0, total)
    loads = []
    for g in range(groups):
        loads.append(
            pltpu.make_async_copy(slots.at[g], own[g].at[everything], load_sem.at[g])
        )
        loads[g].start()
    for buffer in (own, north, south):
        for g in range(groups):
            buffer[g][total] = jnp.zeros((size, cols), BF16)
    atmos_load.wait()
    overflow_load.wait()
    for at in range(0, rows, 16):
        block = atmos[:, at : at + 16, :].astype(F32)
        base[at : at + 16] = jnp.swapaxes(block, 0, 1).astype(BF16)
    greeted(jnp.where(edge, 7, 11) + sum(len(peers) for peers in rounds[1:]))
    send_maximum(0)

    last = lat_count - 1
    lists = []
    for g in range(groups):
        lists.append([])
        for length, sends_down, sends_up, north_comes, south_comes in (
            (count, lat > 0, lat < last, lat > 1, lat < last - 1),
            (edge_count, lat == 0, lat == last, lat == 1, lat == last - 1),
        ):
            low, high = pl.ds(0, length), pl.ds(total - length, length)
            lists[g] += [
                (
                    remote(
                        slots.at[g, high],
                        north[g].at[high],
                        y_send.at[0, g],
                        y_recv.at[0, g],
                        lat + 1,
                        down_lon,
                    ),
                    landed(north[g].at[high], y_recv.at[0, g]),
                    jnp.logical_and(down, sends_down),
                    jnp.logical_and(up, north_comes),
                ),
                (
                    remote(
                        slots.at[g, low],
                        south[g].at[low],
                        y_send.at[1, g],
                        y_recv.at[1, g],
                        lat - 1,
                        up_lon,
                    ),
                    landed(south[g].at[low], y_recv.at[1, g]),
                    jnp.logical_and(up, sends_up),
                    jnp.logical_and(down, south_comes),
                ),
            ]
        for copy, _, sends, _ in lists[g]:
            pl.when(sends)(copy.start)

    def dense(g, lon_there, store):
        def row(t, carry):
            at = lon_there * rows + t
            i, j = at // 128, lax.rem(at, 128)
            a = own_index[1, i, j]
            b = jnp.where(up, north_index[i, j], total)
            c = jnp.where(down, south_index[i, j], total)
            value = own[g][a].astype(F32) + north[g][b].astype(F32) + south[g][c].astype(F32)
            store(t, value.astype(BF16))
            return carry

        lax.fori_loop(0, rows, row, 0, unroll=8)

    core_copies, z_copies = [], []
    for g in range(groups):
        loads[g].wait()
        for _, arrival, _, comes in lists[g]:
            pl.when(comes)(arrival.wait)
        for part, (theirs, ours) in enumerate(((beside_across, across), (beside, lon))):

            def put_away(t, value):
                away[part, g, t] = value

            def put_mine(t, value):
                mine[part, g, t] = value

            dense(g, theirs, put_away)
            copy = remote(
                away.at[part, g],
                from_core.at[part, g],
                core_send.at[part, g],
                core_recv.at[part, g],
                lat,
                beside,
            )
            copy.start()
            core_copies.append(copy)
            dense(g, ours, put_mine)
            if part == 0:
                landed(from_core.at[0, g], core_recv.at[0, g]).wait()
                to_z[g] = (mine[0, g].astype(F32) + from_core[0, g].astype(F32)).astype(BF16)
                copy = remote(
                    to_z.at[g], from_z.at[g], z_send.at[g], z_recv.at[g], lat, across
                )
                copy.start()
                z_copies.append(copy)
        if g < 2:
            held = receive_maximum(partial.at[g])
            send_maximum(g + 1)

    lane = lax.broadcasted_iota(jnp.int32, (size, cols), 1)
    tiles = edges.shape[0]
    for g in range(groups):
        landed(from_core.at[1, g], core_recv.at[1, g]).wait()
        landed(from_z.at[g], z_recv.at[g]).wait()
        part = pl.ds(g * size, size)
        for tile in range(tiles):
            edge = jnp.zeros((size, cols), F32)
            for k in range(32):
                r = tile * 32 + k
                flux = (
                    mine[1, g, r].astype(F32)
                    + from_core[1, g, r].astype(F32)
                    + from_z[g, r].astype(F32)
                )
                v = (base[r, part].astype(F32) + flux).astype(BF16)
                first[r, part] = v
                rolled = pltpu.roll(v.astype(F32), (4 * k + 2) % cols, 1)
                edge = jnp.where(lane // 4 == k, rolled, edge)
            edges[tile, part] = edge.astype(BF16)
    lo, hi = edges.at[0], edges.at[tiles - 1]
    moves = [
        (edges, right.at[pl.ds(1, tiles)], lat, west, always, always),
        (edges, left.at[pl.ds(1, tiles)], lat, east, always, always),
        (first.at[pl.ds(0, 2)], bottom, lat - 1, lon, up, down),
        (first.at[pl.ds(rows - 2, 2)], top, lat + 1, lon, down, up),
        (lo, right.at[tiles + 1], lat - 1, west, up, down),
        (lo, left.at[tiles + 1], lat - 1, east, up, down),
        (hi, right.at[0], lat + 1, west, down, up),
        (hi, left.at[0], lat + 1, east, down, up),
    ]
    copies = [
        remote(src, dst, halo_send.at[i], halo_recv.at[i], a, b)
        for i, (src, dst, a, b, _, _) in enumerate(moves)
    ]
    for copy, move in zip(copies, moves):
        pl.when(move[4])(copy.start)
    receive_maximum(None)
    for copy in core_copies + z_copies + small:
        copy.wait_send()
    for g in range(groups):
        for copy, _, sends, _ in lists[g]:
            pl.when(sends)(copy.wait_send)
    for i, (copy, move) in enumerate(zip(copies, moves)):
        pl.when(move[4])(copy.wait_send)
        pl.when(move[5])(landed(move[1], halo_recv.at[i]).wait)


def couple(operands, count, edge_count, collective_id, lat_count, lon_count):
    _, _, _, slots, atmos, overflow = operands
    groups, total, size, cols = slots.shape
    channels, rows, cols = atmos.shape
    tiles = rows // 32
    vmem = pl.BlockSpec(memory_space=pltpu.VMEM)
    smem = pl.BlockSpec(memory_space=pltpu.SMEM)
    dma = pltpu.SemaphoreType.DMA
    shapes = [(rows, channels, cols)] + [(2, channels, cols)] * 2 + [(tiles + 2, channels, cols)] * 2
    received = pltpu.VMEM((total + 1, size, cols), BF16)
    peers = lon_count - 1 + 3 + lat_count // 4 - 1
    one = pltpu.VMEM((groups, rows, size, cols), BF16)
    two = pltpu.VMEM((2, groups, rows, size, cols), BF16)
    return pl.pallas_call(
        functools.partial(couple_kernel, lat_count, lon_count, count, edge_count),
        out_shape=[jax.ShapeDtypeStruct(s, BF16) for s in shapes]
        + [jax.ShapeDtypeStruct((1,), jnp.int32)],
        in_specs=[smem] * 3 + whole_any(3),
        out_specs=[vmem] + whole_any(4) + [smem],
        scratch_shapes=[received] * (3 * groups)
        + [two] * 3
        + [one] * 2
        + [pltpu.VMEM((tiles, channels, cols), BF16)]
        + [dma((groups,))]
        + [dma((2, groups))] * 4
        + [dma((groups,))] * 2
        + [dma((8,))] * 2
        + [pltpu.VMEM((peers,) + overflow.shape, jnp.int32)]
        + [pltpu.VMEM((2,) + overflow.shape, jnp.int32)]
        + [dma((peers,))] * 2
        + [pltpu.VMEM((rows, channels, cols), BF16)]
        + [pltpu.VMEM(atmos.shape, BF16), pltpu.VMEM(overflow.shape, jnp.int32), dma((2,))],
        compiler_params=pltpu.CompilerParams(
            collective_id=collective_id, has_side_effects=True, vmem_limit_bytes=VMEM_LIMIT
        ),
        name="couple",
    )(*operands)


def atmos_kernel(
    lat_count, a_ref, top_ref, bottom_ref, left_ref, right_ref, w1_ref, b1_ref, w2_ref, b2_ref, out_ref, tall, second
):
    count, channels, cols = a_ref.shape
    lat = lax.axis_index("lat")
    b1, b2 = column(b1_ref[...]), column(b2_ref[...])

    tall[2 : 2 + count, :, 0:cols] = a_ref[...]
    lane = lax.broadcasted_iota(jnp.int32, (channels, cols), 1)
    for tile in range(count // 32 + 2):
        side = jnp.where(lane % 4 < 2, left_ref[tile], right_ref[tile]).astype(F32)
        for k in range(32):
            r = tile * 32 - 32 + k
            if r < -2 or r >= count + 2:
                continue
            v = pltpu.roll(side, (126 - 4 * k) % cols, 1).astype(BF16)
            if r < 0 or r >= count:
                inside = lat > 0 if r < 0 else lat < lat_count - 1
                main = top_ref[r + 2] if r < 0 else bottom_ref[r - count]
                tall[r + 2, :, 0:cols] = jnp.where(inside, main, jnp.zeros_like(main))
                v = jnp.where(inside, v, jnp.zeros_like(v))
            tall[r + 2, :, cols:] = v

    def conv(source, weight, start, group):
        fields = [
            jnp.concatenate([source[start + i + d] for d in range(3)], axis=0)
            for i in range(group)
        ]
        return jnp.dot(weight, jnp.concatenate(fields, axis=1), preferred_element_type=F32)

    def first(step, carry):
        group = FIRST_ROWS
        start = step * group
        taps = conv(tall, w1_ref[...], start, group)
        for i in range(group):
            j = start + i
            value = silu(shifted_sum(taps[:, i * 2 * cols : (i + 1) * 2 * cols]) + b1)
            outside = jnp.logical_or(
                jnp.logical_and(j == 0, lat == 0),
                jnp.logical_and(j == count + 1, lat == lat_count - 1),
            )
            second[j] = jnp.where(outside, 0.0, value).astype(BF16)
        return carry

    lax.fori_loop(0, (count + 2) // FIRST_ROWS, first, 0)

    def last(step, carry):
        group = LAST_ROWS
        start = step * group
        taps = conv(second, w2_ref[...], start, group)
        rows = []
        for i in range(group):
            value = shifted_sum(taps[:, i * 2 * cols : (i + 1) * 2 * cols])[:, :cols]
            rows.append(a_ref[start + i].astype(F32) + (value + b2))
        block = jnp.swapaxes(jnp.stack(rows), 0, 1).astype(BF16)
        out_ref[:, pl.ds(pl.multiple_of(start, group), group), :] = block
        return carry

    lax.fori_loop(0, count // LAST_ROWS, last, 0)


def atmos_step(a, top, bottom, left, right, w1, b1, w2, b2, lat_count):
    count, channels, cols = a.shape
    vmem = pl.BlockSpec(memory_space=pltpu.VMEM)
    return pl.pallas_call(
        functools.partial(atmos_kernel, lat_count),
        out_shape=jax.ShapeDtypeStruct((channels, count, cols), BF16),
        in_specs=[vmem] * 9,
        out_specs=vmem,
        scratch_shapes=[
            pltpu.VMEM((count + 4, channels, 2 * cols), BF16),
            pltpu.VMEM((count + 2, channels, 2 * cols), BF16),
        ],
        compiler_params=pltpu.CompilerParams(vmem_limit_bytes=VMEM_LIMIT),
        name="atmos",
    )(a, top, bottom, left, right, w1, b1, w2, b2)


def per_device(
    ocean_state,
    sea_mask,
    ocean_w1,
    ocean_b1,
    ocean_w2,
    ocean_b2,
    regrid_weight,
    route_dev,
    route_row,
    atmos_state,
    atmos_w1,
    atmos_b1,
    atmos_w2,
    atmos_b2,
):
    lat_count, lon_count = lax.axis_size("lat"), lax.axis_size("lon")
    atmos_rows = atmos_state.shape[1]

    count = route_dev.size
    weights = (ocean_w1, ocean_w2, atmos_w1, atmos_w2)
    hidden, index, north_index, south_index, meta, overflow, *weights = ocean_halo(
        ocean_state,
        sea_mask,
        route_dev,
        route_row,
        weights,
        ocean_b1[None, :],
        lat_count,
        lon_count,
        atmos_rows,
    )
    ocean_next, slots = ocean_step(
        meta,
        hidden,
        sea_mask,
        weights[0],
        ocean_b2[None, :],
        regrid_weight.reshape(-1, 256, 128),
    )
    operands = (index, north_index, south_index, slots, atmos_state, overflow)
    *coupled, overflow = couple(operands, SHORT, EDGE_SHORT, 1, lat_count, lon_count)
    first, top, bottom, left, right = lax.cond(
        overflow[0] > 0,
        lambda short, operands: tuple(couple(operands, count, count, 2, lat_count, lon_count)[:5]),
        lambda short, operands: short,
        tuple(coupled),
        operands,
    )
    atmos_next = atmos_step(
        first,
        top,
        bottom,
        left,
        right,
        weights[1],
        atmos_b1[None, :],
        weights[2],
        atmos_b2[None, :],
        lat_count,
    )
    return ocean_next, atmos_next


def solution(mesh):
    in_specs = (
        P(None, "lat", "lon"),
        P("lat", "lon"),
        P(),
        P(),
        P(),
        P(),
        P(("lat", "lon"), None, None, None),
        P(("lat", "lon"), None),
        P(("lat", "lon"), None),
        P(None, "lat", "lon"),
        P(),
        P(),
        P(),
        P(),
    )
    out_specs = (P(None, "lat", "lon"), P(None, "lat", "lon"))
    return jax.shard_map(
        per_device, mesh=mesh, in_specs=in_specs, out_specs=out_specs, check_vma=False
    )
```
